256 devices in a mesh: dp: 4 (over x), zero: 64 (over y, z, core).
Axes of the slice: x: 4, y: 4, z: 8, core: 2. Of those that a mesh axis runs over, the one named last changes fastest.
Arguments:
- hidden_in: bfloat16 [512, 4608], P(('dp', 'zero')), may hold values from -16 to 16
- targets: bfloat16 [512, 4608], P(('dp', 'zero')), may hold values from -16 to 16
- norm_gain: float32 [4608], replicated, may hold values from 0.5 to 2
- up_weight: bfloat16 [24576, 4608], P('zero'), may hold values from -0.35 to 0.35
- down_weight: bfloat16 [24576, 4608], P('zero'), may hold values from -0.0390625 to 0.0390625
- start: float32 [24576, 4608], P(('zero', 'dp')), may hold values from -24 to 24
Outputs:
- basis_next: float32 [2, 24576, 4608], P(None, ('zero', 'dp'))
- first_quotient: float32 [1], replicated
- coefficients: float32 [2, 2], replicated
The draws below stay inside these ranges and needn't reach their ends.
All inputs are finite; a program needn't handle non-finite values.
Results may differ from the reference program's by a relative error of at most 0.017.
Values may be sent and summed in bfloat16 or wider, within the bound.
A program may use at most 128 MiB of HBM per device.

```python
import math
import jax
import jax.numpy as jnp
from jax import lax

D = 4608
FF = 24576
TOKENS = 512
N_DP = 4
DEVICES = 256


def activation_pieces(key):
    key = jax.random.fold_in(key, 11)
    key_scale, key_main = jax.random.split(key, 2)
    feature_scale = jnp.exp(jax.random.uniform(key_scale, (D,), jnp.float32, 0.0, jnp.log(10.0))) / 4.64
    normal_main = jax.random.normal(key_main, (TOKENS, D), jnp.float32)
    return (feature_scale, normal_main)


def draw_hidden_in(key, part):
    feature_scale, normal_main = activation_pieces(key)
    values = normal_main * feature_scale
    return jnp.clip(values, -16.0, 16.0).astype(jnp.bfloat16)


def draw_targets(key, part):
    feature_scale, normal_main = activation_pieces(key)
    key = jax.random.fold_in(key, 53)
    values = normal_main * feature_scale
    noise = jax.random.normal(key, (TOKENS, D), jnp.float32)
    values = 0.9 * jnp.clip(values, -16.0, 16.0) + 0.45 * noise
    return jnp.clip(values, -16.0, 16.0).astype(jnp.bfloat16)


def draw_up_weight(key, part):
    key = jax.random.fold_in(key, 23)
    key_scale, key_main = jax.random.split(key, 2)
    row_scale = jnp.exp(jax.random.uniform(key_scale, (FF, 1), jnp.float32, 0.0, jnp.log(10.0))) / 3.1623
    values = jax.random.normal(key_main, (FF, D), jnp.float32) * row_scale
    values = values * (1.0 / D ** 0.5)
    return jnp.clip(values, -0.35, 0.35).astype(jnp.bfloat16)


def rising_scale(rise):
    row_ids = jnp.arange(FF, dtype=jnp.int32)
    block_ids = row_ids // (FF // DEVICES)
    dp_pos = (block_ids % N_DP).astype(jnp.float32)
    zero_pos = (block_ids // N_DP).astype(jnp.float32)
    zero_count = float(DEVICES // N_DP)
    along_dp = 1.0 + (rise - 1.0) * dp_pos / float(max(N_DP - 1, 1))
    along_zero = 1.0 + 0.5 * zero_pos / max(zero_count - 1.0, 1.0)
    return along_dp * along_zero


def draw_start(key, part):
    key = jax.random.fold_in(key, 37)
    key_scale, key_main = jax.random.split(key, 2)
    rough = jnp.exp(jax.random.uniform(key_scale, (FF,), jnp.float32, 0.0, jnp.log(2.0)))
    row_scale = rising_scale(3.0) * rough
    values = jax.random.normal(key_main, (FF, D), jnp.float32) * row_scale[:, None]
    return jnp.clip(values, -24.0, 24.0).astype(jnp.float32)


def steps_of(key, extent, cuts, smallest, largest):
    loudness, own = 1.0, jax.random.fold_in(key, 6)
    for position, parts in cuts:
        heights = jnp.exp(jax.random.uniform(jax.random.fold_in(own, position), (parts,), jnp.float32, smallest / len(cuts), largest / len(cuts)))
        loudness = loudness * jnp.repeat(heights, extent[position] // parts).reshape([-1 if axis == position else 1 for axis in range(len(extent))])
    return loudness


def gaussian(rng, extent, width, most, cuts=(), kind=jnp.bfloat16):
    result = width * jax.random.normal(rng, extent, jnp.float32)
    if cuts:
        result = result * steps_of(rng, extent, cuts, -0.22, 0.18)
    return jnp.clip(result, -most, most).astype(kind)


def setup_inputs(seed: int = 0) -> dict:
    key_of = jax.random.split(jax.random.key(seed), 7)
    hidden_in = draw_hidden_in(jax.random.fold_in(key_of[6], 71), 0)
    targets = draw_targets(jax.random.fold_in(key_of[6], 71), 0)
    norm_gain = jnp.clip(jnp.exp(jax.random.uniform(key_of[2], (D,), jnp.float32, math.log(0.5), math.log(2.0))), 0.5, 2.0)
    up_weight = draw_up_weight(jax.random.fold_in(key_of[6], 71), 0)
    down_weight = gaussian(key_of[4], (FF, D), FF ** -0.5, 0.0390625, ((0, 64),))
    start = draw_start(jax.random.fold_in(key_of[6], 71), 0)
    return {"hidden_in": hidden_in, "targets": targets, "norm_gain": norm_gain, "up_weight": up_weight, "down_weight": down_weight, "start": start}


norm_eps = 1e-06
gelu_coef = 0.7978845608028654

def gelu_value(inputs):
    return 0.5 * inputs * (1.0 + jnp.tanh(gelu_coef * (inputs + 0.044715 * inputs * inputs * inputs)))

def gelu_parts(inputs):
    unit_dir = jnp.ones_like(inputs)

    def first_slope(points):
        return jax.jvp(gelu_value, (points,), (unit_dir,))[1]
    return (gelu_value(inputs), first_slope(inputs), jax.jvp(first_slope, (inputs,), (unit_dir,))[1])

def token_loss(branch, residual, target, norm_gain, token_count):
    summed = residual.astype(jnp.float32) + branch
    normed = summed * lax.rsqrt(lax.optimization_barrier(jnp.mean(summed * summed, axis=-1, keepdims=True)) + norm_eps)
    misfit = normed * norm_gain - target.astype(jnp.float32)
    return 0.5 * jnp.sum(misfit * misfit) / token_count

def branch_grad(branch, residual, target, norm_gain, token_count):
    return jax.grad(token_loss)(branch, residual, target, norm_gain, token_count)

def branch_curv(branch, tangent, residual, target, norm_gain, token_count):

    def inner_grad(point):
        return branch_grad(point, residual, target, norm_gain, token_count)
    return jax.jvp(inner_grad, (branch,), (tangent,))[1]

def reference(hidden_in, targets, norm_gain, up_weight, down_weight, start):
    token_count = float(hidden_in.shape[0])
    entry_count = float(FF * D)
    pre_act = jnp.dot(hidden_in, up_weight.T, preferred_element_type=jnp.float32)
    gelu_out, gelu_slope, gelu_bend = gelu_parts(pre_act)
    hidden_act = gelu_out.astype(jnp.bfloat16)
    branch = jnp.dot(hidden_act, down_weight, preferred_element_type=jnp.float32)
    grad_rows = branch_grad(branch, hidden_in, targets, norm_gain, token_count).astype(jnp.bfloat16)
    act_grad = jnp.dot(grad_rows, down_weight.T, preferred_element_type=jnp.float32)

    def curvature(direction):
        direction_bf = direction.astype(jnp.bfloat16)
        pre_tangent = jnp.dot(hidden_in, direction_bf.T, preferred_element_type=jnp.float32)
        act_tangent = (gelu_slope * pre_tangent).astype(jnp.bfloat16)
        branch_tangent = jnp.dot(act_tangent, down_weight, preferred_element_type=jnp.float32)
        grad_tangent = branch_curv(branch, branch_tangent, hidden_in, targets, norm_gain, token_count).astype(jnp.bfloat16)
        act_grad_tangent = jnp.dot(grad_tangent, down_weight.T, preferred_element_type=jnp.float32)
        pre_grad_tangent = (act_grad_tangent * gelu_slope + act_grad * gelu_bend * pre_tangent).astype(jnp.bfloat16)
        return jnp.dot(pre_grad_tangent.T, hidden_in, preferred_element_type=jnp.float32)
    start_square = jnp.sum(start * start) / entry_count
    first_vec = start * lax.rsqrt(start_square + norm_eps)
    image_one = curvature(first_vec)
    coef_one = jnp.sum(first_vec * image_one) / entry_count
    left_one = image_one - coef_one * first_vec
    square_one = jnp.sum(left_one * left_one) / entry_count
    second_vec = left_one * lax.rsqrt(square_one + norm_eps)
    image_two = curvature(second_vec)
    coef_upper = jnp.sum(first_vec * image_two) / entry_count
    coef_diag = jnp.sum(second_vec * image_two) / entry_count
    left_two = image_two - coef_upper * first_vec - coef_diag * second_vec
    square_two = jnp.sum(left_two * left_two) / entry_count
    third_vec = left_two * lax.rsqrt(square_two + norm_eps)
    coefficients = jnp.stack([jnp.stack([coef_upper, coef_diag]), jnp.stack([jnp.sqrt(square_one), jnp.sqrt(square_two)])])
    return (jnp.stack([second_vec, third_vec]), jnp.reshape(coef_one, (1,)), coefficients)
```

```python
import jax
import jax.numpy as jnp
from jax import lax
from jax.experimental import pallas as pl
from jax.experimental.pallas import tpu as pltpu
from jax.sharding import PartitionSpec as P

MESH = pl.DeviceIdType.MESH
f32, bf16 = jnp.float32, jnp.bfloat16
norm_eps = 1e-06
gelu_coef = 0.7978845608028654

N_X, N_Y, N_Z, N_C = 4, 4, 8, 2
D = 4608
ROWS = 96
PAD = 128
HID = N_X * PAD
GRP = 128
TOK = N_X * GRP
HALF = GRP // N_C
BLK = HALF // N_Y
OWN = BLK // N_Z
CHUNKS = 2
W = D // CHUNKS
PIECE = 16
XA = 2560


def gelu_value(inputs):
    return (
        0.5 * inputs * (1.0 + jnp.tanh(gelu_coef * (inputs + 0.044715 * inputs * inputs * inputs)))
    )


def gelu_parts(inputs):
    unit_dir = jnp.ones_like(inputs)

    def first_slope(points):
        return jax.jvp(gelu_value, (points,), (unit_dir,))[1]

    return (
        gelu_value(inputs),
        first_slope(inputs),
        jax.jvp(first_slope, (inputs,), (unit_dir,))[1],
    )


def loss_parts(summed, target, gain):
    r = lax.rsqrt(jnp.sum(summed * summed, axis=-1, keepdims=True) / D + norm_eps)
    normed = summed * r
    pull = (normed * gain - target) * gain
    mean = jnp.sum(pull * normed, axis=-1, keepdims=True) / D
    return r, normed, pull, mean


def loss_grad(summed, target, gain):
    r, normed, pull, mean = loss_parts(summed, target, gain)
    return r * (pull - normed * mean) / float(TOK)


def loss_curv(summed, tangent, target, gain):
    r, normed, pull, mean = loss_parts(summed, target, gain)
    along = jnp.sum(normed * tangent, axis=-1, keepdims=True) / D
    d_normed = r * (tangent - normed * along)
    d_pull = d_normed * gain * gain
    d_mean = jnp.sum(d_pull * normed + pull * d_normed, axis=-1, keepdims=True) / D
    grad = r * (pull - normed * mean)
    d_grad = r * (d_pull - d_normed * mean - normed * d_mean) - (r * along) * grad
    return d_grad / float(TOK)


def dot_t(a, b):
    return lax.dot_general(a, b, (((1,), (1,)), ((), ())), preferred_element_type=f32)


def dot(a, b):
    return jnp.dot(a, b, preferred_element_type=f32)


def tile_sum(v):
    rows, cols = v.shape
    acc = v[0:8, :]
    for i in range(8, rows, 8):
        acc = acc + v[i : i + 8, :]
    out = acc[:, 0:128]
    for k in range(128, cols, 128):
        out = out + acc[:, k : k + 128]
    return out


def par(*gens):
    gens = list(gens)
    while gens:
        for g in list(gens):
            try:
                next(g)
            except StopIteration:
                gens.remove(g)
        if gens:
            yield


def run(*gens):
    for _ in par(*gens):
        pass


def play(gens, order):
    for j in order:
        next(gens[j], None)
    run(*gens)


def kernel(
    hin, tgt, gain, up_hbm, down_hbm, start_hbm,
    kw_hbm, k2_hbm, mix,
    up, down, start, sbf, X, xz, tmp16, part,
    sb, rc, s1f, y1b, y1r, y2b, y2r, sz, rz, az, A,
    slope, bendag, hact, agrad, pt1, ptx, pts, ptr,
    pfull, pr2, gram, kw, k2, arv, arr, tot, bsum,
    ld_sem, xz_s, xz_r, xy_s, xy_r, xc_s, xc_r,
    xa_s, xa_r, xac_s, xac_r, xb_s, xb_r, xby_s, xby_r, xbc_s, xbc_r,
    rc_s, rc_r, y1_s, y1_r, y2_s, y2_r, rz_s, rz_r,
    az_s, az_r, ay_s, ay_r, ac_s, ac_r,
    pt_s, pt_r, pf_s, pf_r, p2_s, p2_r, ar_s, ar_r, out_sem,
):
    x = lax.axis_index("dp")
    shard = lax.axis_index("zero")
    y, z, c = shard // 16, (shard // 2) % 8, shard % 2

    def dev(nx, ny, nz, nc):
        return (nx, ny * 16 + nz * 2 + nc)

    def x_at(k):
        return (x + (k % N_X)) % N_X

    def y_at(k):
        return (y + (k % N_Y)) % N_Y

    def x_peer(k):
        return dev(x_at(k), y, z, c)

    def y_peer(k):
        return dev(x, y_at(k), z, c)

    def z_peer(k):
        return dev(x, y, (z + k) % N_Z, c)

    c_peer = dev(x, y, z, 1 - c)

    def xy_peer(k):
        return dev(x_at(k // N_Y), y_at(k % N_Y), z, c)

    def zc_peer(k):
        return dev(x, y, (z + k // N_C) % N_Z, (c + k % N_C) % N_C)

    def send(src, dst, ssem, rsem, to):
        cp = pltpu.make_async_remote_copy(
            src_ref=src, dst_ref=dst, send_sem=ssem, recv_sem=rsem, device_id=to, device_id_type=MESH
        )
        cp.start()
        return cp

    def rows(start_row, count):
        return pl.ds(pl.multiple_of(start_row, 16), count)

    def wait_all(cps):
        for cp in cps:
            cp.wait()

    loads = []
    for b in range(N_X):
        for j, (src, dst) in enumerate(((up_hbm, up), (down_hbm, down))):
            loads.append(
                pltpu.make_async_copy(
                    src.at[pl.ds(b * ROWS, ROWS)], dst.at[pl.ds(b * PAD, ROWS)], ld_sem.at[2 * b + j]
                )
            )
    loads.append(pltpu.make_async_copy(start_hbm, start, ld_sem.at[2 * N_X]))
    for cp in loads:
        cp.start()

    barrier = pltpu.get_barrier_semaphore()
    peers = [xy_peer(k) for k in range(1, N_X * N_Y)] + [zc_peer(k) for k in range(1, N_Z * N_C)]
    for p in peers:
        pl.semaphore_signal(barrier, inc=1, device_id=p, device_id_type=MESH)
    pl.semaphore_wait(barrier, len(peers))

    def ring_gather(ref, blocks, c0, w, peer, ssem, rsem, then=None):
        half = w // 2
        nb = len(blocks)
        first = []
        for b, (row_of, count) in enumerate(blocks):
            at = (rows(row_of(0), count), pl.ds(c0, w))
            first.append(
                [
                    send(ref.at[at], ref.at[at], ssem.at[2 * b + j], rsem.at[2 * b + j], peer(to))
                    for j, to in enumerate((1, -1))
                ]
            )
        if then:
            then(0)
        yield
        second = []
        for b, (row_of, count) in enumerate(blocks):
            for j, to in enumerate((1, -1)):
                first[b][j].wait()
                at = (rows(row_of(-to), count), pl.ds(c0 + j * half, half))
                i = 2 * (nb + b) + j
                second.append(send(ref.at[at], ref.at[at], ssem.at[i], rsem.at[i], peer(to)))
        if then:
            then(-1)
            then(1)
        yield
        wait_all(second)
        if then:
            then(2)

    def gather_z(own, buf, ssem, rsem):
        buf[z] = own
        return [
            send(buf.at[z], buf.at[z], ssem.at[k - 1], rsem.at[k - 1], z_peer(k)) for k in range(1, N_Z)
        ]

    def join16(buf, c0, w):
        for j in range(N_Z):
            tmp16[pl.ds(OWN * j, OWN), c0 : c0 + w] = buf[j].astype(f32)
        return tmp16[:, c0 : c0 + w].astype(bf16)

    def gather(own, i, h):
        c0, out = h * W, A.at[i]
        cols = pl.ds(c0, W)
        cps = gather_z(own[:, c0 : c0 + W], az.at[i, h], az_s.at[i, h], az_r.at[i, h])
        yield
        wait_all(cps)
        out[rows(c * HALF + y * BLK, BLK), cols] = join16(az.at[i, h], c0, W)
        passed = []

        def pass_on(k):
            at = (rows(c * HALF + y_at(k) * BLK, BLK), cols)
            passed.append(send(out.at[at], out.at[at], ac_s.at[i, h, k % 4], ac_r.at[i, h, k % 4], c_peer))

        yield from ring_gather(
            out,
            [(lambda k: c * HALF + y_at(k) * BLK, BLK)],
            c0,
            W,
            y_peer,
            ay_s.at[i, h],
            ay_r.at[i, h],
            pass_on,
        )
        yield
        wait_all(passed)
        part_grad = dot_t(out[:, cols], down[:, cols])
        if h == 0:
            agrad[i % 2] = part_grad
        else:
            agrad[i % 2] = agrad[i % 2] + part_grad

    def scatter(i, h, make=None):
        c0 = h * W
        cols = slice(c0, c0 + W)
        if make is not None:
            make(h)
        sb[i, h] = part[rows((1 - c) * HALF, HALF), cols].astype(bf16)
        cps = [send(sb.at[i, h], rc.at[i, h], rc_s.at[i, h], rc_r.at[i, h], c_peer)]
        yield
        wait_all(cps)
        s1f[i % 2, :, cols] = part[rows(c * HALF, HALF), cols] + rc[i, h].astype(f32)

        def block(k):
            return s1f[i % 2, rows(y_at(k) * BLK, BLK), cols]

        half = W // 2
        y1b[i, h] = block(2).astype(bf16)
        cps = [
            send(
                y1b.at[i, h, :, pl.ds(j * half, half)],
                y1r.at[i, h, :, pl.ds(j * half, half)],
                y1_s.at[i, h, j],
                y1_r.at[i, h, j],
                y_peer(to),
            )
            for j, to in enumerate((1, -1))
        ]
        yield
        wait_all(cps)
        got = y1r[i, h].astype(f32)
        for j, to in enumerate((1, -1)):
            mine = block(to)
            if j == 0:
                pieces = [mine[:, :half] + got[:, :half], mine[:, half:]]
            else:
                pieces = [mine[:, :half], mine[:, half:] + got[:, half:]]
            y2b[i, h, j, :, pl.ds(0, half)] = pieces[0].astype(bf16)
            y2b[i, h, j, :, pl.ds(half, half)] = pieces[1].astype(bf16)
        cps = [
            send(y2b.at[i, h, j], y2r.at[i, h, j], y2_s.at[i, h, j], y2_r.at[i, h, j], y_peer(to))
            for j, to in enumerate((1, -1))
        ]
        yield
        wait_all(cps)
        tmp16[:, cols] = block(0) + y2r[i, h, 0].astype(f32) + y2r[i, h, 1].astype(f32)
        for j in range(N_Z):
            sz[i, h, j] = tmp16[pl.ds(OWN * j, OWN), cols].astype(bf16)
        cps = [
            send(
                sz.at[i, h, (z + k) % N_Z],
                rz.at[i, h, k - 1],
                rz_s.at[i, h, k - 1],
                rz_r.at[i, h, k - 1],
                z_peer(k),
            )
            for k in range(1, N_Z)
        ]
        yield
        wait_all(cps)
        s3 = sz[i, h, z].astype(f32)
        for k in range(N_Z - 1):
            s3 = s3 + rz[i, h, k].astype(f32)
        tot[i, :, cols] = s3

    def scatters(i, make):
        return par(*[scatter(i, h, make) for h in range(CHUNKS)])

    def gathers(own, i):
        return par(*[gather(own, i, h) for h in range(CHUNKS)])

    def all_sum(i, n):
        for s, peer in enumerate((xy_peer, zc_peer)):
            cps = [
                send(
                    arv.at[i, s, pl.ds(0, n)],
                    arr.at[i, s, k - 1, pl.ds(0, n)],
                    ar_s.at[i, s, k - 1],
                    ar_r.at[i, s, k - 1],
                    peer(k),
                )
                for k in range(1, 16)
            ]
            yield
            wait_all(cps)
            acc = arv[i, s, 0:n]
            for k in range(1, 16):
                acc = acc + arr[i, s, k - 1, 0:n]
            arv[i, s + 1, 0:n] = acc

    group = rows(x * GRP, GRP)

    def group_tokens(h):
        c0 = h * W
        cols = pl.ds(c0, W)
        cps = gather_z(hin[:, c0 : c0 + W], xz.at[h], xz_s.at[h], xz_r.at[h])
        yield
        wait_all(cps)
        X[rows(x * GRP + c * HALF + y * BLK, BLK), cols] = join16(xz.at[h], c0, W)
        passed = []

        def pass_on(k):
            at = (rows(x * GRP + c * HALF + y_at(k) * BLK, BLK), cols)
            passed.append(send(X.at[at], X.at[at], xc_s.at[h, k % 4], xc_r.at[h, k % 4], c_peer))

        yield from ring_gather(
            X,
            [(lambda k: x * GRP + c * HALF + y_at(k) * BLK, BLK)],
            c0,
            W,
            y_peer,
            xy_s.at[h],
            xy_r.at[h],
            pass_on,
        )
        yield
        wait_all(passed)
        pre = dot_t(X[group, cols], up[:, cols])
        if h == 0:
            agrad[0] = pre
        else:
            agrad[0] = agrad[0] + pre

    def local_work():
        for b in range(N_X):
            up[pl.ds(b * PAD + ROWS, PAD - ROWS), :] = jnp.zeros((PAD - ROWS, D), bf16)
            down[pl.ds(b * PAD + ROWS, PAD - ROWS), :] = jnp.zeros((PAD - ROWS, D), bf16)
        sbf[pl.ds(ROWS, PAD - ROWS), :] = jnp.zeros((PAD - ROWS, D), bf16)
        yield
        for cp in loads:
            cp.wait()
        sbf[pl.ds(0, ROWS), :] = start[...].astype(bf16)
        yield
        arv[0, 0, 1] = tile_sum(start[...] * start[...])

    own_xb = ring_gather(
        X, [(lambda k: x_at(k) * GRP + c * HALF + y * BLK, BLK)], XA, D - XA, x_peer, xb_s, xb_r
    )
    tok_gens = [group_tokens(h) for h in range(CHUNKS)]

    def later_xb():
        for _ in range(2):
            next(own_xb)
            yield

    both = list(range(CHUNKS))
    n = CHUNKS
    play(tok_gens + [local_work(), later_xb()], both + [n] + both + [n + 1, n] + both + [n + 1, n] + both)

    def tokens_yx():
        passed = []

        def pass_on(k):
            if k != 0:
                at = (rows(x_at(k) * GRP + c * HALF, HALF), pl.ds(0, XA))
                passed.append(send(X.at[at], X.at[at], xac_s.at[k % 4], xac_r.at[k % 4], c_peer))

        yield from ring_gather(
            X, [(lambda k: x_at(k) * GRP + c * HALF, HALF)], 0, XA, x_peer, xa_s, xa_r, pass_on
        )
        yield
        wait_all(passed)

    def tokens_xy():
        next(own_xb, None)
        blocks = [
            (lambda k, b=b: x_at(b) * GRP + c * HALF + y_at(k) * BLK, BLK) for b in range(1, N_X)
        ]
        yield from ring_gather(X, blocks, XA, D - XA, y_peer, xby_s, xby_r)
        passed = []
        for b in range(1, N_X):
            at = (rows(x_at(b) * GRP + c * HALF, HALF), pl.ds(XA, D - XA))
            passed.append(send(X.at[at], X.at[at], xbc_s.at[b], xbc_r.at[b], c_peer))
        yield
        wait_all(passed)

    def to_branch(h):
        for k in range(h * W, (h + 1) * W, W // 3):
            part[:, k : k + W // 3] = dot(hact[...], down[:, k : k + W // 3])

    def weights():
        return tgt[...].astype(f32), gain[...]

    def forward():
        for b in range(N_X):
            cols = pl.ds(b * PAD, PAD)
            value, first, second = gelu_parts(agrad[0, :, cols])
            hact[:, cols] = value.astype(bf16)
            slope[:, cols] = first
            bendag[:, cols] = second
        yield from scatters(0, to_branch)
        bsum[...] = hin[...].astype(f32) + tot[0]
        yield from gathers(loss_grad(bsum[...], *weights()).astype(bf16), 0)
        bendag[...] = bendag[...] * agrad[0]

    def first_tangent():
        pts[...] = dot_t(X[...], sbf[...])
        ptr[x] = pts[group, :]
        cps = [
            send(
                pts.at[rows(x_at(k) * GRP, GRP)], ptr.at[x], pt_s.at[k - 1], pt_r.at[k - 1], x_peer(k)
            )
            for k in range(1, N_X)
        ]
        yield
        wait_all(cps)
        for b in range(N_X):
            cols = pl.ds(b * PAD, PAD)
            pt1[:, cols] = ptr[b]
            hact[:, cols] = (slope[:, cols] * ptr[b]).astype(bf16)
        yield from scatters(1, to_branch)

    fwd = forward()
    yx, xy = tokens_yx(), tokens_xy()
    for g in (yx, xy, fwd, xy, fwd, xy, fwd, yx, fwd, yx, fwd, xy, yx):
        next(g, None)
    run(xy, yx)
    play((first_tangent(), fwd), (0, 1, 0, 1))
    curv = loss_curv(bsum[...], tot[1], *weights())

    def token_gram():
        half = TOK // 2
        for b in range(2):
            gram[:, pl.ds(b * half, half)] = dot_t(X[group, :], X[pl.ds(b * half, half), :])
            yield

    run(gathers(curv.astype(bf16), 1), token_gram())
    p1 = agrad[1] * slope[...] + bendag[...] * pt1[...]
    pfull[group, :] = p1.astype(bf16)

    def share_p1():
        yield from ring_gather(pfull, [(lambda k: x_at(k) * GRP, GRP)], 0, HID, x_peer, pf_s, pf_r)

    def own_sums():
        arv[0, 0, 0] = tile_sum(p1 * pt1[...])
        yield

    run(share_p1(), own_sums())

    g = gram[...]
    g_hi = g.astype(bf16)
    g_lo = (g - g_hi.astype(f32)).astype(bf16)
    ptx[...] = dot(g_hi, pfull[...]) + dot(g_lo, pfull[...])
    hact[...] = (slope[...] * ptx[...]).astype(bf16)

    def image_one():
        own = pfull[:, pl.ds(pl.multiple_of(x * PAD, PAD), PAD)].T
        for k in range(0, D, 512):
            kw[:, k : k + 512] = dot(own, X[:, k : k + 512])[0:ROWS, :]
            if k % 1536 == 1024:
                yield

    run(scatters(2, to_branch), all_sum(0, 2), image_one())
    count = float(ROWS * 256 * D)
    q = jnp.sum(arv[0, 2, 0], keepdims=True) / count
    ss = jnp.sum(arv[0, 2, 1], keepdims=True) / count
    s1 = lax.rsqrt(ss + norm_eps)
    h11 = s1 * s1 * q
    curv = loss_curv(bsum[...], tot[2] - h11 * tot[1], *weights())

    def remainder():
        ptx[...] = ptx[...] - h11 * pt1[...]
        acc = None
        for k in range(0, D, 1536):
            w = kw[:, k : k + 1536] - h11 * start[:, k : k + 1536]
            kw[:, k : k + 1536] = w
            s = tile_sum(w * w)
            acc = s if acc is None else acc + s
            yield
        arv[1, 0, 0] = acc

    run(gathers(curv.astype(bf16), 2), remainder())
    out_w = pltpu.make_async_copy(kw, kw_hbm, out_sem.at[0])
    out_w.start()
    for b in range(N_X):
        cols = pl.ds(b * PAD, PAD)
        pr2[1, b] = (agrad[0, :, cols] * slope[:, cols] + bendag[:, cols] * ptx[:, cols]).astype(bf16)
    pr2[0, x] = pr2[1, x]
    cps = [
        send(pr2.at[1, x_at(k)], pr2.at[0, x], p2_s.at[k - 1], p2_r.at[k - 1], x_peer(k))
        for k in range(1, N_X)
    ]
    wait_all(cps)
    sums = [None, None, None]
    for k in range(0, D, 512):
        cols = slice(k, k + 512)
        acc = None
        for b in range(N_X):
            term = dot(pr2[0, b].T, X[pl.ds(b * GRP, GRP), cols])
            acc = term if acc is None else acc + term
        acc = acc[0:ROWS, :]
        k2[:, cols] = acc
        for j, other in enumerate((start[:, cols], kw[:, cols], acc)):
            s = tile_sum(other * acc)
            sums[j] = s if sums[j] is None else sums[j] + s
    for j in range(3):
        arv[1, 0, 1 + j] = sums[j]
    out_2 = pltpu.make_async_copy(k2, k2_hbm, out_sem.at[1])
    out_2.start()
    run(all_sum(1, 4))
    ww, sk, wk, kk = [jnp.sum(arv[1, 2, j], keepdims=True) / count for j in range(4)]
    sq1 = s1 * s1 * ww
    scale2 = lax.rsqrt(sq1 + norm_eps)
    s2 = scale2 * s1
    h12 = s1 * s2 * sk
    h22 = s2 * s2 * wk
    cross = s1 * s2 * (q - h11 * ss)
    sq2 = (
        s2 * s2 * kk
        - 2.0 * (h12 * h12 + h22 * h22)
        + h12 * h12 * (s1 * s1 * ss)
        + h22 * h22 * (s2 * s2 * ww)
        + 2.0 * h12 * h22 * cross
    )
    sq2 = jnp.maximum(sq2, 0.0)
    s3 = lax.rsqrt(sq2 + norm_eps)
    results = (h11, h12, h22, jnp.sqrt(sq1), jnp.sqrt(sq2), s2, s3 * s2, -s3 * h12 * s1, -s3 * h22 * s2)
    for j, value in enumerate(results):
        mix[j] = value[0, 0]
    out_w.wait()
    out_2.wait()


def combine(mix, kw_hbm, k2_hbm, start_hbm, basis_hbm, quot, coef, kw, k2, start, out, in_sem, out_sem):
    parts = [pl.ds(r, PIECE) for r in range(0, ROWS, PIECE)]
    ins = [
        [
            pltpu.make_async_copy(src.at[at], dst.at[at], in_sem.at[j, p])
            for j, (src, dst) in enumerate(((kw_hbm, kw), (k2_hbm, k2), (start_hbm, start)))
        ]
        for p, at in enumerate(parts)
    ]
    for cps in ins:
        for cp in cps:
            cp.start()
    quot[0] = mix[0]
    coef[0, 0] = mix[1]
    coef[0, 1] = mix[2]
    coef[1, 0] = mix[3]
    coef[1, 1] = mix[4]
    outs = []
    for p, at in enumerate(parts):
        for cp in ins[p]:
            cp.wait()
        w = kw[at, :]
        out[0, at, :] = mix[5] * w
        out[1, at, :] = mix[6] * k2[at, :] + mix[7] * start[at, :] + mix[8] * w
        for j in range(2):
            cp = pltpu.make_async_copy(out.at[j, at], basis_hbm.at[j, at], out_sem.at[j, p])
            cp.start()
            outs.append(cp)
    for cp in outs:
        cp.wait()


def per_device(hidden_in, targets, norm_gain, up_weight, down_weight, start):
    vm, dma = pltpu.VMEM, pltpu.SemaphoreType.DMA
    any_spec = pl.BlockSpec(memory_space=pl.ANY)
    vmem_spec = pl.BlockSpec(memory_space=pltpu.VMEM)
    smem_spec = pl.BlockSpec(memory_space=pltpu.SMEM)
    scratch = [
        vm((HID, D), bf16),
        vm((HID, D), bf16),
        vm((ROWS, D), f32),
        vm((PAD, D), bf16),
        vm((TOK, D), bf16),
        vm((CHUNKS, N_Z, OWN, W), bf16),
        vm((BLK, D), f32),
        vm((GRP, D), f32),
        vm((3, CHUNKS, HALF, W), bf16),
        vm((3, CHUNKS, HALF, W), bf16),
        vm((2, HALF, D), f32),
        vm((3, CHUNKS, BLK, W), bf16),
        vm((3, CHUNKS, BLK, W), bf16),
        vm((3, CHUNKS, 2, BLK, W), bf16),
        vm((3, CHUNKS, 2, BLK, W), bf16),
        vm((3, CHUNKS, N_Z, OWN, W), bf16),
        vm((3, CHUNKS, N_Z - 1, OWN, W), bf16),
        vm((3, CHUNKS, N_Z, OWN, W), bf16),
        vm((3, GRP, D), bf16),
        vm((GRP, HID), f32),
        vm((GRP, HID), f32),
        vm((GRP, HID), bf16),
        vm((2, GRP, HID), f32),
        vm((GRP, HID), f32),
        vm((GRP, HID), f32),
        vm((TOK, PAD), f32),
        vm((N_X, GRP, PAD), f32),
        vm((TOK, HID), bf16),
        vm((2, N_X, GRP, PAD), bf16),
        vm((GRP, TOK), f32),
        vm((ROWS, D), f32),
        vm((ROWS, D), f32),
        vm((2, 3, 4, 8, 128), f32),
        vm((2, 2, 15, 4, 8, 128), f32),
        vm((3, OWN, D), f32),
        vm((OWN, D), f32),
        dma((2 * N_X + 1,)),
    ]
    pairs = [
        (CHUNKS, N_Z - 1), (CHUNKS, 4), (CHUNKS, 4),
        (4,), (4,), (4,), (12,), (4,),
        (3, CHUNKS), (3, CHUNKS, 2), (3, CHUNKS, 2), (3, CHUNKS, N_Z - 1),
        (3, CHUNKS, N_Z - 1), (3, CHUNKS, 4), (3, CHUNKS, 4),
        (N_X - 1,), (4,), (N_X - 1,), (2, 2, 15),
    ]
    for shape in pairs:
        scratch += [dma(shape), dma(shape)]
    scratch.append(dma((2,)))
    kw, k2, mix = pl.pallas_call(
        kernel,
        out_shape=(
            jax.ShapeDtypeStruct((ROWS, D), f32),
            jax.ShapeDtypeStruct((ROWS, D), f32),
            jax.ShapeDtypeStruct((9,), f32),
        ),
        in_specs=[vmem_spec, vmem_spec, vmem_spec, any_spec, any_spec, any_spec],
        out_specs=(any_spec, any_spec, smem_spec),
        scratch_shapes=scratch,
        compiler_params=pltpu.CompilerParams(
            collective_id=0, has_side_effects=True, vmem_limit_bytes=60 * 1024 * 1024
        ),
        cost_estimate=pl.CostEstimate(flops=5 * 10**9, bytes_accessed=14 * 10**6, transcendentals=10**5),
    )(hidden_in, targets, norm_gain, up_weight, down_weight, start)
    pieces = ROWS // PIECE
    return pl.pallas_call(
        combine,
        out_shape=(
            jax.ShapeDtypeStruct((2, ROWS, D), f32),
            jax.ShapeDtypeStruct((1,), f32),
            jax.ShapeDtypeStruct((2, 2), f32),
        ),
        in_specs=[smem_spec, any_spec, any_spec, any_spec],
        out_specs=(any_spec, smem_spec, smem_spec),
        scratch_shapes=[
            vm((ROWS, D), f32),
            vm((ROWS, D), f32),
            vm((ROWS, D), f32),
            vm((2, ROWS, D), f32),
            dma((3, pieces)),
            dma((2, pieces)),
        ],
        compiler_params=pltpu.CompilerParams(vmem_limit_bytes=60 * 1024 * 1024),
        cost_estimate=pl.CostEstimate(flops=10**7, bytes_accessed=9 * 10**6, transcendentals=0),
    )(mix, kw, k2, start)


def solution(mesh):
    placed = (
        P(("dp", "zero"), None),
        P(("dp", "zero"), None),
        P(),
        P("zero", None),
        P("zero", None),
        P(("zero", "dp"), None),
    )
    return jax.shard_map(
        per_device,
        mesh=mesh,
        in_specs=placed,
        out_specs=(P(None, ("zero", "dp"), None), P(), P()),
        check_vma=False,
    )
```

```python
import jax
import jax.numpy as jnp
from jax import lax
from jax.experimental import pallas as pl
from jax.experimental.pallas import tpu as pltpu
from jax.sharding import PartitionSpec as P

MESH = pl.DeviceIdType.MESH
f32, bf16 = jnp.float32, jnp.bfloat16
norm_eps = 1e-06
gelu_coef = 0.7978845608028654

N_X, N_Y, N_Z, N_C = 4, 4, 8, 2
D = 4608
ROWS = 96
PAD = 128
HID = N_X * PAD
GRP = 128
TOK = N_X * GRP
HALF = GRP // N_C
BLK = HALF // N_Y
OWN = BLK // N_Z
CHUNKS = 2
W = D // CHUNKS
KEEP = 40
PIECE = 32
XA = 2560


def gelu_value(inputs):
    return (
        0.5 * inputs * (1.0 + jnp.tanh(gelu_coef * (inputs + 0.044715 * inputs * inputs * inputs)))
    )


def gelu_parts(inputs):
    unit_dir = jnp.ones_like(inputs)

    def first_slope(points):
        return jax.jvp(gelu_value, (points,), (unit_dir,))[1]

    return (
        gelu_value(inputs),
        first_slope(inputs),
        jax.jvp(first_slope, (inputs,), (unit_dir,))[1],
    )


def loss_parts(summed, target, gain):
    r = lax.rsqrt(jnp.sum(summed * summed, axis=-1, keepdims=True) / D + norm_eps)
    normed = summed * r
    pull = (normed * gain - target) * gain
    mean = jnp.sum(pull * normed, axis=-1, keepdims=True) / D
    return r, normed, pull, mean


def loss_grad(summed, target, gain):
    r, normed, pull, mean = loss_parts(summed, target, gain)
    return r * (pull - normed * mean) / float(TOK)


def loss_curv(summed, tangent, target, gain):
    r, normed, pull, mean = loss_parts(summed, target, gain)
    along = jnp.sum(normed * tangent, axis=-1, keepdims=True) / D
    d_normed = r * (tangent - normed * along)
    d_pull = d_normed * gain * gain
    d_mean = jnp.sum(d_pull * normed + pull * d_normed, axis=-1, keepdims=True) / D
    grad = r * (pull - normed * mean)
    d_grad = r * (d_pull - d_normed * mean - normed * d_mean) - (r * along) * grad
    return d_grad / float(TOK)


def dot_t(a, b):
    return lax.dot_general(a, b, (((1,), (1,)), ((), ())), preferred_element_type=f32)


def dot(a, b):
    return jnp.dot(a, b, preferred_element_type=f32)


def tile_sum(v):
    rows, cols = v.shape
    acc = v[0:8, :]
    for i in range(8, rows, 8):
        acc = acc + v[i : i + 8, :]
    out = acc[:, 0:128]
    for k in range(128, cols, 128):
        out = out + acc[:, k : k + 128]
    return out


def par(*gens):
    gens = list(gens)
    while gens:
        for g in list(gens):
            try:
                next(g)
            except StopIteration:
                gens.remove(g)
        if gens:
            yield


def run(*gens):
    for _ in par(*gens):
        pass


def play(gens, order):
    for j in order:
        next(gens[j], None)
    run(*gens)


def kernel(
    hin, tgt, gain, up_hbm, down_hbm, start_hbm,
    kw_hbm, k2_hbm, mix,
    up, down, start, sbf, X, xz, tmp16, part,
    sb, rc, s1f, y1b, y1r, y2b, y2r, sz, rz, az, A,
    slope, bendag, hact, agrad, pt1, ptx, pts, ptr,
    pfull, pr2, g_hi, g_lo, kw, k2, arv, arr, tot, bsum,
    ld_sem, xz_s, xz_r, xy_s, xy_r, xc_s, xc_r,
    xa_s, xa_r, xac_s, xac_r, xb_s, xb_r, xby_s, xby_r, xbc_s, xbc_r,
    rc_s, rc_r, y1_s, y1_r, y2_s, y2_r, rz_s, rz_r,
    az_s, az_r, ay_s, ay_r, ac_s, ac_r,
    pt_s, pt_r, pf_s, pf_r, p2_s, p2_r, ar_s, ar_r, out_sem,
):
    x = lax.axis_index("dp")
    shard = lax.axis_index("zero")
    y, z, c = shard // 16, (shard // 2) % 8, shard % 2

    def dev(nx, ny, nz, nc):
        return (nx, ny * 16 + nz * 2 + nc)

    pending = []

    def x_at(k):
        return (x + (k % N_X)) % N_X

    def y_at(k):
        return (y + (k % N_Y)) % N_Y

    def x_peer(k):
        return dev(x_at(k), y, z, c)

    def y_peer(k):
        return dev(x, y_at(k), z, c)

    def z_peer(k):
        return dev(x, y, (z + k) % N_Z, c)

    c_peer = dev(x, y, z, 1 - c)

    def xy_peer(k):
        return dev(x_at(k // N_Y), y_at(k % N_Y), z, c)

    def zc_peer(k):
        return dev(x, y, (z + k // N_C) % N_Z, (c + k % N_C) % N_C)

    def send(src, dst, ssem, rsem, to):
        cp = pltpu.make_async_remote_copy(
            src_ref=src, dst_ref=dst, send_sem=ssem, recv_sem=rsem, device_id=to, device_id_type=MESH
        )
        cp.start()
        pending.append(cp)
        return cp

    def send_all(copies, bytes_of, ssem, rsem):
        for src, dst, to in copies:
            pltpu.make_async_remote_copy(
                src_ref=src, dst_ref=dst, send_sem=ssem, recv_sem=rsem, device_id=to, device_id_type=MESH
            ).start()
        cp = pltpu.make_async_remote_copy(
            src_ref=bytes_of,
            dst_ref=bytes_of,
            send_sem=ssem,
            recv_sem=rsem,
            device_id=c_peer,
            device_id_type=MESH,
        )
        pending.append(cp)
        return [cp]

    def settle(keep=KEEP):
        while len(pending) > keep:
            pending.pop(0).wait_send()

    def rows(start_row, count):
        return pl.ds(pl.multiple_of(start_row, 16), count)

    def wait_all(cps):
        settle()
        for cp in cps:
            cp.wait_recv()

    loads = []
    for b in range(N_X):
        for j, (src, dst) in enumerate(((up_hbm, up), (down_hbm, down))):
            loads.append(
                pltpu.make_async_copy(
                    src.at[pl.ds(b * ROWS, ROWS)], dst.at[pl.ds(b * PAD, ROWS)], ld_sem.at[2 * b + j]
                )
            )
    loads.append(pltpu.make_async_copy(start_hbm, start, ld_sem.at[2 * N_X]))
    for cp in loads:
        cp.start()

    barrier = pltpu.get_barrier_semaphore()
    peers = [xy_peer(k) for k in range(1, N_X * N_Y)] + [zc_peer(k) for k in range(1, N_Z * N_C)]
    for p in peers:
        pl.semaphore_signal(barrier, inc=1, device_id=p, device_id_type=MESH)
    pl.semaphore_wait(barrier, len(peers))

    def ring_gather(ref, blocks, c0, w, peer, ssem, rsem, then=None):
        half = w // 2
        nb = len(blocks)
        first = []
        for b, (row_of, count) in enumerate(blocks):
            at = (rows(row_of(0), count), pl.ds(c0, w))
            first.append(
                [
                    send(ref.at[at], ref.at[at], ssem.at[2 * b + j], rsem.at[2 * b + j], peer(to))
                    for j, to in enumerate((1, -1))
                ]
            )
        if then:
            then(0)
        yield
        second = []
        for b, (row_of, count) in enumerate(blocks):
            for j, to in enumerate((1, -1)):
                wait_all([first[b][j]])
                at = (rows(row_of(-to), count), pl.ds(c0 + j * half, half))
                i = 2 * (nb + b) + j
                second.append(send(ref.at[at], ref.at[at], ssem.at[i], rsem.at[i], peer(to)))
        if then:
            then(-1)
            then(1)
        yield
        wait_all(second)
        if then:
            then(2)

    def gather_z(own, buf, ssem, rsem):
        buf[z] = own
        copies = [(buf.at[z], buf.at[z], z_peer(k)) for k in range(1, N_Z)]
        return send_all(copies, buf.at[pl.ds(0, N_Z - 1)], ssem, rsem)

    def join16(buf, c0, w):
        for j in range(N_Z):
            tmp16[pl.ds(OWN * j, OWN), c0 : c0 + w] = buf[j].astype(f32)
        return tmp16[:, c0 : c0 + w].astype(bf16)

    def gather(own, i, h):
        c0, out = h * W, A.at[i]
        cols = pl.ds(c0, W)
        cps = gather_z(own[:, c0 : c0 + W], az.at[i, h], az_s.at[i, h], az_r.at[i, h])
        yield
        wait_all(cps)
        out[rows(c * HALF + y * BLK, BLK), cols] = join16(az.at[i, h], c0, W)
        passed = []

        def pass_on(k):
            at = (rows(c * HALF + y_at(k) * BLK, BLK), cols)
            passed.append(send(out.at[at], out.at[at], ac_s.at[i, h, k % 4], ac_r.at[i, h, k % 4], c_peer))

        yield from ring_gather(
            out,
            [(lambda k: c * HALF + y_at(k) * BLK, BLK)],
            c0,
            W,
            y_peer,
            ay_s.at[i, h],
            ay_r.at[i, h],
            pass_on,
        )
        yield
        wait_all(passed)
        part_grad = dot_t(out[:, cols], down[:, cols])
        if h == 0:
            agrad[i % 2] = part_grad
        else:
            agrad[i % 2] = agrad[i % 2] + part_grad

    def scatter(i, h, make=None):
        c0 = h * W
        cols = slice(c0, c0 + W)
        if make is not None:
            make(h)
        sb[i, h] = part[rows((1 - c) * HALF, HALF), cols].astype(bf16)
        cps = [send(sb.at[i, h], rc.at[i, h], rc_s.at[i, h], rc_r.at[i, h], c_peer)]
        yield
        wait_all(cps)
        s1f[i % 2, :, cols] = part[rows(c * HALF, HALF), cols] + rc[i, h].astype(f32)

        def block(k):
            return s1f[i % 2, rows(y_at(k) * BLK, BLK), cols]

        half = W // 2
        y1b[i, h] = block(2).astype(bf16)
        cps = [
            send(
                y1b.at[i, h, :, pl.ds(j * half, half)],
                y1r.at[i, h, :, pl.ds(j * half, half)],
                y1_s.at[i, h, j],
                y1_r.at[i, h, j],
                y_peer(to),
            )
            for j, to in enumerate((1, -1))
        ]
        yield
        wait_all(cps)
        got = y1r[i, h].astype(f32)
        for j, to in enumerate((1, -1)):
            mine = block(to)
            if j == 0:
                pieces = [mine[:, :half] + got[:, :half], mine[:, half:]]
            else:
                pieces = [mine[:, :half], mine[:, half:] + got[:, half:]]
            y2b[i, h, j, :, pl.ds(0, half)] = pieces[0].astype(bf16)
            y2b[i, h, j, :, pl.ds(half, half)] = pieces[1].astype(bf16)
        cps = [
            send(y2b.at[i, h, j], y2r.at[i, h, j], y2_s.at[i, h, j], y2_r.at[i, h, j], y_peer(to))
            for j, to in enumerate((1, -1))
        ]
        yield
        wait_all(cps)
        tmp16[:, cols] = block(0) + y2r[i, h, 0].astype(f32) + y2r[i, h, 1].astype(f32)
        for j in range(N_Z):
            sz[i, h, j] = tmp16[pl.ds(OWN * j, OWN), cols].astype(bf16)
        copies = [(sz.at[i, h, (z + k) % N_Z], rz.at[i, h, k - 1], z_peer(k)) for k in range(1, N_Z)]
        cps = send_all(copies, rz.at[i, h], rz_s.at[i, h], rz_r.at[i, h])
        yield
        wait_all(cps)
        s3 = sz[i, h, z].astype(f32)
        for k in range(N_Z - 1):
            s3 = s3 + rz[i, h, k].astype(f32)
        tot[i, :, cols] = s3

    def scatters(i, make):
        return par(*[scatter(i, h, make) for h in range(CHUNKS)])

    def gathers(own, i):
        return par(*[gather(own, i, h) for h in range(CHUNKS)])

    def all_sum(i, n):
        for s, peer in enumerate((xy_peer, zc_peer)):
            copies = [
                (arv.at[i, s, pl.ds(0, n)], arr.at[i, s, k - 1, pl.ds(0, n)], peer(k)) for k in range(1, 16)
            ]
            cps = send_all(copies, arr.at[i, s, :, pl.ds(0, n)], ar_s.at[i, s], ar_r.at[i, s])
            yield
            wait_all(cps)
            acc = arv[i, s, 0:n]
            for k in range(1, 16):
                acc = acc + arr[i, s, k - 1, 0:n]
            arv[i, s + 1, 0:n] = acc

    group = rows(x * GRP, GRP)

    def group_tokens(h):
        c0 = h * W
        cols = pl.ds(c0, W)
        cps = gather_z(hin[:, c0 : c0 + W], xz.at[h], xz_s.at[h], xz_r.at[h])
        yield
        wait_all(cps)
        X[rows(x * GRP + c * HALF + y * BLK, BLK), cols] = join16(xz.at[h], c0, W)
        passed = []

        def pass_on(k):
            at = (rows(x * GRP + c * HALF + y_at(k) * BLK, BLK), cols)
            passed.append(send(X.at[at], X.at[at], xc_s.at[h, k % 4], xc_r.at[h, k % 4], c_peer))

        yield from ring_gather(
            X,
            [(lambda k: x * GRP + c * HALF + y_at(k) * BLK, BLK)],
            c0,
            W,
            y_peer,
            xy_s.at[h],
            xy_r.at[h],
            pass_on,
        )
        yield
        wait_all(passed)
        pre = dot_t(X[group, cols], up[:, cols])
        if h == 0:
            agrad[0] = pre
        else:
            agrad[0] = agrad[0] + pre

    def local_work():
        for b in range(N_X):
            up[pl.ds(b * PAD + ROWS, PAD - ROWS), :] = jnp.zeros((PAD - ROWS, D), bf16)
            down[pl.ds(b * PAD + ROWS, PAD - ROWS), :] = jnp.zeros((PAD - ROWS, D), bf16)
        sbf[pl.ds(ROWS, PAD - ROWS), :] = jnp.zeros((PAD - ROWS, D), bf16)
        yield
        for cp in loads:
            cp.wait()
        sbf[pl.ds(0, ROWS), :] = start[...].astype(bf16)
        yield
        arv[0, 0, 1] = tile_sum(start[...] * start[...])

    own_xb = ring_gather(
        X, [(lambda k: x_at(k) * GRP + c * HALF + y * BLK, BLK)], XA, D - XA, x_peer, xb_s, xb_r
    )
    tok_gens = [group_tokens(h) for h in range(CHUNKS)]

    def later_xb():
        for _ in range(2):
            next(own_xb)
            yield

    both = list(range(CHUNKS))
    n = CHUNKS
    play(tok_gens + [local_work(), later_xb()], both + [n] + both + [n + 1, n] + both + [n + 1, n] + both)

    def tokens_yx():
        passed = []

        def pass_on(k):
            if k != 0:
                at = (rows(x_at(k) * GRP + c * HALF, HALF), pl.ds(0, XA))
                passed.append(send(X.at[at], X.at[at], xac_s.at[k % 4], xac_r.at[k % 4], c_peer))

        yield from ring_gather(
            X, [(lambda k: x_at(k) * GRP + c * HALF, HALF)], 0, XA, x_peer, xa_s, xa_r, pass_on
        )
        yield
        wait_all(passed)

    def tokens_xy():
        next(own_xb, None)
        blocks = [
            (lambda k, b=b: x_at(b) * GRP + c * HALF + y_at(k) * BLK, BLK) for b in range(1, N_X)
        ]
        yield from ring_gather(X, blocks, XA, D - XA, y_peer, xby_s, xby_r)
        passed = []
        for b in range(1, N_X):
            at = (rows(x_at(b) * GRP + c * HALF, HALF), pl.ds(XA, D - XA))
            passed.append(send(X.at[at], X.at[at], xbc_s.at[b], xbc_r.at[b], c_peer))
        yield
        wait_all(passed)

    def to_branch(h):
        for k in range(h * W, (h + 1) * W, W // 3):
            part[:, k : k + W // 3] = dot(hact[...], down[:, k : k + W // 3])

    def weights():
        return tgt[...].astype(f32), gain[...]

    def forward():
        for b in range(N_X):
            cols = pl.ds(b * PAD, PAD)
            value, first, second = gelu_parts(agrad[0, :, cols])
            hact[:, cols] = value.astype(bf16)
            slope[:, cols] = first
            bendag[:, cols] = second
        yield from scatters(0, to_branch)
        bsum[...] = hin[...].astype(f32) + tot[0]
        yield from gathers(loss_grad(bsum[...], *weights()).astype(bf16), 0)
        bendag[...] = bendag[...] * agrad[0]

    def first_tangent():
        pts[...] = dot_t(X[...], sbf[...])
        ptr[x] = pts[group, :]
        cps = [
            send(
                pts.at[rows(x_at(k) * GRP, GRP)], ptr.at[x], pt_s.at[k - 1], pt_r.at[k - 1], x_peer(k)
            )
            for k in range(1, N_X)
        ]
        yield
        wait_all(cps)
        for b in range(N_X):
            cols = pl.ds(b * PAD, PAD)
            pt1[:, cols] = ptr[b]
            hact[:, cols] = (slope[:, cols] * ptr[b]).astype(bf16)
        yield from scatters(1, to_branch)

    fwd = forward()
    yx, xy = tokens_yx(), tokens_xy()
    for g in (yx, xy, fwd, xy, fwd, xy, fwd, yx, fwd, yx, fwd, xy, yx):
        next(g, None)
    run(xy, yx)
    play((first_tangent(), fwd), (0, 1, 0, 1))
    curv = loss_curv(bsum[...], tot[1], *weights())

    def token_gram():
        half = TOK // 2
        for b in range(2):
            g = dot_t(X[group, :], X[pl.ds(b * half, half), :])
            hi = g.astype(bf16)
            g_hi[:, pl.ds(b * half, half)] = hi
            g_lo[:, pl.ds(b * half, half)] = (g - hi.astype(f32)).astype(bf16)
            yield

    run(gathers(curv.astype(bf16), 1), token_gram())
    p1 = agrad[1] * slope[...] + bendag[...] * pt1[...]
    pfull[group, :] = p1.astype(bf16)

    def share_p1():
        def use(k):
            block = rows(x_at(k) * GRP, GRP)
            term = dot(g_hi[:, block], pfull[block, :]) + dot(g_lo[:, block], pfull[block, :])
            if k == 0:
                ptx[...] = term
            else:
                ptx[...] = ptx[...] + term

        yield from ring_gather(pfull, [(lambda k: x_at(k) * GRP, GRP)], 0, HID, x_peer, pf_s, pf_r, use)

    def own_sums():
        arv[0, 0, 0] = tile_sum(p1 * pt1[...])
        yield

    run(share_p1(), own_sums())

    hact[...] = (slope[...] * ptx[...]).astype(bf16)

    def image_one():
        own = pfull[:, pl.ds(pl.multiple_of(x * PAD, PAD), PAD)].T
        for k in range(0, D, 512):
            kw[:, k : k + 512] = dot(own, X[:, k : k + 512])[0:ROWS, :]
            if k % 1536 == 1024:
                yield

    run(scatters(2, to_branch), all_sum(0, 2), image_one())
    count = float(ROWS * 256 * D)
    q = jnp.sum(arv[0, 2, 0], keepdims=True) / count
    ss = jnp.sum(arv[0, 2, 1], keepdims=True) / count
    s1 = lax.rsqrt(ss + norm_eps)
    h11 = s1 * s1 * q
    curv = loss_curv(bsum[...], tot[2] - h11 * tot[1], *weights())

    def remainder():
        ptx[...] = ptx[...] - h11 * pt1[...]
        acc = None
        for k in range(0, D, 1536):
            w = kw[:, k : k + 1536] - h11 * start[:, k : k + 1536]
            kw[:, k : k + 1536] = w
            s = tile_sum(w * w)
            acc = s if acc is None else acc + s
            yield
        arv[1, 0, 0] = acc

    run(gathers(curv.astype(bf16), 2), remainder())
    out_w = pltpu.make_async_copy(kw, kw_hbm, out_sem.at[0])
    out_w.start()
    for b in range(N_X):
        cols = pl.ds(b * PAD, PAD)
        pr2[1, b] = (agrad[0, :, cols] * slope[:, cols] + bendag[:, cols] * ptx[:, cols]).astype(bf16)
    pr2[0, x] = pr2[1, x]
    cps = [
        send(pr2.at[1, x_at(k)], pr2.at[0, x], p2_s.at[k - 1], p2_r.at[k - 1], x_peer(k))
        for k in range(1, N_X)
    ]
    wait_all(cps)
    own = pr2[0].reshape(TOK, PAD).T
    sums = [None, None, None]
    for k in range(0, D, 512):
        cols = slice(k, k + 512)
        acc = dot(own, X[:, cols])[0:ROWS, :]
        k2[:, cols] = acc
        for j, other in enumerate((start[:, cols], kw[:, cols], acc)):
            s = tile_sum(other * acc)
            sums[j] = s if sums[j] is None else sums[j] + s
    for j in range(3):
        arv[1, 0, 1 + j] = sums[j]
    out_2 = pltpu.make_async_copy(k2, k2_hbm, out_sem.at[1])
    out_2.start()
    run(all_sum(1, 4))
    ww, sk, wk, kk = [jnp.sum(arv[1, 2, j], keepdims=True) / count for j in range(4)]
    sq1 = s1 * s1 * ww
    scale2 = lax.rsqrt(sq1 + norm_eps)
    s2 = scale2 * s1
    h12 = s1 * s2 * sk
    h22 = s2 * s2 * wk
    cross = s1 * s2 * (q - h11 * ss)
    sq2 = (
        s2 * s2 * kk
        - 2.0 * (h12 * h12 + h22 * h22)
        + h12 * h12 * (s1 * s1 * ss)
        + h22 * h22 * (s2 * s2 * ww)
        + 2.0 * h12 * h22 * cross
    )
    sq2 = jnp.maximum(sq2, 0.0)
    s3 = lax.rsqrt(sq2 + norm_eps)
    results = (h11, h12, h22, jnp.sqrt(sq1), jnp.sqrt(sq2), s2, s3 * s2, -s3 * h12 * s1, -s3 * h22 * s2)
    for j, value in enumerate(results):
        mix[j] = value[0, 0]
    out_w.wait()
    out_2.wait()
    settle(0)


def combine(mix, kw_hbm, k2_hbm, start_hbm, basis_hbm, quot, coef, kw, k2, start, out, in_sem, out_sem):
    parts = [pl.ds(r, PIECE) for r in range(0, ROWS, PIECE)]
    ins = [
        [
            pltpu.make_async_copy(src.at[at], dst.at[at], in_sem.at[j, p])
            for j, (src, dst) in enumerate(((kw_hbm, kw), (k2_hbm, k2), (start_hbm, start)))
        ]
        for p, at in enumerate(parts)
    ]
    for cps in ins:
        for cp in cps:
            cp.start()
    quot[0] = mix[0]
    coef[0, 0] = mix[1]
    coef[0, 1] = mix[2]
    coef[1, 0] = mix[3]
    coef[1, 1] = mix[4]
    outs = []
    for p, at in enumerate(parts):
        for cp in ins[p]:
            cp.wait()
        w = kw[at, :]
        out[0, at, :] = mix[5] * w
        out[1, at, :] = mix[6] * k2[at, :] + mix[7] * start[at, :] + mix[8] * w
        for j in range(2):
            cp = pltpu.make_async_copy(out.at[j, at], basis_hbm.at[j, at], out_sem.at[j, p])
            cp.start()
            outs.append(cp)
    for cp in outs:
        cp.wait()


def per_device(hidden_in, targets, norm_gain, up_weight, down_weight, start):
    vm, dma = pltpu.VMEM, pltpu.SemaphoreType.DMA
    any_spec = pl.BlockSpec(memory_space=pl.ANY)
    vmem_spec = pl.BlockSpec(memory_space=pltpu.VMEM)
    smem_spec = pl.BlockSpec(memory_space=pltpu.SMEM)
    scratch = [
        vm((HID, D), bf16),
        vm((HID, D), bf16),
        vm((ROWS, D), f32),
        vm((PAD, D), bf16),
        vm((TOK, D), bf16),
        vm((CHUNKS, N_Z, OWN, W), bf16),
        vm((BLK, D), f32),
        vm((GRP, D), f32),
        vm((3, CHUNKS, HALF, W), bf16),
        vm((3, CHUNKS, HALF, W), bf16),
        vm((2, HALF, D), f32),
        vm((3, CHUNKS, BLK, W), bf16),
        vm((3, CHUNKS, BLK, W), bf16),
        vm((3, CHUNKS, 2, BLK, W), bf16),
        vm((3, CHUNKS, 2, BLK, W), bf16),
        vm((3, CHUNKS, N_Z, OWN, W), bf16),
        vm((3, CHUNKS, N_Z - 1, OWN, W), bf16),
        vm((3, CHUNKS, N_Z, OWN, W), bf16),
        vm((3, GRP, D), bf16),
        vm((GRP, HID), f32),
        vm((GRP, HID), f32),
        vm((GRP, HID), bf16),
        vm((2, GRP, HID), f32),
        vm((GRP, HID), f32),
        vm((GRP, HID), f32),
        vm((TOK, PAD), f32),
        vm((N_X, GRP, PAD), f32),
        vm((TOK, HID), bf16),
        vm((2, N_X, GRP, PAD), bf16),
        vm((GRP, TOK), bf16),
        vm((GRP, TOK), bf16),
        vm((ROWS, D), f32),
        vm((ROWS, D), f32),
        vm((2, 3, 4, 8, 128), f32),
        vm((2, 2, 15, 4, 8, 128), f32),
        vm((3, OWN, D), f32),
        vm((OWN, D), f32),
        dma((2 * N_X + 1,)),
    ]
    pairs = [
        (CHUNKS,), (CHUNKS, 4), (CHUNKS, 4),
        (4,), (4,), (4,), (12,), (4,),
        (3, CHUNKS), (3, CHUNKS, 2), (3, CHUNKS, 2), (3, CHUNKS),
        (3, CHUNKS), (3, CHUNKS, 4), (3, CHUNKS, 4),
        (N_X - 1,), (4,), (N_X - 1,), (2, 2),
    ]
    for shape in pairs:
        scratch += [dma(shape), dma(shape)]
    scratch.append(dma((2,)))
    kw, k2, mix = pl.pallas_call(
        kernel,
        out_shape=(
            jax.ShapeDtypeStruct((ROWS, D), f32),
            jax.ShapeDtypeStruct((ROWS, D), f32),
            jax.ShapeDtypeStruct((9,), f32),
        ),
        in_specs=[vmem_spec, vmem_spec, vmem_spec, any_spec, any_spec, any_spec],
        out_specs=(any_spec, any_spec, smem_spec),
        scratch_shapes=scratch,
        compiler_params=pltpu.CompilerParams(
            collective_id=0, has_side_effects=True, vmem_limit_bytes=60 * 1024 * 1024
        ),
        cost_estimate=pl.CostEstimate(flops=5 * 10**9, bytes_accessed=14 * 10**6, transcendentals=10**5),
    )(hidden_in, targets, norm_gain, up_weight, down_weight, start)
    pieces = ROWS // PIECE
    return pl.pallas_call(
        combine,
        out_shape=(
            jax.ShapeDtypeStruct((2, ROWS, D), f32),
            jax.ShapeDtypeStruct((1,), f32),
            jax.ShapeDtypeStruct((2, 2), f32),
        ),
        in_specs=[smem_spec, any_spec, any_spec, any_spec],
        out_specs=(any_spec, smem_spec, smem_spec),
        scratch_shapes=[
            vm((ROWS, D), f32),
            vm((ROWS, D), f32),
            vm((ROWS, D), f32),
            vm((2, ROWS, D), f32),
            dma((3, pieces)),
            dma((2, pieces)),
        ],
        compiler_params=pltpu.CompilerParams(vmem_limit_bytes=60 * 1024 * 1024),
        cost_estimate=pl.CostEstimate(flops=10**7, bytes_accessed=9 * 10**6, transcendentals=0),
    )(mix, kw, k2, start)


def solution(mesh):
    placed = (
        P(("dp", "zero"), None),
        P(("dp", "zero"), None),
        P(),
        P("zero", None),
        P("zero", None),
        P(("zero", "dp"), None),
    )
    return jax.shard_map(
        per_device,
        mesh=mesh,
        in_specs=placed,
        out_specs=(P(None, ("zero", "dp"), None), P(), P()),
        check_vma=False,
    )
```

```python
import jax
import jax.numpy as jnp
from jax import lax
from jax.experimental import pallas as pl
from jax.experimental.pallas import tpu as pltpu
from jax.sharding import PartitionSpec as P

MESH = pl.DeviceIdType.MESH
f32, bf16 = jnp.float32, jnp.bfloat16
norm_eps = 1e-06
gelu_coef = 0.7978845608028654

N_X, N_Y, N_Z, N_C = 4, 4, 8, 2
D = 4608
ROWS = 96
PAD = 128
HID = N_X * PAD
GRP = 128
TOK = N_X * GRP
HALF = GRP // N_C
BLK = HALF // N_Y
OWN = BLK // N_Z
CHUNKS = 2
W = D // CHUNKS
KEEP = 40
PIECE = 32
XA = 2560


def gelu_value(inputs):
    return (
        0.5 * inputs * (1.0 + jnp.tanh(gelu_coef * (inputs + 0.044715 * inputs * inputs * inputs)))
    )


def gelu_parts(inputs):
    unit_dir = jnp.ones_like(inputs)

    def first_slope(points):
        return jax.jvp(gelu_value, (points,), (unit_dir,))[1]

    return (
        gelu_value(inputs),
        first_slope(inputs),
        jax.jvp(first_slope, (inputs,), (unit_dir,))[1],
    )


def loss_parts(summed, target, gain):
    r = lax.rsqrt(jnp.sum(summed * summed, axis=-1, keepdims=True) / D + norm_eps)
    normed = summed * r
    pull = (normed * gain - target) * gain
    mean = jnp.sum(pull * normed, axis=-1, keepdims=True) / D
    return r, normed, pull, mean


def loss_grad(summed, target, gain):
    r, normed, pull, mean = loss_parts(summed, target, gain)
    return r * (pull - normed * mean) / float(TOK)


def loss_curv(summed, tangent, target, gain):
    r, normed, pull, mean = loss_parts(summed, target, gain)
    along = jnp.sum(normed * tangent, axis=-1, keepdims=True) / D
    d_normed = r * (tangent - normed * along)
    d_pull = d_normed * gain * gain
    d_mean = jnp.sum(d_pull * normed + pull * d_normed, axis=-1, keepdims=True) / D
    grad = r * (pull - normed * mean)
    d_grad = r * (d_pull - d_normed * mean - normed * d_mean) - (r * along) * grad
    return d_grad / float(TOK)


def dot_t(a, b):
    return lax.dot_general(a, b, (((1,), (1,)), ((), ())), preferred_element_type=f32)


def dot(a, b):
    return jnp.dot(a, b, preferred_element_type=f32)


def tile_sum(v):
    rows, cols = v.shape
    acc = v[0:8, :]
    for i in range(8, rows, 8):
        acc = acc + v[i : i + 8, :]
    out = acc[:, 0:128]
    for k in range(128, cols, 128):
        out = out + acc[:, k : k + 128]
    return out


def par(*gens):
    gens = list(gens)
    while gens:
        for g in list(gens):
            try:
                next(g)
            except StopIteration:
                gens.remove(g)
        if gens:
            yield


def run(*gens):
    for _ in par(*gens):
        pass


def play(gens, order):
    for j in order:
        next(gens[j], None)
    run(*gens)


def kernel(
    hin, tgt, gain, up_hbm, down_hbm, start_hbm,
    kw_hbm, k2_hbm, mix,
    up, down, start, sbf, X, xz, tmp16, part,
    sb, rc, s1f, y1b, y1r, y2b, y2r, sz, rz, az, A,
    slope, bendag, hact, agrad, pt1, ptx, pts,
    pfull, pr2, gram, kw, k2, arv, arr, tot, bsum,
    ld_sem, xz_s, xz_r, xy_s, xy_r, xc_s, xc_r,
    xa_s, xa_r, xac_s, xac_r, xb_s, xb_r, xby_s, xby_r, xbc_s, xbc_r,
    rc_s, rc_r, y1_s, y1_r, y2_s, y2_r, rz_s, rz_r,
    az_s, az_r, ay_s, ay_r, ac_s, ac_r,
    pt_s, pt_r, pf_s, pf_r, p2_s, p2_r, ar_s, ar_r, out_sem,
):
    x = lax.axis_index("dp")
    shard = lax.axis_index("zero")
    y, z, c = shard // 16, (shard // 2) % 8, shard % 2

    def dev(nx, ny, nz, nc):
        return (nx, ny * 16 + nz * 2 + nc)

    pending = []

    def x_at(k):
        return (x + (k % N_X)) % N_X

    def y_at(k):
        return (y + (k % N_Y)) % N_Y

    def x_peer(k):
        return dev(x_at(k), y, z, c)

    def y_peer(k):
        return dev(x, y_at(k), z, c)

    def z_peer(k):
        return dev(x, y, (z + k) % N_Z, c)

    c_peer = dev(x, y, z, 1 - c)

    def xy_peer(k):
        return dev(x_at(k // N_Y), y_at(k % N_Y), z, c)

    def zc_peer(k):
        return dev(x, y, (z + k // N_C) % N_Z, (c + k % N_C) % N_C)

    def send(src, dst, ssem, rsem, to):
        cp = pltpu.make_async_remote_copy(
            src_ref=src, dst_ref=dst, send_sem=ssem, recv_sem=rsem, device_id=to, device_id_type=MESH
        )
        cp.start()
        pending.append(cp)
        return cp

    def send_all(copies, bytes_of, ssem, rsem):
        for src, dst, to in copies:
            pltpu.make_async_remote_copy(
                src_ref=src, dst_ref=dst, send_sem=ssem, recv_sem=rsem, device_id=to, device_id_type=MESH
            ).start()
        cp = pltpu.make_async_remote_copy(
            src_ref=bytes_of,
            dst_ref=bytes_of,
            send_sem=ssem,
            recv_sem=rsem,
            device_id=c_peer,
            device_id_type=MESH,
        )
        pending.append(cp)
        return [cp]

    def settle(keep=KEEP):
        while len(pending) > keep:
            pending.pop(0).wait_send()

    def rows(start_row, count):
        return pl.ds(pl.multiple_of(start_row, 16), count)

    def wait_all(cps):
        settle()
        for cp in cps:
            cp.wait_recv()

    loads = []
    for b in range(N_X):
        for j, (src, dst) in enumerate(((up_hbm, up), (down_hbm, down))):
            loads.append(
                pltpu.make_async_copy(
                    src.at[pl.ds(b * ROWS, ROWS)], dst.at[pl.ds(b * PAD, ROWS)], ld_sem.at[2 * b + j]
                )
            )
    loads.append(pltpu.make_async_copy(start_hbm, start, ld_sem.at[2 * N_X]))
    for cp in loads:
        cp.start()

    barrier = pltpu.get_barrier_semaphore()
    peers = [xy_peer(k) for k in range(1, N_X * N_Y)] + [zc_peer(k) for k in range(1, N_Z * N_C)]
    for p in peers:
        pl.semaphore_signal(barrier, inc=1, device_id=p, device_id_type=MESH)
    pl.semaphore_wait(barrier, len(peers))

    def ring_gather(ref, blocks, c0, w, peer, ssem, rsem, then=None, by_rows=False):
        half = w // 2
        nb = len(blocks)
        first = []
        for b, (row_of, count) in enumerate(blocks):
            at = (rows(row_of(0), count), pl.ds(c0, w))
            first.append(
                [
                    send(ref.at[at], ref.at[at], ssem.at[2 * b + j], rsem.at[2 * b + j], peer(to))
                    for j, to in enumerate((1, -1))
                ]
            )
        if then:
            then(0)
        yield
        second = []
        for b, (row_of, count) in enumerate(blocks):
            for j, to in enumerate((1, -1)):
                wait_all([first[b][j]])
                if by_rows:
                    at = (rows(row_of(-to) + j * (count // 2), count // 2), pl.ds(c0, w))
                else:
                    at = (rows(row_of(-to), count), pl.ds(c0 + j * half, half))
                i = 2 * (nb + b) + j
                second.append(send(ref.at[at], ref.at[at], ssem.at[i], rsem.at[i], peer(to)))
        if then:
            then(-1)
            then(1)
        yield
        wait_all(second)
        if then:
            then(2)

    def gather_z(own, buf, ssem, rsem):
        buf[z] = own
        copies = [(buf.at[z], buf.at[z], z_peer(k)) for k in range(1, N_Z)]
        return send_all(copies, buf.at[pl.ds(0, N_Z - 1)], ssem, rsem)

    def join16(buf, c0, w):
        for j in range(N_Z):
            tmp16[pl.ds(OWN * j, OWN), c0 : c0 + w] = buf[j].astype(f32)
        return tmp16[:, c0 : c0 + w].astype(bf16)

    def gather(own, i, h):
        c0, out = h * W, A.at[i]
        cols = pl.ds(c0, W)
        cps = gather_z(own[:, c0 : c0 + W], az.at[i, h], az_s.at[i, h], az_r.at[i, h])
        yield
        wait_all(cps)
        out[rows(c * HALF + y * BLK, BLK), cols] = join16(az.at[i, h], c0, W)
        passed = []

        def pass_on(k):
            at = (rows(c * HALF + y_at(k) * BLK, BLK), cols)
            passed.append(send(out.at[at], out.at[at], ac_s.at[i, h, k % 4], ac_r.at[i, h, k % 4], c_peer))

        yield from ring_gather(
            out,
            [(lambda k: c * HALF + y_at(k) * BLK, BLK)],
            c0,
            W,
            y_peer,
            ay_s.at[i, h],
            ay_r.at[i, h],
            pass_on,
        )
        yield
        wait_all(passed)
        part_grad = dot_t(down[:, cols], out[:, cols])
        if h == 0:
            agrad[i % 2] = part_grad
        else:
            agrad[i % 2] = agrad[i % 2] + part_grad

    def scatter(i, h, make=None):
        c0 = h * W
        cols = slice(c0, c0 + W)
        if make is not None:
            make(h)
        sb[i, h] = part[rows((1 - c) * HALF, HALF), cols].astype(bf16)
        cps = [send(sb.at[i, h], rc.at[i, h], rc_s.at[i, h], rc_r.at[i, h], c_peer)]
        yield
        wait_all(cps)
        s1f[i % 2, :, cols] = part[rows(c * HALF, HALF), cols] + rc[i, h].astype(f32)

        def block(k):
            return s1f[i % 2, rows(y_at(k) * BLK, BLK), cols]

        half = W // 2
        y1b[i, h] = block(2).astype(bf16)
        cps = [
            send(
                y1b.at[i, h, :, pl.ds(j * half, half)],
                y1r.at[i, h, :, pl.ds(j * half, half)],
                y1_s.at[i, h, j],
                y1_r.at[i, h, j],
                y_peer(to),
            )
            for j, to in enumerate((1, -1))
        ]
        yield
        wait_all(cps)
        got = y1r[i, h].astype(f32)
        for j, to in enumerate((1, -1)):
            mine = block(to)
            if j == 0:
                pieces = [mine[:, :half] + got[:, :half], mine[:, half:]]
            else:
                pieces = [mine[:, :half], mine[:, half:] + got[:, half:]]
            y2b[i, h, j, :, pl.ds(0, half)] = pieces[0].astype(bf16)
            y2b[i, h, j, :, pl.ds(half, half)] = pieces[1].astype(bf16)
        cps = [
            send(y2b.at[i, h, j], y2r.at[i, h, j], y2_s.at[i, h, j], y2_r.at[i, h, j], y_peer(to))
            for j, to in enumerate((1, -1))
        ]
        yield
        wait_all(cps)
        tmp16[:, cols] = block(0) + y2r[i, h, 0].astype(f32) + y2r[i, h, 1].astype(f32)
        for j in range(N_Z):
            sz[i, h, j] = tmp16[pl.ds(OWN * j, OWN), cols].astype(bf16)
        copies = [(sz.at[i, h, (z + k) % N_Z], rz.at[i, h, k - 1], z_peer(k)) for k in range(1, N_Z)]
        cps = send_all(copies, rz.at[i, h], rz_s.at[i, h], rz_r.at[i, h])
        yield
        wait_all(cps)
        s3 = sz[i, h, z].astype(f32)
        for k in range(N_Z - 1):
            s3 = s3 + rz[i, h, k].astype(f32)
        tot[i, :, cols] = s3

    def scatters(i, make):
        return par(*[scatter(i, h, make) for h in range(CHUNKS)])

    def gathers(own, i):
        return par(*[gather(own, i, h) for h in range(CHUNKS)])

    def all_sum(i, n):
        for s, peer in enumerate((xy_peer, zc_peer)):
            copies = [
                (arv.at[i, s, pl.ds(0, n)], arr.at[i, s, k - 1, pl.ds(0, n)], peer(k)) for k in range(1, 16)
            ]
            cps = send_all(copies, arr.at[i, s, :, pl.ds(0, n)], ar_s.at[i, s], ar_r.at[i, s])
            yield
            wait_all(cps)
            acc = arv[i, s, 0:n]
            for k in range(1, 16):
                acc = acc + arr[i, s, k - 1, 0:n]
            arv[i, s + 1, 0:n] = acc

    group = rows(x * GRP, GRP)

    def group_tokens(h):
        c0 = h * W
        cols = pl.ds(c0, W)
        cps = gather_z(hin[:, c0 : c0 + W], xz.at[h], xz_s.at[h], xz_r.at[h])
        yield
        wait_all(cps)
        X[rows(x * GRP + c * HALF + y * BLK, BLK), cols] = join16(xz.at[h], c0, W)
        passed = []

        def pass_on(k):
            at = (rows(x * GRP + c * HALF + y_at(k) * BLK, BLK), cols)
            passed.append(send(X.at[at], X.at[at], xc_s.at[h, k % 4], xc_r.at[h, k % 4], c_peer))

        yield from ring_gather(
            X,
            [(lambda k: x * GRP + c * HALF + y_at(k) * BLK, BLK)],
            c0,
            W,
            y_peer,
            xy_s.at[h],
            xy_r.at[h],
            pass_on,
        )
        yield
        wait_all(passed)
        pre = dot_t(up[:, cols], X[group, cols])
        if h == 0:
            agrad[0] = pre
        else:
            agrad[0] = agrad[0] + pre

    def local_work():
        for b in range(N_X):
            up[pl.ds(b * PAD + ROWS, PAD - ROWS), :] = jnp.zeros((PAD - ROWS, D), bf16)
            down[pl.ds(b * PAD + ROWS, PAD - ROWS), :] = jnp.zeros((PAD - ROWS, D), bf16)
        sbf[pl.ds(ROWS, PAD - ROWS), :] = jnp.zeros((PAD - ROWS, D), bf16)
        yield
        for cp in loads:
            cp.wait()
        sbf[pl.ds(0, ROWS), :] = start[...].astype(bf16)
        yield
        arv[0, 0, 1] = tile_sum(start[...] * start[...])

    own_xb = ring_gather(
        X, [(lambda k: x_at(k) * GRP + c * HALF + y * BLK, BLK)], XA, D - XA, x_peer, xb_s, xb_r
    )
    tok_gens = [group_tokens(h) for h in range(CHUNKS)]

    def later_xb():
        for _ in range(2):
            next(own_xb)
            yield

    both = list(range(CHUNKS))
    n = CHUNKS
    play(tok_gens + [local_work(), later_xb()], both + [n] + both + [n + 1, n] + both + [n + 1, n] + both)

    def tokens_yx():
        passed = []

        def pass_on(k):
            if k != 0:
                at = (rows(x_at(k) * GRP + c * HALF, HALF), pl.ds(0, XA))
                passed.append(send(X.at[at], X.at[at], xac_s.at[k % 4], xac_r.at[k % 4], c_peer))

        yield from ring_gather(
            X, [(lambda k: x_at(k) * GRP + c * HALF, HALF)], 0, XA, x_peer, xa_s, xa_r, pass_on
        )
        yield
        wait_all(passed)

    def tokens_xy():
        next(own_xb, None)
        blocks = [
            (lambda k, b=b: x_at(b) * GRP + c * HALF + y_at(k) * BLK, BLK) for b in range(1, N_X)
        ]
        yield from ring_gather(X, blocks, XA, D - XA, y_peer, xby_s, xby_r)
        passed = []
        for b in range(1, N_X):
            at = (rows(x_at(b) * GRP + c * HALF, HALF), pl.ds(XA, D - XA))
            passed.append(send(X.at[at], X.at[at], xbc_s.at[b], xbc_r.at[b], c_peer))
        yield
        wait_all(passed)

    def to_branch(h):
        for k in range(h * W, (h + 1) * W, W // 3):
            part[:, k : k + W // 3] = dot(hact[...], down[:, k : k + W // 3])

    def to_act(b, tangent):
        hid = pl.ds(b * PAD, PAD)
        hact[:, hid] = (slope[hid, :] * tangent[hid, :]).T.astype(bf16)

    def weights():
        return tgt[...].astype(f32), gain[...]

    def forward():
        for b in range(N_X):
            hid = pl.ds(b * PAD, PAD)
            value, first, second = gelu_parts(agrad[0, hid, :])
            hact[:, hid] = value.T.astype(bf16)
            slope[hid, :] = first
            bendag[hid, :] = second
        yield from scatters(0, to_branch)
        bsum[...] = hin[...].astype(f32) + tot[0]
        yield from gathers(loss_grad(bsum[...], *weights()).astype(bf16), 0)
        bendag[...] = bendag[...] * agrad[0]

    def first_tangent():
        prod = dot_t(X[...], sbf[...])
        for b in range(N_X):
            pts[pl.ds(b * PAD, PAD), :] = prod[b * GRP : (b + 1) * GRP, :].T
        own = rows(x * PAD, PAD)
        pt1[own, :] = pts[own, :]
        cps = [
            send(
                pts.at[rows(x_at(k) * PAD, PAD)], pt1.at[own], pt_s.at[k - 1], pt_r.at[k - 1], x_peer(k)
            )
            for k in range(1, N_X)
        ]
        yield
        wait_all(cps)
        for b in range(N_X):
            to_act(b, pt1)
        yield from scatters(1, to_branch)

    fwd = forward()
    yx, xy = tokens_yx(), tokens_xy()
    for g in (yx, xy, fwd, xy, fwd, xy, fwd, yx, fwd, yx, fwd, xy, yx):
        next(g, None)
    run(xy, yx)
    play((first_tangent(), fwd), (0, 1, 0, 1))
    curv = loss_curv(bsum[...], tot[1], *weights())

    def token_gram():
        half = TOK // 2
        for b in range(0, TOK, half):
            g = dot_t(X[pl.ds(b, half), :], X[group, :])
            hi = g.astype(bf16)
            gram[pl.ds(b, half), pl.ds(0, GRP)] = hi
            gram[pl.ds(b, half), pl.ds(GRP, GRP)] = (g - hi.astype(f32)).astype(bf16)
            yield

    run(gathers(curv.astype(bf16), 1), token_gram())
    p1 = agrad[1] * slope[...] + bendag[...] * pt1[...]
    pfull[rows(x * HID, HID), :] = p1.astype(bf16)

    def share_p1():
        def use(k):
            both_parts = dot(pfull[rows(x_at(k) * HID, HID), :], gram[rows(x_at(k) * GRP, GRP), :])
            term = both_parts[:, 0:GRP] + both_parts[:, GRP : 2 * GRP]
            if k == 0:
                ptx[...] = term
            else:
                ptx[...] = ptx[...] + term

        yield from ring_gather(
            pfull, [(lambda k: x_at(k) * HID, HID)], 0, GRP, x_peer, pf_s, pf_r, use, by_rows=True
        )

    def own_sums():
        arv[0, 0, 0] = tile_sum(p1 * pt1[...])
        yield

    run(share_p1(), own_sums())

    for b in range(N_X):
        to_act(b, ptx)

    def image_one():
        own = jnp.concatenate([pfull[rows(b * HID + x * PAD, PAD), :] for b in range(N_X)], axis=1)
        for k in range(0, D, 512):
            kw[:, k : k + 512] = dot(own, X[:, k : k + 512])[0:ROWS, :]
            if k % 1536 == 1024:
                yield

    run(scatters(2, to_branch), all_sum(0, 2), image_one())
    count = float(ROWS * 256 * D)
    q = jnp.sum(arv[0, 2, 0], keepdims=True) / count
    ss = jnp.sum(arv[0, 2, 1], keepdims=True) / count
    s1 = lax.rsqrt(ss + norm_eps)
    h11 = s1 * s1 * q
    curv = loss_curv(bsum[...], tot[2] - h11 * tot[1], *weights())

    def remainder():
        ptx[...] = ptx[...] - h11 * pt1[...]
        acc = None
        for k in range(0, D, 1536):
            w = kw[:, k : k + 1536] - h11 * start[:, k : k + 1536]
            kw[:, k : k + 1536] = w
            s = tile_sum(w * w)
            acc = s if acc is None else acc + s
            yield
        arv[1, 0, 0] = acc

    run(gathers(curv.astype(bf16), 2), remainder())
    out_w = pltpu.make_async_copy(kw, kw_hbm, out_sem.at[0])
    out_w.start()
    for b in range(N_X):
        hid = pl.ds(b * PAD, PAD)
        pr2[1, b] = (agrad[0, hid, :] * slope[hid, :] + bendag[hid, :] * ptx[hid, :]).astype(bf16)
    pr2[0, x] = pr2[1, x]
    cps = [
        send(pr2.at[1, x_at(k)], pr2.at[0, x], p2_s.at[k - 1], p2_r.at[k - 1], x_peer(k))
        for k in range(1, N_X)
    ]
    wait_all(cps)
    own = jnp.concatenate([pr2[0, b] for b in range(N_X)], axis=1)
    sums = [None, None, None]
    for k in range(0, D, 512):
        cols = slice(k, k + 512)
        acc = dot(own, X[:, cols])[0:ROWS, :]
        k2[:, cols] = acc
        for j, other in enumerate((start[:, cols], kw[:, cols], acc)):
            s = tile_sum(other * acc)
            sums[j] = s if sums[j] is None else sums[j] + s
    for j in range(3):
        arv[1, 0, 1 + j] = sums[j]
    out_2 = pltpu.make_async_copy(k2, k2_hbm, out_sem.at[1])
    out_2.start()
    run(all_sum(1, 4))
    ww, sk, wk, kk = [jnp.sum(arv[1, 2, j], keepdims=True) / count for j in range(4)]
    sq1 = s1 * s1 * ww
    scale2 = lax.rsqrt(sq1 + norm_eps)
    s2 = scale2 * s1
    h12 = s1 * s2 * sk
    h22 = s2 * s2 * wk
    cross = s1 * s2 * (q - h11 * ss)
    sq2 = (
        s2 * s2 * kk
        - 2.0 * (h12 * h12 + h22 * h22)
        + h12 * h12 * (s1 * s1 * ss)
        + h22 * h22 * (s2 * s2 * ww)
        + 2.0 * h12 * h22 * cross
    )
    sq2 = jnp.maximum(sq2, 0.0)
    s3 = lax.rsqrt(sq2 + norm_eps)
    results = (h11, h12, h22, jnp.sqrt(sq1), jnp.sqrt(sq2), s2, s3 * s2, -s3 * h12 * s1, -s3 * h22 * s2)
    for j, value in enumerate(results):
        mix[j] = value[0, 0]
    out_w.wait()
    out_2.wait()
    settle(0)


def combine(mix, kw_hbm, k2_hbm, start_hbm, basis_hbm, quot, coef, kw, k2, start, out, in_sem, out_sem):
    parts = [pl.ds(r, PIECE) for r in range(0, ROWS, PIECE)]
    ins = [
        [
            pltpu.make_async_copy(src.at[at], dst.at[at], in_sem.at[j, p])
            for j, (src, dst) in enumerate(((kw_hbm, kw), (k2_hbm, k2), (start_hbm, start)))
        ]
        for p, at in enumerate(parts)
    ]
    for cps in ins:
        for cp in cps:
            cp.start()
    quot[0] = mix[0]
    coef[0, 0] = mix[1]
    coef[0, 1] = mix[2]
    coef[1, 0] = mix[3]
    coef[1, 1] = mix[4]
    outs = []
    for p, at in enumerate(parts):
        for cp in ins[p]:
            cp.wait()
        w = kw[at, :]
        out[0, at, :] = mix[5] * w
        out[1, at, :] = mix[6] * k2[at, :] + mix[7] * start[at, :] + mix[8] * w
        for j in range(2):
            cp = pltpu.make_async_copy(out.at[j, at], basis_hbm.at[j, at], out_sem.at[j, p])
            cp.start()
            outs.append(cp)
    for cp in outs:
        cp.wait()


def per_device(hidden_in, targets, norm_gain, up_weight, down_weight, start):
    vm, dma = pltpu.VMEM, pltpu.SemaphoreType.DMA
    any_spec = pl.BlockSpec(memory_space=pl.ANY)
    vmem_spec = pl.BlockSpec(memory_space=pltpu.VMEM)
    smem_spec = pl.BlockSpec(memory_space=pltpu.SMEM)
    scratch = [
        vm((HID, D), bf16),
        vm((HID, D), bf16),
        vm((ROWS, D), f32),
        vm((PAD, D), bf16),
        vm((TOK, D), bf16),
        vm((CHUNKS, N_Z, OWN, W), bf16),
        vm((BLK, D), f32),
        vm((GRP, D), f32),
        vm((3, CHUNKS, HALF, W), bf16),
        vm((3, CHUNKS, HALF, W), bf16),
        vm((2, HALF, D), f32),
        vm((3, CHUNKS, BLK, W), bf16),
        vm((3, CHUNKS, BLK, W), bf16),
        vm((3, CHUNKS, 2, BLK, W), bf16),
        vm((3, CHUNKS, 2, BLK, W), bf16),
        vm((3, CHUNKS, N_Z, OWN, W), bf16),
        vm((3, CHUNKS, N_Z - 1, OWN, W), bf16),
        vm((3, CHUNKS, N_Z, OWN, W), bf16),
        vm((3, GRP, D), bf16),
        vm((HID, GRP), f32),
        vm((HID, GRP), f32),
        vm((GRP, HID), bf16),
        vm((2, HID, GRP), f32),
        vm((HID, GRP), f32),
        vm((HID, GRP), f32),
        vm((HID, GRP), f32),
        vm((N_X * HID, GRP), bf16),
        vm((2, N_X, PAD, GRP), bf16),
        vm((TOK, 2 * GRP), bf16),
        vm((ROWS, D), f32),
        vm((ROWS, D), f32),
        vm((2, 3, 4, 8, 128), f32),
        vm((2, 2, 15, 4, 8, 128), f32),
        vm((3, OWN, D), f32),
        vm((OWN, D), f32),
        dma((2 * N_X + 1,)),
    ]
    pairs = [
        (CHUNKS,), (CHUNKS, 4), (CHUNKS, 4),
        (4,), (4,), (4,), (12,), (4,),
        (3, CHUNKS), (3, CHUNKS, 2), (3, CHUNKS, 2), (3, CHUNKS),
        (3, CHUNKS), (3, CHUNKS, 4), (3, CHUNKS, 4),
        (N_X - 1,), (4,), (N_X - 1,), (2, 2),
    ]
    for shape in pairs:
        scratch += [dma(shape), dma(shape)]
    scratch.append(dma((2,)))
    kw, k2, mix = pl.pallas_call(
        kernel,
        out_shape=(
            jax.ShapeDtypeStruct((ROWS, D), f32),
            jax.ShapeDtypeStruct((ROWS, D), f32),
            jax.ShapeDtypeStruct((9,), f32),
        ),
        in_specs=[vmem_spec, vmem_spec, vmem_spec, any_spec, any_spec, any_spec],
        out_specs=(any_spec, any_spec, smem_spec),
        scratch_shapes=scratch,
        compiler_params=pltpu.CompilerParams(
            collective_id=0, has_side_effects=True, vmem_limit_bytes=60 * 1024 * 1024
        ),
        cost_estimate=pl.CostEstimate(flops=5 * 10**9, bytes_accessed=14 * 10**6, transcendentals=10**5),
    )(hidden_in, targets, norm_gain, up_weight, down_weight, start)
    pieces = ROWS // PIECE
    return pl.pallas_call(
        combine,
        out_shape=(
            jax.ShapeDtypeStruct((2, ROWS, D), f32),
            jax.ShapeDtypeStruct((1,), f32),
            jax.ShapeDtypeStruct((2, 2), f32),
        ),
        in_specs=[smem_spec, any_spec, any_spec, any_spec],
        out_specs=(any_spec, smem_spec, smem_spec),
        scratch_shapes=[
            vm((ROWS, D), f32),
            vm((ROWS, D), f32),
            vm((ROWS, D), f32),
            vm((2, ROWS, D), f32),
            dma((3, pieces)),
            dma((2, pieces)),
        ],
        compiler_params=pltpu.CompilerParams(vmem_limit_bytes=60 * 1024 * 1024),
        cost_estimate=pl.CostEstimate(flops=10**7, bytes_accessed=9 * 10**6, transcendentals=0),
    )(mix, kw, k2, start)


def solution(mesh):
    placed = (
        P(("dp", "zero"), None),
        P(("dp", "zero"), None),
        P(),
        P("zero", None),
        P("zero", None),
        P(("zero", "dp"), None),
    )
    return jax.shard_map(
        per_device,
        mesh=mesh,
        in_specs=placed,
        out_specs=(P(None, ("zero", "dp"), None), P(), P()),
        check_vma=False,
    )
```

```python
import jax
import jax.numpy as jnp
from jax import lax
from jax.experimental import pallas as pl
from jax.experimental.pallas import tpu as pltpu
from jax.sharding import PartitionSpec as P

MESH = pl.DeviceIdType.MESH
f32, bf16 = jnp.float32, jnp.bfloat16
norm_eps = 1e-06
gelu_coef = 0.7978845608028654

N_X, N_Y, N_Z, N_C = 4, 4, 8, 2
D = 4608
ROWS = 96
PAD = 128
HID = N_X * PAD
GRP = 128
TOK = N_X * GRP
HALF = GRP // N_C
BLK = HALF // N_Y
OWN = BLK // N_Z
CHUNKS = 2
W = D // CHUNKS
KEEP = 40
PIECE = 32


def gelu_value(inputs):
    return (
        0.5 * inputs * (1.0 + jnp.tanh(gelu_coef * (inputs + 0.044715 * inputs * inputs * inputs)))
    )


def gelu_parts(inputs):
    unit_dir = jnp.ones_like(inputs)

    def first_slope(points):
        return jax.jvp(gelu_value, (points,), (unit_dir,))[1]

    return (
        gelu_value(inputs),
        first_slope(inputs),
        jax.jvp(first_slope, (inputs,), (unit_dir,))[1],
    )


def loss_parts(summed, target, gain):
    r = lax.rsqrt(jnp.sum(summed * summed, axis=-1, keepdims=True) / D + norm_eps)
    normed = summed * r
    pull = (normed * gain - target) * gain
    mean = jnp.sum(pull * normed, axis=-1, keepdims=True) / D
    return r, normed, pull, mean


def loss_grad(summed, target, gain):
    r, normed, pull, mean = loss_parts(summed, target, gain)
    return r * (pull - normed * mean) / float(TOK)


def loss_curv(summed, tangent, target, gain):
    r, normed, pull, mean = loss_parts(summed, target, gain)
    along = jnp.sum(normed * tangent, axis=-1, keepdims=True) / D
    d_normed = r * (tangent - normed * along)
    d_pull = d_normed * gain * gain
    d_mean = jnp.sum(d_pull * normed + pull * d_normed, axis=-1, keepdims=True) / D
    grad = r * (pull - normed * mean)
    d_grad = r * (d_pull - d_normed * mean - normed * d_mean) - (r * along) * grad
    return d_grad / float(TOK)


def dot_t(a, b):
    return lax.dot_general(a, b, (((1,), (1,)), ((), ())), preferred_element_type=f32)


def dot(a, b):
    return jnp.dot(a, b, preferred_element_type=f32)


def tile_sum(v):
    rows, cols = v.shape
    acc = v[0:8, :]
    for i in range(8, rows, 8):
        acc = acc + v[i : i + 8, :]
    out = acc[:, 0:128]
    for k in range(128, cols, 128):
        out = out + acc[:, k : k + 128]
    return out


def par(*gens):
    gens = list(gens)
    while gens:
        for g in list(gens):
            try:
                next(g)
            except StopIteration:
                gens.remove(g)
        if gens:
            yield


def run(*gens):
    for _ in par(*gens):
        pass


def play(gens, order):
    for j in order:
        next(gens[j], None)
    run(*gens)


def kernel(
    hin, tgt, gain, up_hbm, down_hbm, start_hbm,
    kw_hbm, k2_hbm, mix,
    up, down, start, dirs, X, xz, tmp16, part,
    sb, rc, s1f, y1b, y1r, y2b, y2r, sz, rz, az, A,
    slope, bendag, hact, agrad, pt1, ptx,
    pfull, pr2, g_hi, g_lo, kw, k2, arv, arr, tot, bsum,
    ld_sem, xz_s, xz_r, xy_s, xy_r, xc_s, xc_r,
    xa_s, xa_r, xac_s, xac_r, sx_s, sx_r,
    rc_s, rc_r, y1_s, y1_r, y2_s, y2_r, rz_s, rz_r,
    az_s, az_r, ay_s, ay_r, ac_s, ac_r,
    pf_s, pf_r, p2_s, p2_r, ar_s, ar_r, out_sem,
):
    x = lax.axis_index("dp")
    shard = lax.axis_index("zero")
    y, z, c = shard // 16, (shard // 2) % 8, shard % 2

    def dev(nx, ny, nz, nc):
        return (nx, ny * 16 + nz * 2 + nc)

    pending = []

    def x_at(k):
        return (x + (k % N_X)) % N_X

    def y_at(k):
        return (y + (k % N_Y)) % N_Y

    def x_peer(k):
        return dev(x_at(k), y, z, c)

    def y_peer(k):
        return dev(x, y_at(k), z, c)

    def z_peer(k):
        return dev(x, y, (z + k) % N_Z, c)

    c_peer = dev(x, y, z, 1 - c)

    def xy_peer(k):
        return dev(x_at(k // N_Y), y_at(k % N_Y), z, c)

    def zc_peer(k):
        return dev(x, y, (z + k // N_C) % N_Z, (c + k % N_C) % N_C)

    def send(src, dst, ssem, rsem, to):
        cp = pltpu.make_async_remote_copy(
            src_ref=src, dst_ref=dst, send_sem=ssem, recv_sem=rsem, device_id=to, device_id_type=MESH
        )
        cp.start()
        pending.append(cp)
        return cp

    def send_all(copies, bytes_of, ssem, rsem):
        for src, dst, to in copies:
            pltpu.make_async_remote_copy(
                src_ref=src, dst_ref=dst, send_sem=ssem, recv_sem=rsem, device_id=to, device_id_type=MESH
            ).start()
        cp = pltpu.make_async_remote_copy(
            src_ref=bytes_of,
            dst_ref=bytes_of,
            send_sem=ssem,
            recv_sem=rsem,
            device_id=c_peer,
            device_id_type=MESH,
        )
        pending.append(cp)
        return [cp]

    def settle(keep=KEEP):
        while len(pending) > keep:
            pending.pop(0).wait_send()

    def rows(start_row, count):
        return pl.ds(pl.multiple_of(start_row, 16), count)

    def wait_all(cps):
        settle()
        for cp in cps:
            cp.wait_recv()

    loads = []
    for b in range(N_X):
        for j, (src, dst) in enumerate(((up_hbm, up), (down_hbm, down))):
            loads.append(
                pltpu.make_async_copy(
                    src.at[pl.ds(b * ROWS, ROWS)], dst.at[pl.ds(b * PAD, ROWS)], ld_sem.at[2 * b + j]
                )
            )
    loads.append(pltpu.make_async_copy(start_hbm, start, ld_sem.at[2 * N_X]))
    for cp in loads:
        cp.start()

    barrier = pltpu.get_barrier_semaphore()
    peers = [xy_peer(k) for k in range(1, N_X * N_Y)] + [zc_peer(k) for k in range(1, N_Z * N_C)]
    for p in peers:
        pl.semaphore_signal(barrier, inc=1, device_id=p, device_id_type=MESH)
    pl.semaphore_wait(barrier, len(peers))

    def ring_gather(ref, blocks, c0, w, peer, ssem, rsem, then=None):
        half = w // 2
        nb = len(blocks)
        first = []
        for b, (row_of, count) in enumerate(blocks):
            at = (rows(row_of(0), count), pl.ds(c0, w))
            first.append(
                [
                    send(ref.at[at], ref.at[at], ssem.at[2 * b + j], rsem.at[2 * b + j], peer(to))
                    for j, to in enumerate((1, -1))
                ]
            )
        if then:
            then(0)
        yield
        second = []
        for b, (row_of, count) in enumerate(blocks):
            for j, to in enumerate((1, -1)):
                wait_all([first[b][j]])
                at = (rows(row_of(-to), count), pl.ds(c0 + j * half, half))
                i = 2 * (nb + b) + j
                second.append(send(ref.at[at], ref.at[at], ssem.at[i], rsem.at[i], peer(to)))
        if then:
            then(-1)
            then(1)
        yield
        wait_all(second)
        if then:
            then(2)

    def gather_z(own, buf, ssem, rsem):
        buf[z] = own
        copies = [(buf.at[z], buf.at[z], z_peer(k)) for k in range(1, N_Z)]
        return send_all(copies, buf.at[pl.ds(0, N_Z - 1)], ssem, rsem)

    def join16(buf, c0, w):
        for j in range(N_Z):
            tmp16[pl.ds(OWN * j, OWN), c0 : c0 + w] = buf[j].astype(f32)
        return tmp16[:, c0 : c0 + w].astype(bf16)

    def gather(own, i, h):
        c0, out = h * W, A.at[i]
        cols = pl.ds(c0, W)
        cps = gather_z(own[:, c0 : c0 + W], az.at[i, h], az_s.at[i, h], az_r.at[i, h])
        yield
        wait_all(cps)
        out[rows(c * HALF + y * BLK, BLK), cols] = join16(az.at[i, h], c0, W)
        passed = []

        def pass_on(k):
            at = (rows(c * HALF + y_at(k) * BLK, BLK), cols)
            passed.append(send(out.at[at], out.at[at], ac_s.at[i, h, k % 4], ac_r.at[i, h, k % 4], c_peer))

        yield from ring_gather(
            out,
            [(lambda k: c * HALF + y_at(k) * BLK, BLK)],
            c0,
            W,
            y_peer,
            ay_s.at[i, h],
            ay_r.at[i, h],
            pass_on,
        )
        yield
        wait_all(passed)
        part_grad = dot_t(out[:, cols], down[:, cols])
        if h == 0:
            agrad[i % 2] = part_grad
        else:
            agrad[i % 2] = agrad[i % 2] + part_grad

    def scatter(i, h, make=None):
        c0 = h * W
        cols = slice(c0, c0 + W)
        if make is not None:
            make(h)
        sb[i, h] = part[rows((1 - c) * HALF, HALF), cols].astype(bf16)
        cps = [send(sb.at[i, h], rc.at[i, h], rc_s.at[i, h], rc_r.at[i, h], c_peer)]
        yield
        wait_all(cps)
        s1f[i % 2, :, cols] = part[rows(c * HALF, HALF), cols] + rc[i, h].astype(f32)

        def block(k):
            return s1f[i % 2, rows(y_at(k) * BLK, BLK), cols]

        half = W // 2
        y1b[i, h] = block(2).astype(bf16)
        cps = [
            send(
                y1b.at[i, h, :, pl.ds(j * half, half)],
                y1r.at[i, h, :, pl.ds(j * half, half)],
                y1_s.at[i, h, j],
                y1_r.at[i, h, j],
                y_peer(to),
            )
            for j, to in enumerate((1, -1))
        ]
        yield
        wait_all(cps)
        got = y1r[i, h].astype(f32)
        for j, to in enumerate((1, -1)):
            mine = block(to)
            if j == 0:
                pieces = [mine[:, :half] + got[:, :half], mine[:, half:]]
            else:
                pieces = [mine[:, :half], mine[:, half:] + got[:, half:]]
            y2b[i, h, j, :, pl.ds(0, half)] = pieces[0].astype(bf16)
            y2b[i, h, j, :, pl.ds(half, half)] = pieces[1].astype(bf16)
        cps = [
            send(y2b.at[i, h, j], y2r.at[i, h, j], y2_s.at[i, h, j], y2_r.at[i, h, j], y_peer(to))
            for j, to in enumerate((1, -1))
        ]
        yield
        wait_all(cps)
        tmp16[:, cols] = block(0) + y2r[i, h, 0].astype(f32) + y2r[i, h, 1].astype(f32)
        for j in range(N_Z):
            sz[i, h, j] = tmp16[pl.ds(OWN * j, OWN), cols].astype(bf16)
        copies = [(sz.at[i, h, (z + k) % N_Z], rz.at[i, h, k - 1], z_peer(k)) for k in range(1, N_Z)]
        cps = send_all(copies, rz.at[i, h], rz_s.at[i, h], rz_r.at[i, h])
        yield
        wait_all(cps)
        s3 = sz[i, h, z].astype(f32)
        for k in range(N_Z - 1):
            s3 = s3 + rz[i, h, k].astype(f32)
        tot[i, :, cols] = s3

    def scatters(i, make):
        return par(*[scatter(i, h, make) for h in range(CHUNKS)])

    def gathers(own, i):
        return par(*[gather(own, i, h) for h in range(CHUNKS)])

    def all_sum(i, n):
        for s, peer in enumerate((xy_peer, zc_peer)):
            copies = [
                (arv.at[i, s, pl.ds(0, n)], arr.at[i, s, k - 1, pl.ds(0, n)], peer(k)) for k in range(1, 16)
            ]
            cps = send_all(copies, arr.at[i, s, :, pl.ds(0, n)], ar_s.at[i, s], ar_r.at[i, s])
            yield
            wait_all(cps)
            acc = arv[i, s, 0:n]
            for k in range(1, 16):
                acc = acc + arr[i, s, k - 1, 0:n]
            arv[i, s + 1, 0:n] = acc

    group = rows(x * GRP, GRP)

    def group_tokens(h):
        c0 = h * W
        cols = pl.ds(c0, W)
        cps = gather_z(hin[:, c0 : c0 + W], xz.at[h], xz_s.at[h], xz_r.at[h])
        yield
        wait_all(cps)
        X[rows(x * GRP + c * HALF + y * BLK, BLK), cols] = join16(xz.at[h], c0, W)
        passed = []

        def pass_on(k):
            at = (rows(x * GRP + c * HALF + y_at(k) * BLK, BLK), cols)
            passed.append(send(X.at[at], X.at[at], xc_s.at[h, k % 4], xc_r.at[h, k % 4], c_peer))

        yield from ring_gather(
            X,
            [(lambda k: x * GRP + c * HALF + y_at(k) * BLK, BLK)],
            c0,
            W,
            y_peer,
            xy_s.at[h],
            xy_r.at[h],
            pass_on,
        )
        yield
        wait_all(passed)
        pre = dot_t(X[group, cols], up[:, cols])
        if h == 0:
            agrad[0] = pre
        else:
            agrad[0] = agrad[0] + pre

    def accumulate_pt1(h, k):
        cols = pl.ds(h * W, W)
        block = rows(x_at(k) * PAD, PAD)
        lanes = pl.ds(pl.multiple_of(x_at(k) * PAD, PAD), PAD)
        term = dot_t(X[group, cols], dirs[block, cols])
        if h == 0:
            pt1[:, lanes] = term
        else:
            pt1[:, lanes] = pt1[:, lanes] + term

    def start_rows(h):
        ring = ring_gather(
            dirs, [(lambda k: x_at(k) * PAD, ROWS)], h * W, W, x_peer, sx_s.at[h], sx_r.at[h]
        )
        next(ring)
        yield
        next(ring)
        yield
        for k in (0, -1, 1):
            accumulate_pt1(h, k)
        yield
        run(ring)
        accumulate_pt1(h, 2)

    def other_tokens(h):
        cols = pl.ds(h * W, W)
        passed = []

        def pass_on(k):
            if k != 0:
                at = (rows(x_at(k) * GRP + c * HALF, HALF), cols)
                passed.append(send(X.at[at], X.at[at], xac_s.at[h, k % 4], xac_r.at[h, k % 4], c_peer))

        yield from ring_gather(
            X, [(lambda k: x_at(k) * GRP + c * HALF, HALF)], h * W, W, x_peer, xa_s.at[h], xa_r.at[h], pass_on
        )
        yield
        wait_all(passed)

    def local_work():
        loads[-1].wait()
        dirs[rows(x * PAD, ROWS), :] = start[...].astype(bf16)
        for g in s_gens:
            next(g)
        for b in range(N_X):
            pad = pl.ds(b * PAD + ROWS, PAD - ROWS)
            up[pad, :] = jnp.zeros((PAD - ROWS, D), bf16)
            down[pad, :] = jnp.zeros((PAD - ROWS, D), bf16)
            dirs[pad, :] = jnp.zeros((PAD - ROWS, D), bf16)
        yield
        for cp in loads[:-1]:
            cp.wait()
        arv[0, 0, 1] = tile_sum(start[...] * start[...])

    s_gens = [start_rows(h) for h in range(CHUNKS)]
    both = list(range(CHUNKS))
    n = CHUNKS
    play([group_tokens(h) for h in range(CHUNKS)] + [local_work()], both + [n] + both + [n] + both + both)

    def to_branch(h):
        for k in range(h * W, (h + 1) * W, W // 3):
            part[:, k : k + W // 3] = dot(hact[...], down[:, k : k + W // 3])

    def weights():
        return tgt[...].astype(f32), gain[...]

    def forward():
        for b in range(N_X):
            cols = pl.ds(b * PAD, PAD)
            value, first, second = gelu_parts(agrad[0, :, cols])
            hact[:, cols] = value.astype(bf16)
            slope[:, cols] = first
            bendag[:, cols] = second
        yield from scatters(0, to_branch)
        bsum[...] = hin[...].astype(f32) + tot[0]
        yield from gathers(loss_grad(bsum[...], *weights()).astype(bf16), 0)
        bendag[...] = bendag[...] * agrad[0]

    def first_tangent():
        hact[...] = (slope[...] * pt1[...]).astype(bf16)
        yield from scatters(1, to_branch)

    fwd = forward()
    others = [other_tokens(h) for h in range(CHUNKS)]
    for g in s_gens + [fwd] + s_gens + [fwd, fwd] + s_gens:
        next(g, None)
    tangent = first_tangent()
    for g in [tangent, fwd] + others:
        next(g, None)
    run(tangent, fwd)
    curv = loss_curv(bsum[...], tot[1], *weights())

    def token_gram():
        half = TOK // 2
        for b in range(2):
            g = dot_t(X[group, :], X[pl.ds(b * half, half), :])
            hi = g.astype(bf16)
            g_hi[:, pl.ds(b * half, half)] = hi
            g_lo[:, pl.ds(b * half, half)] = (g - hi.astype(f32)).astype(bf16)
            yield

    grads = gathers(curv.astype(bf16), 1)
    for g in [grads] + others + [grads] + others + [grads] + others + [grads]:
        next(g, None)
    run(token_gram())
    run(grads)
    p1 = agrad[1] * slope[...] + bendag[...] * pt1[...]
    pfull[group, :] = p1.astype(bf16)

    def share_p1():
        def use(k):
            block = rows(x_at(k) * GRP, GRP)
            term = dot(g_hi[:, block], pfull[block, :]) + dot(g_lo[:, block], pfull[block, :])
            if k == 0:
                ptx[...] = term
            else:
                ptx[...] = ptx[...] + term

        cps = [
            send(pfull.at[group], pfull.at[group], pf_s.at[k - 1], pf_r.at[k - 1], x_peer(k))
            for k in range(1, N_X)
        ]
        use(0)
        yield
        for k in (1, 3, 2):
            wait_all([cps[k - 1]])
            use(N_X - k)

    def own_sums():
        arv[0, 0, 0] = tile_sum(p1 * pt1[...])
        yield

    run(share_p1(), own_sums())

    hact[...] = (slope[...] * ptx[...]).astype(bf16)

    def image_one():
        own = pfull[:, pl.ds(pl.multiple_of(x * PAD, PAD), PAD)].T
        for k in range(0, D, 512):
            kw[:, k : k + 512] = dot(own, X[:, k : k + 512])[0:ROWS, :]
            if k % 1536 == 1024:
                yield

    run(scatters(2, to_branch), all_sum(0, 2), image_one())
    count = float(ROWS * 256 * D)
    q = jnp.sum(arv[0, 2, 0], keepdims=True) / count
    ss = jnp.sum(arv[0, 2, 1], keepdims=True) / count
    s1 = lax.rsqrt(ss + norm_eps)
    h11 = s1 * s1 * q
    curv = loss_curv(bsum[...], tot[2] - h11 * tot[1], *weights())

    def remainder():
        ptx[...] = ptx[...] - h11 * pt1[...]
        acc = None
        for k in range(0, D, 1536):
            w = kw[:, k : k + 1536] - h11 * start[:, k : k + 1536]
            kw[:, k : k + 1536] = w
            s = tile_sum(w * w)
            acc = s if acc is None else acc + s
            yield
        arv[1, 0, 0] = acc

    run(gathers(curv.astype(bf16), 2), remainder())
    out_w = pltpu.make_async_copy(kw, kw_hbm, out_sem.at[0])
    out_w.start()
    for b in range(N_X):
        cols = pl.ds(b * PAD, PAD)
        pr2[1, b] = (agrad[0, :, cols] * slope[:, cols] + bendag[:, cols] * ptx[:, cols]).astype(bf16)
    pr2[0, x] = pr2[1, x]
    cps = [
        send(pr2.at[1, x_at(k)], pr2.at[0, x], p2_s.at[k - 1], p2_r.at[k - 1], x_peer(k))
        for k in range(1, N_X)
    ]
    wait_all(cps)
    own = pr2[0].reshape(TOK, PAD).T
    sums = [None, None, None]
    for k in range(0, D, 512):
        cols = slice(k, k + 512)
        acc = dot(own, X[:, cols])[0:ROWS, :]
        k2[:, cols] = acc
        for j, other in enumerate((start[:, cols], kw[:, cols], acc)):
            s = tile_sum(other * acc)
            sums[j] = s if sums[j] is None else sums[j] + s
    for j in range(3):
        arv[1, 0, 1 + j] = sums[j]
    out_2 = pltpu.make_async_copy(k2, k2_hbm, out_sem.at[1])
    out_2.start()
    run(all_sum(1, 4))
    ww, sk, wk, kk = [jnp.sum(arv[1, 2, j], keepdims=True) / count for j in range(4)]
    sq1 = s1 * s1 * ww
    scale2 = lax.rsqrt(sq1 + norm_eps)
    s2 = scale2 * s1
    h12 = s1 * s2 * sk
    h22 = s2 * s2 * wk
    cross = s1 * s2 * (q - h11 * ss)
    sq2 = (
        s2 * s2 * kk
        - 2.0 * (h12 * h12 + h22 * h22)
        + h12 * h12 * (s1 * s1 * ss)
        + h22 * h22 * (s2 * s2 * ww)
        + 2.0 * h12 * h22 * cross
    )
    sq2 = jnp.maximum(sq2, 0.0)
    s3 = lax.rsqrt(sq2 + norm_eps)
    results = (h11, h12, h22, jnp.sqrt(sq1), jnp.sqrt(sq2), s2, s3 * s2, -s3 * h12 * s1, -s3 * h22 * s2)
    for j, value in enumerate(results):
        mix[j] = value[0, 0]
    out_w.wait()
    out_2.wait()
    settle(0)


def combine(mix, kw_hbm, k2_hbm, start_hbm, basis_hbm, quot, coef, kw, k2, start, out, in_sem, out_sem):
    parts = [pl.ds(r, PIECE) for r in range(0, ROWS, PIECE)]
    ins = [
        [
            pltpu.make_async_copy(src.at[at], dst.at[at], in_sem.at[j, p])
            for j, (src, dst) in enumerate(((kw_hbm, kw), (k2_hbm, k2), (start_hbm, start)))
        ]
        for p, at in enumerate(parts)
    ]
    for cps in ins:
        for cp in cps:
            cp.start()
    quot[0] = mix[0]
    coef[0, 0] = mix[1]
    coef[0, 1] = mix[2]
    coef[1, 0] = mix[3]
    coef[1, 1] = mix[4]
    outs = []
    for p, at in enumerate(parts):
        for cp in ins[p]:
            cp.wait()
        w = kw[at, :]
        out[0, at, :] = mix[5] * w
        out[1, at, :] = mix[6] * k2[at, :] + mix[7] * start[at, :] + mix[8] * w
        for j in range(2):
            cp = pltpu.make_async_copy(out.at[j, at], basis_hbm.at[j, at], out_sem.at[j, p])
            cp.start()
            outs.append(cp)
    for cp in outs:
        cp.wait()


def per_device(hidden_in, targets, norm_gain, up_weight, down_weight, start):
    vm, dma = pltpu.VMEM, pltpu.SemaphoreType.DMA
    any_spec = pl.BlockSpec(memory_space=pl.ANY)
    vmem_spec = pl.BlockSpec(memory_space=pltpu.VMEM)
    smem_spec = pl.BlockSpec(memory_space=pltpu.SMEM)
    scratch = [
        vm((HID, D), bf16),
        vm((HID, D), bf16),
        vm((ROWS, D), f32),
        vm((HID, D), bf16),
        vm((TOK, D), bf16),
        vm((CHUNKS, N_Z, OWN, W), bf16),
        vm((BLK, D), f32),
        vm((GRP, D), f32),
        vm((3, CHUNKS, HALF, W), bf16),
        vm((3, CHUNKS, HALF, W), bf16),
        vm((2, HALF, D), f32),
        vm((3, CHUNKS, BLK, W), bf16),
        vm((3, CHUNKS, BLK, W), bf16),
        vm((3, CHUNKS, 2, BLK, W), bf16),
        vm((3, CHUNKS, 2, BLK, W), bf16),
        vm((3, CHUNKS, N_Z, OWN, W), bf16),
        vm((3, CHUNKS, N_Z - 1, OWN, W), bf16),
        vm((3, CHUNKS, N_Z, OWN, W), bf16),
        vm((3, GRP, D), bf16),
        vm((GRP, HID), f32),
        vm((GRP, HID), f32),
        vm((GRP, HID), bf16),
        vm((2, GRP, HID), f32),
        vm((GRP, HID), f32),
        vm((GRP, HID), f32),
        vm((TOK, HID), bf16),
        vm((2, N_X, GRP, PAD), bf16),
        vm((GRP, TOK), bf16),
        vm((GRP, TOK), bf16),
        vm((ROWS, D), f32),
        vm((ROWS, D), f32),
        vm((2, 3, 4, 8, 128), f32),
        vm((2, 2, 15, 4, 8, 128), f32),
        vm((3, OWN, D), f32),
        vm((OWN, D), f32),
        dma((2 * N_X + 1,)),
    ]
    pairs = [
        (CHUNKS,), (CHUNKS, 4), (CHUNKS, 4),
        (CHUNKS, 4), (CHUNKS, 4), (CHUNKS, 4),
        (3, CHUNKS), (3, CHUNKS, 2), (3, CHUNKS, 2), (3, CHUNKS),
        (3, CHUNKS), (3, CHUNKS, 4), (3, CHUNKS, 4),
        (N_X - 1,), (N_X - 1,), (2, 2),
    ]
    for shape in pairs:
        scratch += [dma(shape), dma(shape)]
    scratch.append(dma((2,)))
    kw, k2, mix = pl.pallas_call(
        kernel,
        out_shape=(
            jax.ShapeDtypeStruct((ROWS, D), f32),
            jax.ShapeDtypeStruct((ROWS, D), f32),
            jax.ShapeDtypeStruct((9,), f32),
        ),
        in_specs=[vmem_spec, vmem_spec, vmem_spec, any_spec, any_spec, any_spec],
        out_specs=(any_spec, any_spec, smem_spec),
        scratch_shapes=scratch,
        compiler_params=pltpu.CompilerParams(
            collective_id=0, has_side_effects=True, vmem_limit_bytes=60 * 1024 * 1024
        ),
        cost_estimate=pl.CostEstimate(flops=5 * 10**9, bytes_accessed=14 * 10**6, transcendentals=10**5),
    )(hidden_in, targets, norm_gain, up_weight, down_weight, start)
    pieces = ROWS // PIECE
    return pl.pallas_call(
        combine,
        out_shape=(
            jax.ShapeDtypeStruct((2, ROWS, D), f32),
            jax.ShapeDtypeStruct((1,), f32),
            jax.ShapeDtypeStruct((2, 2), f32),
        ),
        in_specs=[smem_spec, any_spec, any_spec, any_spec],
        out_specs=(any_spec, smem_spec, smem_spec),
        scratch_shapes=[
            vm((ROWS, D), f32),
            vm((ROWS, D), f32),
            vm((ROWS, D), f32),
            vm((2, ROWS, D), f32),
            dma((3, pieces)),
            dma((2, pieces)),
        ],
        compiler_params=pltpu.CompilerParams(vmem_limit_bytes=60 * 1024 * 1024),
        cost_estimate=pl.CostEstimate(flops=10**7, bytes_accessed=9 * 10**6, transcendentals=0),
    )(mix, kw, k2, start)


def solution(mesh):
    placed = (
        P(("dp", "zero"), None),
        P(("dp", "zero"), None),
        P(),
        P("zero", None),
        P("zero", None),
        P(("zero", "dp"), None),
    )
    return jax.shard_map(
        per_device,
        mesh=mesh,
        in_specs=placed,
        out_specs=(P(None, ("zero", "dp"), None), P(), P()),
        check_vma=False,
    )
```

```python
import jax
import jax.numpy as jnp
from jax import lax
from jax.experimental import pallas as pl
from jax.experimental.pallas import tpu as pltpu
from jax.sharding import PartitionSpec as P

MESH = pl.DeviceIdType.MESH
f32, bf16 = jnp.float32, jnp.bfloat16
norm_eps = 1e-06
gelu_coef = 0.7978845608028654

N_X, N_Y, N_Z, N_C = 4, 4, 8, 2
D = 4608
ROWS = 96
PAD = 128
HID = N_X * PAD
GRP = 128
TOK = N_X * GRP
HALF = GRP // N_C
BLK = HALF // N_Y
OWN = BLK // N_Z
CHUNKS = 2
W = D // CHUNKS
KEEP = 40
PIECE = 32


def gelu_value(inputs):
    return (
        0.5 * inputs * (1.0 + jnp.tanh(gelu_coef * (inputs + 0.044715 * inputs * inputs * inputs)))
    )


def gelu_parts(inputs):
    unit_dir = jnp.ones_like(inputs)

    def first_slope(points):
        return jax.jvp(gelu_value, (points,), (unit_dir,))[1]

    return (
        gelu_value(inputs),
        first_slope(inputs),
        jax.jvp(first_slope, (inputs,), (unit_dir,))[1],
    )


def loss_parts(summed, target, gain):
    r = lax.rsqrt(jnp.sum(summed * summed, axis=-1, keepdims=True) / D + norm_eps)
    normed = summed * r
    pull = (normed * gain - target) * gain
    mean = jnp.sum(pull * normed, axis=-1, keepdims=True) / D
    return r, normed, pull, mean


def loss_grad(summed, target, gain):
    r, normed, pull, mean = loss_parts(summed, target, gain)
    return r * (pull - normed * mean) / float(TOK)


def loss_curv(summed, tangent, target, gain):
    r, normed, pull, mean = loss_parts(summed, target, gain)
    along = jnp.sum(normed * tangent, axis=-1, keepdims=True) / D
    d_normed = r * (tangent - normed * along)
    d_pull = d_normed * gain * gain
    d_mean = jnp.sum(d_pull * normed + pull * d_normed, axis=-1, keepdims=True) / D
    grad = r * (pull - normed * mean)
    d_grad = r * (d_pull - d_normed * mean - normed * d_mean) - (r * along) * grad
    return d_grad / float(TOK)


def dot_t(a, b):
    return lax.dot_general(a, b, (((1,), (1,)), ((), ())), preferred_element_type=f32)


def dot(a, b):
    return jnp.dot(a, b, preferred_element_type=f32)


def tile_sum(v):
    rows, cols = v.shape
    acc = v[0:8, :]
    for i in range(8, rows, 8):
        acc = acc + v[i : i + 8, :]
    out = acc[:, 0:128]
    for k in range(128, cols, 128):
        out = out + acc[:, k : k + 128]
    return out


def par(*gens):
    gens = list(gens)
    while gens:
        for g in list(gens):
            try:
                next(g)
            except StopIteration:
                gens.remove(g)
        if gens:
            yield


def run(*gens):
    for _ in par(*gens):
        pass


def play(gens, order):
    for j in order:
        next(gens[j], None)
    run(*gens)


def kernel(
    hin, tgt, gain, up_hbm, down_hbm, start_hbm,
    kw_hbm, k2_hbm, mix,
    up, down, start, dirs, X, xz, tmp16, part,
    sb, rc, y1b, y1r, y2b, y2r, sz, rz, az, A,
    slope, bendag, hact, agrad, pt1, ptx,
    pfull, pr2, g_hi, g_lo, kw, k2, arv, arr, tot, bsum,
    ld_sem, xz_s, xz_r, xy_s, xy_r, xc_s, xc_r,
    xa_s, xa_r, xac_s, xac_r, sx_s, sx_r,
    rc_s, rc_r, y1_s, y1_r, y2_s, y2_r, rz_s, rz_r,
    az_s, az_r, ay_s, ay_r, ac_s, ac_r,
    pf_s, pf_r, p2_s, p2_r, ar_s, ar_r, out_sem,
):
    x = lax.axis_index("dp")
    shard = lax.axis_index("zero")
    y, z, c = shard // 16, (shard // 2) % 8, shard % 2

    def dev(nx, ny, nz, nc):
        return (nx, ny * 16 + nz * 2 + nc)

    pending = []

    def x_at(k):
        return (x + (k % N_X)) % N_X

    def y_at(k):
        return (y + (k % N_Y)) % N_Y

    def x_peer(k):
        return dev(x_at(k), y, z, c)

    def y_peer(k):
        return dev(x, y_at(k), z, c)

    def z_peer(k):
        return dev(x, y, (z + k) % N_Z, c)

    c_peer = dev(x, y, z, 1 - c)

    def cross_peer(k):
        return dev(x, y_at(k), z, 1 - c)

    def xy_peer(k):
        return dev(x_at(k // N_Y), y_at(k % N_Y), z, c)

    def zc_peer(k):
        return dev(x, y, (z + k // N_C) % N_Z, (c + k % N_C) % N_C)

    def send(src, dst, ssem, rsem, to):
        cp = pltpu.make_async_remote_copy(
            src_ref=src, dst_ref=dst, send_sem=ssem, recv_sem=rsem, device_id=to, device_id_type=MESH
        )
        cp.start()
        pending.append(cp)
        return cp

    def send_all(copies, bytes_of, ssem, rsem):
        for src, dst, to in copies:
            pltpu.make_async_remote_copy(
                src_ref=src, dst_ref=dst, send_sem=ssem, recv_sem=rsem, device_id=to, device_id_type=MESH
            ).start()
        cp = pltpu.make_async_remote_copy(
            src_ref=bytes_of,
            dst_ref=bytes_of,
            send_sem=ssem,
            recv_sem=rsem,
            device_id=c_peer,
            device_id_type=MESH,
        )
        pending.append(cp)
        return [cp]

    def settle(keep=KEEP):
        while len(pending) > keep:
            pending.pop(0).wait_send()

    def rows(start_row, count):
        return pl.ds(pl.multiple_of(start_row, 16), count)

    def wait_all(cps):
        settle()
        for cp in cps:
            cp.wait_recv()

    loads = []
    for b in range(N_X):
        for j, (src, dst) in enumerate(((up_hbm, up), (down_hbm, down))):
            loads.append(
                pltpu.make_async_copy(
                    src.at[pl.ds(b * ROWS, ROWS)], dst.at[pl.ds(b * PAD, ROWS)], ld_sem.at[2 * b + j]
                )
            )
    loads.append(pltpu.make_async_copy(start_hbm, start, ld_sem.at[2 * N_X]))
    for cp in loads:
        cp.start()

    barrier = pltpu.get_barrier_semaphore()
    peers = [xy_peer(k) for k in range(1, N_X * N_Y)] + [zc_peer(k) for k in range(1, N_Z * N_C)]
    peers += [cross_peer(1), cross_peer(-1)]
    for p in peers:
        pl.semaphore_signal(barrier, inc=1, device_id=p, device_id_type=MESH)
    pl.semaphore_wait(barrier, len(peers))

    def ring_gather(ref, blocks, c0, w, peer, ssem, rsem, then=None, cross=None):
        half = w // 2
        nb = len(blocks)
        first = []
        for b, (row_of, count) in enumerate(blocks):
            at = (rows(row_of(0), count), pl.ds(c0, w))
            first.append(
                [
                    send(ref.at[at], ref.at[at], ssem.at[2 * b + j], rsem.at[2 * b + j], peer(to))
                    for j, to in enumerate((1, -1))
                ]
            )
        if then:
            then(0)
        yield
        second = []
        for b, (row_of, count) in enumerate(blocks):
            for j, to in enumerate((1, -1)):
                wait_all([first[b][j]])
                at = (rows(row_of(-to), count), pl.ds(c0 + j * half, half))
                i = 2 * (nb + b) + j
                second.append(send(ref.at[at], ref.at[at], ssem.at[i], rsem.at[i], peer(to)))
                if cross:
                    second.append(send(ref.at[at], ref.at[at], ssem.at[i + 2], rsem.at[i + 2], cross(to)))
        if then:
            then(-1)
            then(1)
        yield
        wait_all(second)
        if then:
            then(2)

    def gather_z(own, buf, ssem, rsem):
        buf[z] = own
        copies = [(buf.at[z], buf.at[z], z_peer(k)) for k in range(1, N_Z)]
        return send_all(copies, buf.at[pl.ds(0, N_Z - 1)], ssem, rsem)

    def join16(buf, c0, w):
        for j in range(N_Z):
            tmp16[pl.ds(OWN * j, OWN), c0 : c0 + w] = buf[j].astype(f32)
        return tmp16[:, c0 : c0 + w].astype(bf16)

    def gather(own, i, h):
        c0, out = h * W, A.at[i]
        cols = pl.ds(c0, W)
        cps = gather_z(own[:, c0 : c0 + W], az.at[i, h], az_s.at[i, h], az_r.at[i, h])
        yield
        wait_all(cps)
        out[rows(c * HALF + y * BLK, BLK), cols] = join16(az.at[i, h], c0, W)
        passed = []

        def pass_on(k):
            if k != 2:
                at = (rows(c * HALF + y_at(k) * BLK, BLK), cols)
                passed.append(send(out.at[at], out.at[at], ac_s.at[i, h, k % 4], ac_r.at[i, h, k % 4], c_peer))

        yield from ring_gather(
            out,
            [(lambda k: c * HALF + y_at(k) * BLK, BLK)],
            c0,
            W,
            y_peer,
            ay_s.at[i, h],
            ay_r.at[i, h],
            pass_on,
            cross_peer,
        )
        wait_all(passed)
        part_grad = dot_t(out[:, cols], down[:, cols])
        if h == 0:
            agrad[i % 2] = part_grad
        else:
            agrad[i % 2] = agrad[i % 2] + part_grad

    def scatter(i, h, make):
        c0 = h * W
        cols = slice(c0, c0 + W)
        make(i, h)
        buf = part.at[i % 2]

        def mine(k):
            return buf[rows(c * HALF + y_at(k) * BLK, BLK), cols]

        def other(k):
            return buf[rows((1 - c) * HALF + y_at(k) * BLK, BLK), cols]

        half = W // 2
        y1b[i, h, 0] = mine(2).astype(bf16)
        y1b[i, h, 1] = other(2).astype(bf16)
        cps = [
            send(
                y1b.at[i, h, p, :, pl.ds(j * half, half)],
                y1r.at[i, h, p, :, pl.ds(j * half, half)],
                y1_s.at[i, h, 2 * p + j],
                y1_r.at[i, h, 2 * p + j],
                peer(to),
            )
            for p, peer in enumerate((y_peer, cross_peer))
            for j, to in enumerate((1, -1))
        ]
        for n, k in enumerate((0, 1, -1)):
            sb[i, h, n] = other(k).astype(bf16)
        cps.append(send(sb.at[i, h], rc.at[i, h], rc_s.at[i, h], rc_r.at[i, h], c_peer))
        yield
        wait_all(cps)
        got = y1r[i, h, 0].astype(f32) + y1r[i, h, 1].astype(f32)
        for j, to in enumerate((1, -1)):
            both_cores = mine(to) + rc[i, h, 1 + j].astype(f32)
            for p in range(2):
                at = slice(p * half, (p + 1) * half)
                piece = both_cores[:, at] + got[:, at] if p == j else both_cores[:, at]
                y2b[i, h, j, :, at] = piece.astype(bf16)
        cps = [
            send(y2b.at[i, h, j], y2r.at[i, h, j], y2_s.at[i, h, j], y2_r.at[i, h, j], y_peer(to))
            for j, to in enumerate((1, -1))
        ]
        yield
        wait_all(cps)
        tmp16[:, cols] = (
            mine(0) + rc[i, h, 0].astype(f32) + y2r[i, h, 0].astype(f32) + y2r[i, h, 1].astype(f32)
        )
        for j in range(N_Z):
            sz[i, h, j] = tmp16[pl.ds(OWN * j, OWN), cols].astype(bf16)
        copies = [(sz.at[i, h, (z + k) % N_Z], rz.at[i, h, k - 1], z_peer(k)) for k in range(1, N_Z)]
        cps = send_all(copies, rz.at[i, h], rz_s.at[i, h], rz_r.at[i, h])
        yield
        wait_all(cps)
        s3 = sz[i, h, z].astype(f32)
        for k in range(N_Z - 1):
            s3 = s3 + rz[i, h, k].astype(f32)
        tot[i, :, cols] = s3

    def scatters(i, make):
        return par(*[scatter(i, h, make) for h in range(CHUNKS)])

    def gathers(own, i):
        return par(*[gather(own, i, h) for h in range(CHUNKS)])

    def all_sum(i, n):
        for s, peer in enumerate((xy_peer, zc_peer)):
            copies = [
                (arv.at[i, s, pl.ds(0, n)], arr.at[i, s, k - 1, pl.ds(0, n)], peer(k)) for k in range(1, 16)
            ]
            cps = send_all(copies, arr.at[i, s, :, pl.ds(0, n)], ar_s.at[i, s], ar_r.at[i, s])
            yield
            wait_all(cps)
            acc = arv[i, s, 0:n]
            for k in range(1, 16):
                acc = acc + arr[i, s, k - 1, 0:n]
            arv[i, s + 1, 0:n] = acc

    group = rows(x * GRP, GRP)

    def group_tokens(h):
        c0 = h * W
        cols = pl.ds(c0, W)
        cps = gather_z(hin[:, c0 : c0 + W], xz.at[h], xz_s.at[h], xz_r.at[h])
        yield
        wait_all(cps)
        X[rows(x * GRP + c * HALF + y * BLK, BLK), cols] = join16(xz.at[h], c0, W)
        passed = []

        def pass_on(k):
            if k != 2:
                at = (rows(x * GRP + c * HALF + y_at(k) * BLK, BLK), cols)
                passed.append(send(X.at[at], X.at[at], xc_s.at[h, k % 4], xc_r.at[h, k % 4], c_peer))

        yield from ring_gather(
            X,
            [(lambda k: x * GRP + c * HALF + y_at(k) * BLK, BLK)],
            c0,
            W,
            y_peer,
            xy_s.at[h],
            xy_r.at[h],
            pass_on,
            cross_peer,
        )
        wait_all(passed)
        pre = dot_t(X[group, cols], up[:, cols])
        if h == 0:
            agrad[0] = pre
        else:
            agrad[0] = agrad[0] + pre

    def accumulate_pt1(h, k):
        cols = pl.ds(h * W, W)
        block = rows(x_at(k) * PAD, PAD)
        lanes = pl.ds(pl.multiple_of(x_at(k) * PAD, PAD), PAD)
        term = dot_t(X[group, cols], dirs[block, cols])
        if h == 0:
            pt1[:, lanes] = term
        else:
            pt1[:, lanes] = pt1[:, lanes] + term

    def start_rows(h):
        ring = ring_gather(
            dirs, [(lambda k: x_at(k) * PAD, ROWS)], h * W, W, x_peer, sx_s.at[h], sx_r.at[h]
        )
        next(ring)
        yield
        next(ring)
        yield
        for k in (0, -1, 1):
            accumulate_pt1(h, k)
        yield
        run(ring)
        accumulate_pt1(h, 2)

    def other_tokens(h):
        cols = pl.ds(h * W, W)
        passed = []

        def pass_on(k):
            if k != 0:
                at = (rows(x_at(k) * GRP + c * HALF, HALF), cols)
                passed.append(send(X.at[at], X.at[at], xac_s.at[h, k % 4], xac_r.at[h, k % 4], c_peer))

        yield from ring_gather(
            X, [(lambda k: x_at(k) * GRP + c * HALF, HALF)], h * W, W, x_peer, xa_s.at[h], xa_r.at[h], pass_on
        )
        yield
        wait_all(passed)

    def local_work():
        loads[-1].wait()
        dirs[rows(x * PAD, ROWS), :] = start[...].astype(bf16)
        for g in s_gens:
            next(g)
        for b in range(N_X):
            pad = pl.ds(b * PAD + ROWS, PAD - ROWS)
            up[pad, :] = jnp.zeros((PAD - ROWS, D), bf16)
            down[pad, :] = jnp.zeros((PAD - ROWS, D), bf16)
            dirs[pad, :] = jnp.zeros((PAD - ROWS, D), bf16)
        yield
        for cp in loads[:-1]:
            cp.wait()
        arv[0, 0, 1] = tile_sum(start[...] * start[...])

    s_gens = [start_rows(h) for h in range(CHUNKS)]
    both = list(range(CHUNKS))
    n = CHUNKS
    play([group_tokens(h) for h in range(CHUNKS)] + [local_work()], both + [n] + both + [n] + both + both)

    def to_branch(i, h):
        for k in range(h * W, (h + 1) * W, W // 3):
            part[i % 2, :, k : k + W // 3] = dot(hact[...], down[:, k : k + W // 3])

    def weights():
        return tgt[...].astype(f32), gain[...]

    def forward():
        for b in range(N_X):
            cols = pl.ds(b * PAD, PAD)
            value, first, second = gelu_parts(agrad[0, :, cols])
            hact[:, cols] = value.astype(bf16)
            slope[:, cols] = first
            bendag[:, cols] = second
        yield from scatters(0, to_branch)
        bsum[...] = hin[...].astype(f32) + tot[0]
        yield from gathers(loss_grad(bsum[...], *weights()).astype(bf16), 0)
        bendag[...] = bendag[...] * agrad[0]

    def first_tangent():
        hact[...] = (slope[...] * pt1[...]).astype(bf16)
        yield from scatters(1, to_branch)

    fwd = forward()
    others = [other_tokens(h) for h in range(CHUNKS)]
    for g in s_gens + [fwd] + s_gens + [fwd] + s_gens + [fwd]:
        next(g, None)
    tangent = first_tangent()
    for g in [tangent, fwd] + others:
        next(g, None)
    run(tangent, fwd)
    curv = loss_curv(bsum[...], tot[1], *weights())

    def token_gram():
        half = TOK // 2
        for b in range(2):
            g = dot_t(X[group, :], X[pl.ds(b * half, half), :])
            hi = g.astype(bf16)
            g_hi[:, pl.ds(b * half, half)] = hi
            g_lo[:, pl.ds(b * half, half)] = (g - hi.astype(f32)).astype(bf16)
            yield

    grads = gathers(curv.astype(bf16), 1)
    for g in [grads] + others + [grads] + others + [grads] + others + [grads]:
        next(g, None)
    run(token_gram())
    run(grads)
    p1 = agrad[1] * slope[...] + bendag[...] * pt1[...]
    pfull[group, :] = p1.astype(bf16)

    def share_p1():
        def use(k):
            block = rows(x_at(k) * GRP, GRP)
            term = dot(g_hi[:, block], pfull[block, :]) + dot(g_lo[:, block], pfull[block, :])
            if k == 0:
                ptx[...] = term
            else:
                ptx[...] = ptx[...] + term

        cps = [
            send(pfull.at[group], pfull.at[group], pf_s.at[k - 1], pf_r.at[k - 1], x_peer(k))
            for k in range(1, N_X)
        ]
        use(0)
        yield
        for k in (1, 3, 2):
            wait_all([cps[k - 1]])
            use(N_X - k)

    def own_sums():
        arv[0, 0, 0] = tile_sum(p1 * pt1[...])
        yield

    run(share_p1(), own_sums())

    hact[...] = (slope[...] * ptx[...]).astype(bf16)

    def image_one():
        own = pfull[:, pl.ds(pl.multiple_of(x * PAD, PAD), PAD)].T
        for k in range(0, D, 512):
            kw[:, k : k + 512] = dot(own, X[:, k : k + 512])[0:ROWS, :]
            if k % 1536 == 1024:
                yield

    run(scatters(2, to_branch), all_sum(0, 2), image_one())
    count = float(ROWS * 256 * D)
    q = jnp.sum(arv[0, 2, 0], keepdims=True) / count
    ss = jnp.sum(arv[0, 2, 1], keepdims=True) / count
    s1 = lax.rsqrt(ss + norm_eps)
    h11 = s1 * s1 * q
    curv = loss_curv(bsum[...], tot[2] - h11 * tot[1], *weights())

    def remainder():
        ptx[...] = ptx[...] - h11 * pt1[...]
        acc = None
        for k in range(0, D, 1536):
            w = kw[:, k : k + 1536] - h11 * start[:, k : k + 1536]
            kw[:, k : k + 1536] = w
            s = tile_sum(w * w)
            acc = s if acc is None else acc + s
            yield
        arv[1, 0, 0] = acc

    run(gathers(curv.astype(bf16), 2), remainder())
    out_w = pltpu.make_async_copy(kw, kw_hbm, out_sem.at[0])
    out_w.start()
    for b in range(N_X):
        cols = pl.ds(b * PAD, PAD)
        pr2[1, b] = (agrad[0, :, cols] * slope[:, cols] + bendag[:, cols] * ptx[:, cols]).astype(bf16)
    pr2[0, x] = pr2[1, x]
    cps = [
        send(pr2.at[1, x_at(k)], pr2.at[0, x], p2_s.at[k - 1], p2_r.at[k - 1], x_peer(k))
        for k in range(1, N_X)
    ]
    wait_all(cps)
    own = pr2[0].reshape(TOK, PAD).T
    sums = [None, None, None]
    for k in range(0, D, 512):
        cols = slice(k, k + 512)
        acc = dot(own, X[:, cols])[0:ROWS, :]
        k2[:, cols] = acc
        for j, other in enumerate((start[:, cols], kw[:, cols], acc)):
            s = tile_sum(other * acc)
            sums[j] = s if sums[j] is None else sums[j] + s
    for j in range(3):
        arv[1, 0, 1 + j] = sums[j]
    out_2 = pltpu.make_async_copy(k2, k2_hbm, out_sem.at[1])
    out_2.start()
    run(all_sum(1, 4))
    ww, sk, wk, kk = [jnp.sum(arv[1, 2, j], keepdims=True) / count for j in range(4)]
    sq1 = s1 * s1 * ww
    scale2 = lax.rsqrt(sq1 + norm_eps)
    s2 = scale2 * s1
    h12 = s1 * s2 * sk
    h22 = s2 * s2 * wk
    cross = s1 * s2 * (q - h11 * ss)
    sq2 = (
        s2 * s2 * kk
        - 2.0 * (h12 * h12 + h22 * h22)
        + h12 * h12 * (s1 * s1 * ss)
        + h22 * h22 * (s2 * s2 * ww)
        + 2.0 * h12 * h22 * cross
    )
    sq2 = jnp.maximum(sq2, 0.0)
    s3 = lax.rsqrt(sq2 + norm_eps)
    results = (h11, h12, h22, jnp.sqrt(sq1), jnp.sqrt(sq2), s2, s3 * s2, -s3 * h12 * s1, -s3 * h22 * s2)
    for j, value in enumerate(results):
        mix[j] = value[0, 0]
    out_w.wait()
    out_2.wait()
    settle(0)


def combine(mix, kw_hbm, k2_hbm, start_hbm, basis_hbm, quot, coef, kw, k2, start, out, in_sem, out_sem):
    parts = [pl.ds(r, PIECE) for r in range(0, ROWS, PIECE)]
    ins = [
        [
            pltpu.make_async_copy(src.at[at], dst.at[at], in_sem.at[j, p])
            for j, (src, dst) in enumerate(((kw_hbm, kw), (k2_hbm, k2), (start_hbm, start)))
        ]
        for p, at in enumerate(parts)
    ]
    for cps in ins:
        for cp in cps:
            cp.start()
    quot[0] = mix[0]
    coef[0, 0] = mix[1]
    coef[0, 1] = mix[2]
    coef[1, 0] = mix[3]
    coef[1, 1] = mix[4]
    outs = []
    for p, at in enumerate(parts):
        for cp in ins[p]:
            cp.wait()
        w = kw[at, :]
        out[0, at, :] = mix[5] * w
        out[1, at, :] = mix[6] * k2[at, :] + mix[7] * start[at, :] + mix[8] * w
        for j in range(2):
            cp = pltpu.make_async_copy(out.at[j, at], basis_hbm.at[j, at], out_sem.at[j, p])
            cp.start()
            outs.append(cp)
    for cp in outs:
        cp.wait()


def per_device(hidden_in, targets, norm_gain, up_weight, down_weight, start):
    vm, dma = pltpu.VMEM, pltpu.SemaphoreType.DMA
    any_spec = pl.BlockSpec(memory_space=pl.ANY)
    vmem_spec = pl.BlockSpec(memory_space=pltpu.VMEM)
    smem_spec = pl.BlockSpec(memory_space=pltpu.SMEM)
    scratch = [
        vm((HID, D), bf16),
        vm((HID, D), bf16),
        vm((ROWS, D), f32),
        vm((HID, D), bf16),
        vm((TOK, D), bf16),
        vm((CHUNKS, N_Z, OWN, W), bf16),
        vm((BLK, D), f32),
        vm((2, GRP, D), f32),
        vm((3, CHUNKS, 3, BLK, W), bf16),
        vm((3, CHUNKS, 3, BLK, W), bf16),
        vm((3, CHUNKS, 2, BLK, W), bf16),
        vm((3, CHUNKS, 2, BLK, W), bf16),
        vm((3, CHUNKS, 2, BLK, W), bf16),
        vm((3, CHUNKS, 2, BLK, W), bf16),
        vm((3, CHUNKS, N_Z, OWN, W), bf16),
        vm((3, CHUNKS, N_Z - 1, OWN, W), bf16),
        vm((3, CHUNKS, N_Z, OWN, W), bf16),
        vm((3, GRP, D), bf16),
        vm((GRP, HID), f32),
        vm((GRP, HID), f32),
        vm((GRP, HID), bf16),
        vm((2, GRP, HID), f32),
        vm((GRP, HID), f32),
        vm((GRP, HID), f32),
        vm((TOK, HID), bf16),
        vm((2, N_X, GRP, PAD), bf16),
        vm((GRP, TOK), bf16),
        vm((GRP, TOK), bf16),
        vm((ROWS, D), f32),
        vm((ROWS, D), f32),
        vm((2, 3, 4, 8, 128), f32),
        vm((2, 2, 15, 4, 8, 128), f32),
        vm((3, OWN, D), f32),
        vm((OWN, D), f32),
        dma((2 * N_X + 1,)),
    ]
    pairs = [
        (CHUNKS,), (CHUNKS, 6), (CHUNKS, 4),
        (CHUNKS, 4), (CHUNKS, 4), (CHUNKS, 4),
        (3, CHUNKS), (3, CHUNKS, 4), (3, CHUNKS, 2), (3, CHUNKS),
        (3, CHUNKS), (3, CHUNKS, 6), (3, CHUNKS, 4),
        (N_X - 1,), (N_X - 1,), (2, 2),
    ]
    for shape in pairs:
        scratch += [dma(shape), dma(shape)]
    scratch.append(dma((2,)))
    kw, k2, mix = pl.pallas_call(
        kernel,
        out_shape=(
            jax.ShapeDtypeStruct((ROWS, D), f32),
            jax.ShapeDtypeStruct((ROWS, D), f32),
            jax.ShapeDtypeStruct((9,), f32),
        ),
        in_specs=[vmem_spec, vmem_spec, vmem_spec, any_spec, any_spec, any_spec],
        out_specs=(any_spec, any_spec, smem_spec),
        scratch_shapes=scratch,
        compiler_params=pltpu.CompilerParams(
            collective_id=0, has_side_effects=True, vmem_limit_bytes=60 * 1024 * 1024
        ),
        cost_estimate=pl.CostEstimate(flops=5 * 10**9, bytes_accessed=14 * 10**6, transcendentals=10**5),
    )(hidden_in, targets, norm_gain, up_weight, down_weight, start)
    pieces = ROWS // PIECE
    return pl.pallas_call(
        combine,
        out_shape=(
            jax.ShapeDtypeStruct((2, ROWS, D), f32),
            jax.ShapeDtypeStruct((1,), f32),
            jax.ShapeDtypeStruct((2, 2), f32),
        ),
        in_specs=[smem_spec, any_spec, any_spec, any_spec],
        out_specs=(any_spec, smem_spec, smem_spec),
        scratch_shapes=[
            vm((ROWS, D), f32),
            vm((ROWS, D), f32),
            vm((ROWS, D), f32),
            vm((2, ROWS, D), f32),
            dma((3, pieces)),
            dma((2, pieces)),
        ],
        compiler_params=pltpu.CompilerParams(vmem_limit_bytes=60 * 1024 * 1024),
        cost_estimate=pl.CostEstimate(flops=10**7, bytes_accessed=9 * 10**6, transcendentals=0),
    )(mix, kw, k2, start)


def solution(mesh):
    placed = (
        P(("dp", "zero"), None),
        P(("dp", "zero"), None),
        P(),
        P("zero", None),
        P("zero", None),
        P(("zero", "dp"), None),
    )
    return jax.shard_map(
        per_device,
        mesh=mesh,
        in_specs=placed,
        out_specs=(P(None, ("zero", "dp"), None), P(), P()),
        check_vma=False,
    )
```

```python
import jax
import jax.numpy as jnp
from jax import lax
from jax.experimental import pallas as pl
from jax.experimental.pallas import tpu as pltpu
from jax.sharding import PartitionSpec as P

MESH = pl.DeviceIdType.MESH
f32, bf16 = jnp.float32, jnp.bfloat16
norm_eps = 1e-06
gelu_coef = 0.7978845608028654

N_X, N_Y, N_Z, N_C = 4, 4, 8, 2
D = 4608
ROWS = 96
PAD = 128
HID = N_X * PAD
GRP = 128
TOK = N_X * GRP
HALF = GRP // N_C
BLK = HALF // N_Y
OWN = BLK // N_Z
CHUNKS = 2
W = D // CHUNKS
KEEP = 40
PIECE = 32


def gelu_value(inputs):
    return (
        0.5 * inputs * (1.0 + jnp.tanh(gelu_coef * (inputs + 0.044715 * inputs * inputs * inputs)))
    )


def gelu_parts(inputs):
    unit_dir = jnp.ones_like(inputs)

    def first_slope(points):
        return jax.jvp(gelu_value, (points,), (unit_dir,))[1]

    return (
        gelu_value(inputs),
        first_slope(inputs),
        jax.jvp(first_slope, (inputs,), (unit_dir,))[1],
    )


def loss_parts(summed, target, gain):
    r = lax.rsqrt(jnp.sum(summed * summed, axis=-1, keepdims=True) / D + norm_eps)
    normed = summed * r
    pull = (normed * gain - target) * gain
    mean = jnp.sum(pull * normed, axis=-1, keepdims=True) / D
    return r, normed, pull, mean


def loss_grad(summed, target, gain):
    r, normed, pull, mean = loss_parts(summed, target, gain)
    return r * (pull - normed * mean) / float(TOK)


def loss_curv(summed, tangent, target, gain):
    r, normed, pull, mean = loss_parts(summed, target, gain)
    along = jnp.sum(normed * tangent, axis=-1, keepdims=True) / D
    d_normed = r * (tangent - normed * along)
    d_pull = d_normed * gain * gain
    d_mean = jnp.sum(d_pull * normed + pull * d_normed, axis=-1, keepdims=True) / D
    grad = r * (pull - normed * mean)
    d_grad = r * (d_pull - d_normed * mean - normed * d_mean) - (r * along) * grad
    return d_grad / float(TOK)


def dot_t(a, b):
    return lax.dot_general(a, b, (((1,), (1,)), ((), ())), preferred_element_type=f32)


def dot(a, b):
    return jnp.dot(a, b, preferred_element_type=f32)


def tile_sum(v):
    rows, cols = v.shape
    acc = v[0:8, :]
    for i in range(8, rows, 8):
        acc = acc + v[i : i + 8, :]
    out = acc[:, 0:128]
    for k in range(128, cols, 128):
        out = out + acc[:, k : k + 128]
    return out


def par(*gens):
    gens = list(gens)
    while gens:
        for g in list(gens):
            try:
                next(g)
            except StopIteration:
                gens.remove(g)
        if gens:
            yield


def run(*gens):
    for _ in par(*gens):
        pass


def play(gens, order):
    for j in order:
        next(gens[j], None)
    run(*gens)


def kernel(
    hin_hbm, tgt_hbm, gain_hbm, up_hbm, down_hbm, start_hbm,
    kw_hbm, k2_hbm, mix,
    hin, tgt, gain, up, down, start, dirs, X, xz, part,
    sb, rc, y1b, y1r, y2b, y2r, sz, rz, az, A,
    slope, bendag, hact, agrad, pt1, ptx,
    pfull, pr2, g_hi, g_lo, kw, k2, arv, arr, tot, bsum,
    ld_sem, xz_s, xz_r, xy_s, xy_r, xc_s, xc_r,
    xa_s, xa_r, xac_s, xac_r, sx_s, sx_r,
    rc_s, rc_r, y1_s, y1_r, y2_s, y2_r, rz_s, rz_r,
    az_s, az_r, ay_s, ay_r, ac_s, ac_r,
    pf_s, pf_r, p2_s, p2_r, ar_s, ar_r, out_sem,
):
    x = lax.axis_index("dp")
    shard = lax.axis_index("zero")
    y, z, c = shard // 16, (shard // 2) % 8, shard % 2

    def dev(nx, ny, nz, nc):
        return (nx, ny * 16 + nz * 2 + nc)

    pending = []

    xs = [x] + [(x + k) % N_X for k in range(1, N_X)]
    ys = [y] + [(y + k) % N_Y for k in range(1, N_Y)]
    zs = [z] + [(z + k) % N_Z for k in range(1, N_Z)]

    def x_at(k):
        return xs[k % N_X]

    def y_at(k):
        return ys[k % N_Y]

    def x_peer(k):
        return dev(x_at(k), y, z, c)

    def y_peer(k):
        return dev(x, y_at(k), z, c)

    def z_peer(k):
        return dev(x, y, zs[k], c)

    c_peer = dev(x, y, z, 1 - c)

    def cross_peer(k):
        return dev(x, y_at(k), z, 1 - c)

    def xy_peer(k):
        return dev(x_at(k // N_Y), y_at(k % N_Y), z, c)

    def zc_peer(k):
        return dev(x, y, zs[k // N_C], c if k % N_C == 0 else 1 - c)

    def send(src, dst, ssem, rsem, to):
        cp = pltpu.make_async_remote_copy(
            src_ref=src, dst_ref=dst, send_sem=ssem, recv_sem=rsem, device_id=to, device_id_type=MESH
        )
        cp.start()
        pending.append(cp)
        return cp

    def send_all(copies, bytes_of, ssem, rsem):
        for src, dst, to in copies:
            pltpu.make_async_remote_copy(
                src_ref=src, dst_ref=dst, send_sem=ssem, recv_sem=rsem, device_id=to, device_id_type=MESH
            ).start()
        cp = pltpu.make_async_remote_copy(
            src_ref=bytes_of,
            dst_ref=bytes_of,
            send_sem=ssem,
            recv_sem=rsem,
            device_id=c_peer,
            device_id_type=MESH,
        )
        pending.append(cp)
        return [cp]

    def settle(keep=KEEP):
        while len(pending) > keep:
            pending.pop(0).wait_send()

    def rows(start_row, count):
        return pl.ds(pl.multiple_of(start_row, 16), count)

    def wait_all(cps):
        settle()
        for cp in cps:
            cp.wait_recv()

    small = [
        pltpu.make_async_copy(src, dst, ld_sem.at[2 * N_X + 1 + j])
        for j, (src, dst) in enumerate(((hin_hbm, hin), (tgt_hbm, tgt), (gain_hbm, gain)))
    ]
    for cp in small:
        cp.start()
    loads = []
    for b in range(N_X):
        for j, (src, dst) in enumerate(((up_hbm, up), (down_hbm, down))):
            loads.append(
                pltpu.make_async_copy(
                    src.at[pl.ds(b * ROWS, ROWS)], dst.at[pl.ds(b * PAD, ROWS)], ld_sem.at[2 * b + j]
                )
            )
    loads.append(pltpu.make_async_copy(start_hbm, start, ld_sem.at[2 * N_X]))
    for cp in loads:
        cp.start()

    barrier = pltpu.get_barrier_semaphore()
    peers = [xy_peer(k) for k in range(1, N_X * N_Y)] + [zc_peer(k) for k in range(1, N_Z * N_C)]
    peers += [cross_peer(1), cross_peer(-1)]
    for p in peers:
        pl.semaphore_signal(barrier, inc=1, device_id=p, device_id_type=MESH)
    pl.semaphore_wait(barrier, len(peers))
    for cp in small:
        cp.wait()

    def ring_gather(ref, blocks, c0, w, peer, ssem, rsem, then=None, cross=None):
        half = w // 2
        nb = len(blocks)
        first = []
        for b, (row_of, count) in enumerate(blocks):
            at = (rows(row_of(0), count), pl.ds(c0, w))
            first.append(
                [
                    send(ref.at[at], ref.at[at], ssem.at[2 * b + j], rsem.at[2 * b + j], peer(to))
                    for j, to in enumerate((1, -1))
                ]
            )
        if then:
            then(0)
        yield
        second = []
        for b, (row_of, count) in enumerate(blocks):
            for j, to in enumerate((1, -1)):
                wait_all([first[b][j]])
                at = (rows(row_of(-to), count), pl.ds(c0 + j * half, half))
                i = 2 * (nb + b) + j
                second.append(send(ref.at[at], ref.at[at], ssem.at[i], rsem.at[i], peer(to)))
                if cross:
                    second.append(send(ref.at[at], ref.at[at], ssem.at[i + 2], rsem.at[i + 2], cross(to)))
        if then:
            then(-1)
            then(1)
        yield
        wait_all(second)
        if then:
            then(2)

    def gather_z(own, buf, ssem, rsem):
        buf[z] = own
        copies = [(buf.at[z], buf.at[z], z_peer(k)) for k in range(1, N_Z)]
        return send_all(copies, buf.at[pl.ds(0, N_Z - 1)], ssem, rsem)

    def join16(buf):
        return buf[...].reshape(BLK, W)

    def gather(own, i, h):
        c0, out = h * W, A.at[i]
        cols = pl.ds(c0, W)
        cps = gather_z(own[:, c0 : c0 + W], az.at[i, h], az_s.at[i, h], az_r.at[i, h])
        yield
        wait_all(cps)
        out[rows(c * HALF + y * BLK, BLK), cols] = join16(az.at[i, h])
        passed = []

        def pass_on(k):
            if k != 2:
                at = (rows(c * HALF + y_at(k) * BLK, BLK), cols)
                passed.append(send(out.at[at], out.at[at], ac_s.at[i, h, k % 4], ac_r.at[i, h, k % 4], c_peer))

        yield from ring_gather(
            out,
            [(lambda k: c * HALF + y_at(k) * BLK, BLK)],
            c0,
            W,
            y_peer,
            ay_s.at[i, h],
            ay_r.at[i, h],
            pass_on,
            cross_peer,
        )
        wait_all(passed)
        part_grad = dot_t(out[:, cols], down[:, cols])
        if h == 0:
            agrad[i % 2] = part_grad
        else:
            agrad[i % 2] = agrad[i % 2] + part_grad

    def scatter(i, h, make):
        c0 = h * W
        cols = slice(c0, c0 + W)
        make(i, h)
        buf = part.at[i % 2]

        def mine(k):
            return buf[rows(c * HALF + y_at(k) * BLK, BLK), cols]

        def other(k):
            return buf[rows((1 - c) * HALF + y_at(k) * BLK, BLK), cols]

        half = W // 2
        y1b[i, h, 0] = mine(2).astype(bf16)
        y1b[i, h, 1] = other(2).astype(bf16)
        cps = [
            send(
                y1b.at[i, h, p, :, pl.ds(j * half, half)],
                y1r.at[i, h, p, :, pl.ds(j * half, half)],
                y1_s.at[i, h, 2 * p + j],
                y1_r.at[i, h, 2 * p + j],
                peer(to),
            )
            for p, peer in enumerate((y_peer, cross_peer))
            for j, to in enumerate((1, -1))
        ]
        for n, k in enumerate((0, 1, -1)):
            sb[i, h, n] = other(k).astype(bf16)
        cps.append(send(sb.at[i, h], rc.at[i, h], rc_s.at[i, h], rc_r.at[i, h], c_peer))
        yield
        wait_all(cps)
        got = y1r[i, h, 0].astype(f32) + y1r[i, h, 1].astype(f32)
        for j, to in enumerate((1, -1)):
            both_cores = mine(to) + rc[i, h, 1 + j].astype(f32)
            for p in range(2):
                at = slice(p * half, (p + 1) * half)
                piece = both_cores[:, at] + got[:, at] if p == j else both_cores[:, at]
                y2b[i, h, j, :, at] = piece.astype(bf16)
        cps = [
            send(y2b.at[i, h, j], y2r.at[i, h, j], y2_s.at[i, h, j], y2_r.at[i, h, j], y_peer(to))
            for j, to in enumerate((1, -1))
        ]
        yield
        wait_all(cps)
        total = mine(0) + rc[i, h, 0].astype(f32) + y2r[i, h, 0].astype(f32) + y2r[i, h, 1].astype(f32)
        sz[i, h] = total.astype(bf16).reshape(N_Z, OWN, W)
        copies = [(sz.at[i, h, zs[k]], rz.at[i, h, k - 1], z_peer(k)) for k in range(1, N_Z)]
        cps = send_all(copies, rz.at[i, h], rz_s.at[i, h], rz_r.at[i, h])
        yield
        wait_all(cps)
        s3 = sz[i, h, z].astype(f32)
        for k in range(N_Z - 1):
            s3 = s3 + rz[i, h, k].astype(f32)
        tot[i, :, cols] = s3

    def scatters(i, make):
        return par(*[scatter(i, h, make) for h in range(CHUNKS)])

    def gathers(own, i):
        return par(*[gather(own, i, h) for h in range(CHUNKS)])

    def all_sum(i, n):
        for s, peer in enumerate((xy_peer, zc_peer)):
            copies = [
                (arv.at[i, s, pl.ds(0, n)], arr.at[i, s, k - 1, pl.ds(0, n)], peer(k)) for k in range(1, 16)
            ]
            cps = send_all(copies, arr.at[i, s, :, pl.ds(0, n)], ar_s.at[i, s], ar_r.at[i, s])
            yield
            wait_all(cps)
            acc = arv[i, s, 0:n]
            for k in range(1, 16):
                acc = acc + arr[i, s, k - 1, 0:n]
            arv[i, s + 1, 0:n] = acc

    group = rows(x * GRP, GRP)

    def group_tokens(h):
        c0 = h * W
        cols = pl.ds(c0, W)
        cps = gather_z(hin[:, c0 : c0 + W], xz.at[h], xz_s.at[h], xz_r.at[h])
        yield
        wait_all(cps)
        X[rows(x * GRP + c * HALF + y * BLK, BLK), cols] = join16(xz.at[h])
        passed = []

        def pass_on(k):
            if k != 2:
                at = (rows(x * GRP + c * HALF + y_at(k) * BLK, BLK), cols)
                passed.append(send(X.at[at], X.at[at], xc_s.at[h, k % 4], xc_r.at[h, k % 4], c_peer))

        yield from ring_gather(
            X,
            [(lambda k: x * GRP + c * HALF + y_at(k) * BLK, BLK)],
            c0,
            W,
            y_peer,
            xy_s.at[h],
            xy_r.at[h],
            pass_on,
            cross_peer,
        )
        wait_all(passed)
        pre = dot_t(X[group, cols], up[:, cols])
        if h == 0:
            agrad[0] = pre
        else:
            agrad[0] = agrad[0] + pre

    def accumulate_pt1(h, k):
        cols = pl.ds(h * W, W)
        block = rows(x_at(k) * PAD, PAD)
        lanes = pl.ds(pl.multiple_of(x_at(k) * PAD, PAD), PAD)
        term = dot_t(X[group, cols], dirs[block, cols])
        if h == 0:
            pt1[:, lanes] = term
        else:
            pt1[:, lanes] = pt1[:, lanes] + term

    def start_rows(h):
        ring = ring_gather(
            dirs, [(lambda k: x_at(k) * PAD, ROWS)], h * W, W, x_peer, sx_s.at[h], sx_r.at[h]
        )
        next(ring)
        yield
        next(ring)
        yield
        for k in (0, -1, 1):
            accumulate_pt1(h, k)
        yield
        run(ring)
        accumulate_pt1(h, 2)

    def other_tokens(h):
        cols = pl.ds(h * W, W)
        passed = []

        def pass_on(k):
            if k != 0:
                at = (rows(x_at(k) * GRP + c * HALF, HALF), cols)
                passed.append(send(X.at[at], X.at[at], xac_s.at[h, k % 4], xac_r.at[h, k % 4], c_peer))

        yield from ring_gather(
            X, [(lambda k: x_at(k) * GRP + c * HALF, HALF)], h * W, W, x_peer, xa_s.at[h], xa_r.at[h], pass_on
        )
        yield
        wait_all(passed)

    def local_work():
        loads[-1].wait()
        dirs[rows(x * PAD, ROWS), :] = start[...].astype(bf16)
        for g in s_gens:
            next(g)
        for b in range(N_X):
            pad = pl.ds(b * PAD + ROWS, PAD - ROWS)
            up[pad, :] = jnp.zeros((PAD - ROWS, D), bf16)
            down[pad, :] = jnp.zeros((PAD - ROWS, D), bf16)
            dirs[pad, :] = jnp.zeros((PAD - ROWS, D), bf16)
        yield
        for cp in loads[:-1]:
            cp.wait()
        arv[0, 0, 1] = tile_sum(start[...] * start[...])

    s_gens = [start_rows(h) for h in range(CHUNKS)]
    both = list(range(CHUNKS))
    n = CHUNKS
    play([group_tokens(h) for h in range(CHUNKS)] + [local_work()], both + [n] + both + [n] + both + both)

    def to_branch(i, h):
        for k in range(h * W, (h + 1) * W, W // 3):
            part[i % 2, :, k : k + W // 3] = dot(hact[...], down[:, k : k + W // 3])

    def weights():
        return tgt[...].astype(f32), gain[...]

    def forward():
        for b in range(N_X):
            cols = pl.ds(b * PAD, PAD)
            value, first, second = gelu_parts(agrad[0, :, cols])
            hact[:, cols] = value.astype(bf16)
            slope[:, cols] = first
            bendag[:, cols] = second
        yield from scatters(0, to_branch)
        bsum[...] = hin[...].astype(f32) + tot[0]
        yield from gathers(loss_grad(bsum[...], *weights()).astype(bf16), 0)
        bendag[...] = bendag[...] * agrad[0]

    def first_tangent():
        hact[...] = (slope[...] * pt1[...]).astype(bf16)
        yield from scatters(1, to_branch)

    fwd = forward()
    others = [other_tokens(h) for h in range(CHUNKS)]
    for g in s_gens + [fwd] + s_gens + [fwd] + s_gens + [fwd]:
        next(g, None)
    tangent = first_tangent()
    for g in [tangent, fwd] + others:
        next(g, None)
    run(tangent, fwd)
    curv = loss_curv(bsum[...], tot[1], *weights())

    def token_gram(k):
        mine = rows(x_at(k) * GRP, GRP)
        g = dot_t(X[mine, :], X[...])
        hi = g.astype(bf16)
        g_hi[mine, :] = hi
        g_lo[mine, :] = (g - hi.astype(f32)).astype(bf16)

    grads = gathers(curv.astype(bf16), 1)
    for g in [grads] + others + [grads] + others + [grads] + others + [grads]:
        next(g, None)
    token_gram(0)
    run(grads)
    p1 = agrad[1] * slope[...] + bendag[...] * pt1[...]
    pfull[group, :] = p1.astype(bf16)

    def share_p1():
        def use(k):
            block = rows(x_at(k) * GRP, GRP)
            term = dot(g_hi[group, block], pfull[block, :]) + dot(g_lo[group, block], pfull[block, :])
            if k == 0:
                ptx[...] = term
            else:
                ptx[...] = ptx[...] + term

        cps = [
            send(pfull.at[group], pfull.at[group], pf_s.at[k - 1], pf_r.at[k - 1], x_peer(k))
            for k in range(1, N_X)
        ]
        use(0)
        yield
        for k in (1, 3, 2):
            wait_all([cps[k - 1]])
            use(N_X - k)

    def own_sums():
        arv[0, 0, 0] = tile_sum(p1 * pt1[...])
        yield

    run(share_p1(), own_sums())

    hact[...] = (slope[...] * ptx[...]).astype(bf16)

    def image_one():
        own = pfull[:, pl.ds(pl.multiple_of(x * PAD, PAD), PAD)].T
        for k in range(0, D, 512):
            kw[:, k : k + 512] = dot(own, X[:, k : k + 512])[0:ROWS, :]
            if k % 1536 == 1024:
                yield

    run(scatters(2, to_branch), all_sum(0, 2), image_one())
    count = float(ROWS * 256 * D)
    q = jnp.sum(arv[0, 2, 0], keepdims=True) / count
    ss = jnp.sum(arv[0, 2, 1], keepdims=True) / count
    s1 = lax.rsqrt(ss + norm_eps)
    h11 = s1 * s1 * q
    curv = loss_curv(bsum[...], tot[2] - h11 * tot[1], *weights())

    def remainder():
        ptx[...] = ptx[...] - h11 * pt1[...]
        acc = None
        for k in range(0, D, 1536):
            w = kw[:, k : k + 1536] - h11 * start[:, k : k + 1536]
            kw[:, k : k + 1536] = w
            s = tile_sum(w * w)
            acc = s if acc is None else acc + s
            token_gram(k // 1536 + 1)
            yield
        arv[1, 0, 0] = acc

    run(gathers(curv.astype(bf16), 2), remainder())
    out_w = pltpu.make_async_copy(kw, kw_hbm, out_sem.at[0])
    out_w.start()
    for b in range(N_X):
        cols = pl.ds(b * PAD, PAD)
        pr2[1, b] = (agrad[0, :, cols] * slope[:, cols] + bendag[:, cols] * ptx[:, cols]).astype(bf16)
    pr2[0, x] = pr2[1, x]
    cps = [
        send(pr2.at[1, x_at(k)], pr2.at[0, x], p2_s.at[k - 1], p2_r.at[k - 1], x_peer(k))
        for k in range(1, N_X)
    ]
    sums = [None, None]
    for b in range(N_X):
        cols = pl.ds(b * PAD, PAD)
        for j, other in enumerate((pt1, ptx)):
            t = tile_sum(other[:, cols] * pr2[1, b].astype(f32))
            sums[j] = t if sums[j] is None else sums[j] + t
    for j in range(2):
        arv[1, 0, 1 + j] = sums[j]
    wait_all(cps)
    own = pr2[0].reshape(TOK, PAD)
    arv[1, 0, 3] = tile_sum((dot(g_hi[...], own) + dot(g_lo[...], own)) * own.astype(f32))
    outs = [out_w]

    def image_two():
        turned = own.T
        for k in range(0, D, 512):
            k2[:, k : k + 512] = dot(turned, X[:, k : k + 512])[0:ROWS, :]
            if k == 2048:
                yield
        outs.append(pltpu.make_async_copy(k2, k2_hbm, out_sem.at[1]))
        outs[1].start()

    run(all_sum(1, 4), image_two())
    ww, sk, wk, kk = [jnp.sum(arv[1, 2, j], keepdims=True) / count for j in range(4)]
    sq1 = s1 * s1 * ww
    scale2 = lax.rsqrt(sq1 + norm_eps)
    s2 = scale2 * s1
    h12 = s1 * s2 * sk
    h22 = s2 * s2 * wk
    cross = s1 * s2 * (q - h11 * ss)
    sq2 = (
        s2 * s2 * kk
        - 2.0 * (h12 * h12 + h22 * h22)
        + h12 * h12 * (s1 * s1 * ss)
        + h22 * h22 * (s2 * s2 * ww)
        + 2.0 * h12 * h22 * cross
    )
    sq2 = jnp.maximum(sq2, 0.0)
    s3 = lax.rsqrt(sq2 + norm_eps)
    results = (h11, h12, h22, jnp.sqrt(sq1), jnp.sqrt(sq2), s2, s3 * s2, -s3 * h12 * s1, -s3 * h22 * s2)
    for j, value in enumerate(results):
        mix[j] = value[0, 0]
    for cp in outs:
        cp.wait()
    settle(0)


def combine(mix, kw_hbm, k2_hbm, start_hbm, basis_hbm, quot, coef, kw, k2, start, out, in_sem, out_sem):
    parts = [pl.ds(r, PIECE) for r in range(0, ROWS, PIECE)]
    ins = [
        [
            pltpu.make_async_copy(src.at[at], dst.at[at], in_sem.at[j, p])
            for j, (src, dst) in enumerate(((kw_hbm, kw), (k2_hbm, k2), (start_hbm, start)))
        ]
        for p, at in enumerate(parts)
    ]
    for cps in ins:
        for cp in cps:
            cp.start()
    quot[0] = mix[0]
    coef[0, 0] = mix[1]
    coef[0, 1] = mix[2]
    coef[1, 0] = mix[3]
    coef[1, 1] = mix[4]
    outs = []
    for p, at in enumerate(parts):
        for cp in ins[p]:
            cp.wait()
        w = kw[at, :]
        out[0, at, :] = mix[5] * w
        out[1, at, :] = mix[6] * k2[at, :] + mix[7] * start[at, :] + mix[8] * w
        for j in range(2):
            cp = pltpu.make_async_copy(out.at[j, at], basis_hbm.at[j, at], out_sem.at[j, p])
            cp.start()
            outs.append(cp)
    for cp in outs:
        cp.wait()


def per_device(hidden_in, targets, norm_gain, up_weight, down_weight, start):
    vm, dma = pltpu.VMEM, pltpu.SemaphoreType.DMA
    any_spec = pl.BlockSpec(memory_space=pl.ANY)
    smem_spec = pl.BlockSpec(memory_space=pltpu.SMEM)
    scratch = [
        vm((OWN, D), bf16),
        vm((OWN, D), bf16),
        vm((D,), f32),
        vm((HID, D), bf16),
        vm((HID, D), bf16),
        vm((ROWS, D), f32),
        vm((HID, D), bf16),
        vm((TOK, D), bf16),
        vm((CHUNKS, N_Z, OWN, W), bf16),
        vm((2, GRP, D), f32),
        vm((3, CHUNKS, 3, BLK, W), bf16),
        vm((3, CHUNKS, 3, BLK, W), bf16),
        vm((3, CHUNKS, 2, BLK, W), bf16),
        vm((3, CHUNKS, 2, BLK, W), bf16),
        vm((3, CHUNKS, 2, BLK, W), bf16),
        vm((3, CHUNKS, 2, BLK, W), bf16),
        vm((3, CHUNKS, N_Z, OWN, W), bf16),
        vm((3, CHUNKS, N_Z - 1, OWN, W), bf16),
        vm((3, CHUNKS, N_Z, OWN, W), bf16),
        vm((3, GRP, D), bf16),
        vm((GRP, HID), f32),
        vm((GRP, HID), f32),
        vm((GRP, HID), bf16),
        vm((2, GRP, HID), f32),
        vm((GRP, HID), f32),
        vm((GRP, HID), f32),
        vm((TOK, HID), bf16),
        vm((2, N_X, GRP, PAD), bf16),
        vm((TOK, TOK), bf16),
        vm((TOK, TOK), bf16),
        vm((ROWS, D), f32),
        vm((ROWS, D), f32),
        vm((2, 3, 4, 8, 128), f32),
        vm((2, 2, 15, 4, 8, 128), f32),
        vm((3, OWN, D), f32),
        vm((OWN, D), f32),
        dma((2 * N_X + 4,)),
    ]
    pairs = [
        (CHUNKS,), (CHUNKS, 6), (CHUNKS, 4),
        (CHUNKS, 4), (CHUNKS, 4), (CHUNKS, 4),
        (3, CHUNKS), (3, CHUNKS, 4), (3, CHUNKS, 2), (3, CHUNKS),
        (3, CHUNKS), (3, CHUNKS, 6), (3, CHUNKS, 4),
        (N_X - 1,), (N_X - 1,), (2, 2),
    ]
    for shape in pairs:
        scratch += [dma(shape), dma(shape)]
    scratch.append(dma((2,)))
    kw, k2, mix = pl.pallas_call(
        kernel,
        out_shape=(
            jax.ShapeDtypeStruct((ROWS, D), f32),
            jax.ShapeDtypeStruct((ROWS, D), f32),
            jax.ShapeDtypeStruct((9,), f32),
        ),
        in_specs=[any_spec] * 6,
        out_specs=(any_spec, any_spec, smem_spec),
        scratch_shapes=scratch,
        compiler_params=pltpu.CompilerParams(
            collective_id=0, has_side_effects=True, vmem_limit_bytes=60 * 1024 * 1024
        ),
        cost_estimate=pl.CostEstimate(flops=5 * 10**9, bytes_accessed=14 * 10**6, transcendentals=10**5),
    )(hidden_in, targets, norm_gain, up_weight, down_weight, start)
    pieces = ROWS // PIECE
    return pl.pallas_call(
        combine,
        out_shape=(
            jax.ShapeDtypeStruct((2, ROWS, D), f32),
            jax.ShapeDtypeStruct((1,), f32),
            jax.ShapeDtypeStruct((2, 2), f32),
        ),
        in_specs=[smem_spec, any_spec, any_spec, any_spec],
        out_specs=(any_spec, smem_spec, smem_spec),
        scratch_shapes=[
            vm((ROWS, D), f32),
            vm((ROWS, D), f32),
            vm((ROWS, D), f32),
            vm((2, ROWS, D), f32),
            dma((3, pieces)),
            dma((2, pieces)),
        ],
        compiler_params=pltpu.CompilerParams(vmem_limit_bytes=60 * 1024 * 1024),
        cost_estimate=pl.CostEstimate(flops=10**7, bytes_accessed=9 * 10**6, transcendentals=0),
    )(mix, kw, k2, start)


def solution(mesh):
    placed = (
        P(("dp", "zero"), None),
        P(("dp", "zero"), None),
        P(),
        P("zero", None),
        P("zero", None),
        P(("zero", "dp"), None),
    )
    return jax.shard_map(
        per_device,
        mesh=mesh,
        in_specs=placed,
        out_specs=(P(None, ("zero", "dp"), None), P(), P()),
        check_vma=False,
    )
```

```python
import jax
import jax.numpy as jnp
from jax import lax
from jax.experimental import pallas as pl
from jax.experimental.pallas import tpu as pltpu
from jax.sharding import PartitionSpec as P

MESH = pl.DeviceIdType.MESH
f32, bf16 = jnp.float32, jnp.bfloat16
norm_eps = 1e-06
gelu_coef = 0.7978845608028654

N_X, N_Y, N_Z, N_C = 4, 4, 8, 2
D = 4608
ROWS = 96
PAD = 128
HID = N_X * PAD
GRP = 128
TOK = N_X * GRP
HALF = GRP // N_C
BLK = HALF // N_Y
OWN = BLK // N_Z
CHUNKS = 2
W = D // CHUNKS
SPANS = ((0, 1536), (1536, 1280))
XA = 2816
KEEP = 40
PIECE = 32


def gelu_value(inputs):
    return (
        0.5 * inputs * (1.0 + jnp.tanh(gelu_coef * (inputs + 0.044715 * inputs * inputs * inputs)))
    )


def gelu_parts(inputs):
    unit_dir = jnp.ones_like(inputs)

    def first_slope(points):
        return jax.jvp(gelu_value, (points,), (unit_dir,))[1]

    return (
        gelu_value(inputs),
        first_slope(inputs),
        jax.jvp(first_slope, (inputs,), (unit_dir,))[1],
    )


def loss_parts(summed, target, gain):
    r = lax.rsqrt(jnp.sum(summed * summed, axis=-1, keepdims=True) / D + norm_eps)
    normed = summed * r
    pull = (normed * gain - target) * gain
    mean = jnp.sum(pull * normed, axis=-1, keepdims=True) / D
    return r, normed, pull, mean


def loss_grad(summed, target, gain):
    r, normed, pull, mean = loss_parts(summed, target, gain)
    return r * (pull - normed * mean) / float(TOK)


def loss_curv(summed, tangent, target, gain):
    r, normed, pull, mean = loss_parts(summed, target, gain)
    along = jnp.sum(normed * tangent, axis=-1, keepdims=True) / D
    d_normed = r * (tangent - normed * along)
    d_pull = d_normed * gain * gain
    d_mean = jnp.sum(d_pull * normed + pull * d_normed, axis=-1, keepdims=True) / D
    grad = r * (pull - normed * mean)
    d_grad = r * (d_pull - d_normed * mean - normed * d_mean) - (r * along) * grad
    return d_grad / float(TOK)


def dot_t(a, b):
    return lax.dot_general(a, b, (((1,), (1,)), ((), ())), preferred_element_type=f32)


def dot(a, b):
    return jnp.dot(a, b, preferred_element_type=f32)


def tile_sum(v):
    rows, cols = v.shape
    acc = v[0:8, :]
    for i in range(8, rows, 8):
        acc = acc + v[i : i + 8, :]
    out = acc[:, 0:128]
    for k in range(128, cols, 128):
        out = out + acc[:, k : k + 128]
    return out


def par(*gens):
    gens = list(gens)
    while gens:
        for g in list(gens):
            try:
                next(g)
            except StopIteration:
                gens.remove(g)
        if gens:
            yield


def run(*gens):
    for _ in par(*gens):
        pass


def kernel(
    hin_hbm, tgt_hbm, gain_hbm, up_hbm, down_hbm, start_hbm,
    kw_hbm, k2_hbm, mix,
    hin, tgt, gain, up, down, start, dirs, X, xz, part,
    sb, rc, y1b, y1r, y2b, y2r, sz, rz, az, A,
    slope, bendag, hact, agrad, pt1, ptx, pts, ptr,
    pfull, pr2, g_hi, g_lo, kw, k2, arv, arr, tot, bsum,
    ld_sem, xz_s, xz_r, xy_s, xy_r, xc_s, xc_r,
    xa_s, xa_r, xac_s, xac_r, sx_s, sx_r, xb_s, xb_r, xby_s, xby_r, xbc_s, xbc_r, pt_s, pt_r,
    rc_s, rc_r, y1_s, y1_r, y2_s, y2_r, rz_s, rz_r,
    az_s, az_r, ay_s, ay_r, ac_s, ac_r,
    pf_s, pf_r, p2_s, p2_r, ar_s, ar_r, out_sem,
):
    x = lax.axis_index("dp")
    shard = lax.axis_index("zero")
    y, z, c = shard // 16, (shard // 2) % 8, shard % 2

    def dev(nx, ny, nz, nc):
        return (nx, ny * 16 + nz * 2 + nc)

    pending = []

    xs = [x] + [(x + k) % N_X for k in range(1, N_X)]
    ys = [y] + [(y + k) % N_Y for k in range(1, N_Y)]
    zs = [z] + [(z + k) % N_Z for k in range(1, N_Z)]

    def x_at(k):
        return xs[k % N_X]

    def y_at(k):
        return ys[k % N_Y]

    def x_peer(k):
        return dev(x_at(k), y, z, c)

    def y_peer(k):
        return dev(x, y_at(k), z, c)

    def z_peer(k):
        return dev(x, y, zs[k], c)

    c_peer = dev(x, y, z, 1 - c)

    def cross_peer(k):
        return dev(x, y_at(k), z, 1 - c)

    def xy_peer(k):
        return dev(x_at(k // N_Y), y_at(k % N_Y), z, c)

    def zc_peer(k):
        return dev(x, y, zs[k // N_C], c if k % N_C == 0 else 1 - c)

    def send(src, dst, ssem, rsem, to):
        cp = pltpu.make_async_remote_copy(
            src_ref=src, dst_ref=dst, send_sem=ssem, recv_sem=rsem, device_id=to, device_id_type=MESH
        )
        cp.start()
        pending.append(cp)
        return cp

    def send_all(copies, bytes_of, ssem, rsem):
        for src, dst, to in copies:
            pltpu.make_async_remote_copy(
                src_ref=src, dst_ref=dst, send_sem=ssem, recv_sem=rsem, device_id=to, device_id_type=MESH
            ).start()
        cp = pltpu.make_async_remote_copy(
            src_ref=bytes_of,
            dst_ref=bytes_of,
            send_sem=ssem,
            recv_sem=rsem,
            device_id=c_peer,
            device_id_type=MESH,
        )
        pending.append(cp)
        return [cp]

    def settle(keep=KEEP):
        while len(pending) > keep:
            pending.pop(0).wait_send()

    def rows(start_row, count):
        return pl.ds(pl.multiple_of(start_row, 16), count)

    def wait_all(cps):
        settle()
        for cp in cps:
            cp.wait_recv()

    small = [
        pltpu.make_async_copy(src, dst, ld_sem.at[2 * N_X + 1 + j])
        for j, (src, dst) in enumerate(((hin_hbm, hin), (tgt_hbm, tgt), (gain_hbm, gain)))
    ]
    for cp in small:
        cp.start()
    loads = []
    for b in range(N_X):
        for j, (src, dst) in enumerate(((up_hbm, up), (down_hbm, down))):
            loads.append(
                pltpu.make_async_copy(
                    src.at[pl.ds(b * ROWS, ROWS)], dst.at[pl.ds(b * PAD, ROWS)], ld_sem.at[2 * b + j]
                )
            )
    loads.append(pltpu.make_async_copy(start_hbm, start, ld_sem.at[2 * N_X]))
    for cp in loads:
        cp.start()

    barrier = pltpu.get_barrier_semaphore()
    peers = [xy_peer(k) for k in range(1, N_X * N_Y)] + [zc_peer(k) for k in range(1, N_Z * N_C)]
    peers += [cross_peer(1), cross_peer(-1)]
    for p in peers:
        pl.semaphore_signal(barrier, inc=1, device_id=p, device_id_type=MESH)
    pl.semaphore_wait(barrier, len(peers))
    for cp in small:
        cp.wait()

    def ring_gather(ref, blocks, c0, w, peer, ssem, rsem, then=None, cross=None):
        half = w // 2
        nb = len(blocks)
        first = []
        for b, (row_of, count) in enumerate(blocks):
            at = (rows(row_of(0), count), pl.ds(c0, w))
            first.append(
                [
                    send(ref.at[at], ref.at[at], ssem.at[2 * b + j], rsem.at[2 * b + j], peer(to))
                    for j, to in enumerate((1, -1))
                ]
            )
        if then:
            then(0)
        yield
        second = []
        for b, (row_of, count) in enumerate(blocks):
            for j, to in enumerate((1, -1)):
                wait_all([first[b][j]])
                at = (rows(row_of(-to), count), pl.ds(c0 + j * half, half))
                i = 2 * (nb + b) + j
                second.append(send(ref.at[at], ref.at[at], ssem.at[i], rsem.at[i], peer(to)))
                if cross:
                    second.append(send(ref.at[at], ref.at[at], ssem.at[i + 2], rsem.at[i + 2], cross(to)))
        if then:
            then(-1)
            then(1)
        yield
        wait_all(second)
        if then:
            then(2)

    def gather_z(own, buf, ssem, rsem):
        buf[z] = own
        copies = [(buf.at[z], buf.at[z], z_peer(k)) for k in range(1, N_Z)]
        return send_all(copies, buf.at[pl.ds(0, N_Z - 1)], ssem, rsem)

    def join16(buf):
        return buf[...].reshape(BLK, W)

    def gather(own, i, h):
        c0, out = h * W, A.at[i]
        cols = pl.ds(c0, W)
        cps = gather_z(own[:, c0 : c0 + W], az.at[i, h], az_s.at[i, h], az_r.at[i, h])
        yield
        wait_all(cps)
        out[rows(c * HALF + y * BLK, BLK), cols] = join16(az.at[i, h])
        passed = []

        def pass_on(k):
            if k != 2:
                at = (rows(c * HALF + y_at(k) * BLK, BLK), cols)
                passed.append(send(out.at[at], out.at[at], ac_s.at[i, h, k % 4], ac_r.at[i, h, k % 4], c_peer))

        yield from ring_gather(
            out,
            [(lambda k: c * HALF + y_at(k) * BLK, BLK)],
            c0,
            W,
            y_peer,
            ay_s.at[i, h],
            ay_r.at[i, h],
            pass_on,
            cross_peer,
        )
        wait_all(passed)
        part_grad = dot_t(out[:, cols], down[:, cols])
        if h == 0:
            agrad[i % 2] = part_grad
        else:
            agrad[i % 2] = agrad[i % 2] + part_grad

    def scatter(i, h, make):
        c0 = h * W
        cols = slice(c0, c0 + W)
        make(i, h)
        buf = part.at[i % 2]

        def mine(k):
            return buf[rows(c * HALF + y_at(k) * BLK, BLK), cols]

        def other(k):
            return buf[rows((1 - c) * HALF + y_at(k) * BLK, BLK), cols]

        half = W // 2
        y1b[i, h, 0] = mine(2).astype(bf16)
        y1b[i, h, 1] = other(2).astype(bf16)
        cps = [
            send(
                y1b.at[i, h, p, :, pl.ds(j * half, half)],
                y1r.at[i, h, p, :, pl.ds(j * half, half)],
                y1_s.at[i, h, 2 * p + j],
                y1_r.at[i, h, 2 * p + j],
                peer(to),
            )
            for p, peer in enumerate((y_peer, cross_peer))
            for j, to in enumerate((1, -1))
        ]
        for n, k in enumerate((0, 1, -1)):
            sb[i, h, n] = other(k).astype(bf16)
        cps.append(send(sb.at[i, h], rc.at[i, h], rc_s.at[i, h], rc_r.at[i, h], c_peer))
        yield
        wait_all(cps)
        got = y1r[i, h, 0].astype(f32) + y1r[i, h, 1].astype(f32)
        for j, to in enumerate((1, -1)):
            both_cores = mine(to) + rc[i, h, 1 + j].astype(f32)
            for p in range(2):
                at = slice(p * half, (p + 1) * half)
                piece = both_cores[:, at] + got[:, at] if p == j else both_cores[:, at]
                y2b[i, h, j, :, at] = piece.astype(bf16)
        cps = [
            send(y2b.at[i, h, j], y2r.at[i, h, j], y2_s.at[i, h, j], y2_r.at[i, h, j], y_peer(to))
            for j, to in enumerate((1, -1))
        ]
        yield
        wait_all(cps)
        total = mine(0) + rc[i, h, 0].astype(f32) + y2r[i, h, 0].astype(f32) + y2r[i, h, 1].astype(f32)
        sz[i, h] = total.astype(bf16).reshape(N_Z, OWN, W)
        copies = [(sz.at[i, h, zs[k]], rz.at[i, h, k - 1], z_peer(k)) for k in range(1, N_Z)]
        cps = send_all(copies, rz.at[i, h], rz_s.at[i, h], rz_r.at[i, h])
        yield
        wait_all(cps)
        s3 = sz[i, h, z].astype(f32)
        for k in range(N_Z - 1):
            s3 = s3 + rz[i, h, k].astype(f32)
        tot[i, :, cols] = s3

    def scatters(i, make):
        return par(*[scatter(i, h, make) for h in range(CHUNKS)])

    def gathers(own, i):
        return par(*[gather(own, i, h) for h in range(CHUNKS)])

    def all_sum(i, n):
        for s, peer in enumerate((xy_peer, zc_peer)):
            copies = [
                (arv.at[i, s, pl.ds(0, n)], arr.at[i, s, k - 1, pl.ds(0, n)], peer(k)) for k in range(1, 16)
            ]
            cps = send_all(copies, arr.at[i, s, :, pl.ds(0, n)], ar_s.at[i, s], ar_r.at[i, s])
            yield
            wait_all(cps)
            acc = arv[i, s, 0:n]
            for k in range(1, 16):
                acc = acc + arr[i, s, k - 1, 0:n]
            arv[i, s + 1, 0:n] = acc

    group = rows(x * GRP, GRP)

    def group_tokens(h):
        c0 = h * W
        cols = pl.ds(c0, W)
        cps = gather_z(hin[:, c0 : c0 + W], xz.at[h], xz_s.at[h], xz_r.at[h])
        yield
        wait_all(cps)
        X[rows(x * GRP + c * HALF + y * BLK, BLK), cols] = join16(xz.at[h])
        passed = []

        def pass_on(k):
            if k != 2:
                at = (rows(x * GRP + c * HALF + y_at(k) * BLK, BLK), cols)
                passed.append(send(X.at[at], X.at[at], xc_s.at[h, k % 4], xc_r.at[h, k % 4], c_peer))

        yield from ring_gather(
            X,
            [(lambda k: x * GRP + c * HALF + y_at(k) * BLK, BLK)],
            c0,
            W,
            y_peer,
            xy_s.at[h],
            xy_r.at[h],
            pass_on,
            cross_peer,
        )
        wait_all(passed)
        pre = dot_t(X[group, cols], up[:, cols])
        if h == 0:
            agrad[0] = pre
        else:
            agrad[0] = agrad[0] + pre

    def accumulate_pt1(h, k):
        cols = pl.ds(*SPANS[h])
        block = rows(x_at(k) * PAD, PAD)
        lanes = pl.ds(pl.multiple_of(x_at(k) * PAD, PAD), PAD)
        term = dot_t(X[group, cols], dirs[block, cols])
        if h == 0:
            pt1[:, lanes] = term
        else:
            pt1[:, lanes] = pt1[:, lanes] + term

    def start_rows(h):
        ring = ring_gather(
            dirs, [(lambda k: x_at(k) * PAD, ROWS)], *SPANS[h], x_peer, sx_s.at[h], sx_r.at[h]
        )
        next(ring)
        yield
        next(ring)
        yield
        for k in (0, -1, 1):
            accumulate_pt1(h, k)
        yield
        run(ring)
        accumulate_pt1(h, 2)

    def other_tokens(h):
        cols = pl.ds(*SPANS[h])
        passed = []

        def pass_on(k):
            if k != 0:
                at = (rows(x_at(k) * GRP + c * HALF, HALF), cols)
                passed.append(send(X.at[at], X.at[at], xac_s.at[h, k % 4], xac_r.at[h, k % 4], c_peer))

        yield from ring_gather(
            X,
            [(lambda k: x_at(k) * GRP + c * HALF, HALF)],
            *SPANS[h],
            x_peer,
            xa_s.at[h],
            xa_r.at[h],
            pass_on,
        )
        yield
        wait_all(passed)

    def far_tokens():
        yield from ring_gather(
            X, [(lambda k: x_at(k) * GRP + c * HALF + y * BLK, BLK)], XA, D - XA, x_peer, xb_s, xb_r
        )
        blocks = [
            (lambda k, b=b: x_at(b) * GRP + c * HALF + y_at(k) * BLK, BLK) for b in range(1, N_X)
        ]
        yield from ring_gather(X, blocks, XA, D - XA, y_peer, xby_s, xby_r)
        passed = []
        for b in range(1, N_X):
            at = (rows(x_at(b) * GRP + c * HALF, HALF), pl.ds(XA, D - XA))
            passed.append(send(X.at[at], X.at[at], xbc_s.at[b], xbc_r.at[b], c_peer))
        yield
        wait_all(passed)
        cols = pl.ds(XA, D - XA)
        pts[...] = dot_t(X[:, cols], dirs[rows(x * PAD, PAD), cols])
        ptr[x] = pts[group, :]
        cps = [
            send(pts.at[rows(x_at(k) * GRP, GRP)], ptr.at[x], pt_s.at[k - 1], pt_r.at[k - 1], x_peer(k))
            for k in range(1, N_X)
        ]
        yield
        wait_all(cps)

    def local_work():
        loads[-1].wait()
        dirs[rows(x * PAD, ROWS), :] = start[...].astype(bf16)
        for g in s_gens:
            next(g)
        for b in range(N_X):
            pad = pl.ds(b * PAD + ROWS, PAD - ROWS)
            up[pad, :] = jnp.zeros((PAD - ROWS, D), bf16)
            down[pad, :] = jnp.zeros((PAD - ROWS, D), bf16)
            dirs[pad, :] = jnp.zeros((PAD - ROWS, D), bf16)
        yield
        for cp in loads[:-1]:
            cp.wait()
        arv[0, 0, 1] = tile_sum(start[...] * start[...])

    s_gens = [start_rows(h) for h in range(2)]
    far = far_tokens()
    local_work_gen = local_work()
    toks = [group_tokens(h) for h in range(CHUNKS)]
    for g in toks + [local_work_gen] + toks + [far, local_work_gen] + toks + [far] + toks:
        next(g, None)

    def to_branch(i, h):
        for k in range(h * W, (h + 1) * W, W // 3):
            part[i % 2, :, k : k + W // 3] = dot(hact[...], down[:, k : k + W // 3])

    def weights():
        return tgt[...].astype(f32), gain[...]

    def forward():
        for b in range(N_X):
            cols = pl.ds(b * PAD, PAD)
            value, first, second = gelu_parts(agrad[0, :, cols])
            hact[:, cols] = value.astype(bf16)
            slope[:, cols] = first
            bendag[:, cols] = second
        yield from scatters(0, to_branch)
        bsum[...] = hin[...].astype(f32) + tot[0]
        yield from gathers(loss_grad(bsum[...], *weights()).astype(bf16), 0)
        bendag[...] = bendag[...] * agrad[0]

    def first_tangent():
        for b in range(N_X):
            lanes = pl.ds(b * PAD, PAD)
            whole = pt1[:, lanes] + ptr[b]
            pt1[:, lanes] = whole
            hact[:, lanes] = (slope[:, lanes] * whole).astype(bf16)
        yield from scatters(1, to_branch)

    fwd = forward()
    others = [other_tokens(h) for h in range(2)]
    for g in [far] + s_gens + [fwd, far] + s_gens + [fwd, far] + s_gens + [far, fwd, far]:
        next(g, None)
    tangent = first_tangent()
    for g in [tangent, fwd] + others:
        next(g, None)
    run(tangent, fwd)
    curv = loss_curv(bsum[...], tot[1], *weights())

    def token_gram(k):
        mine = rows(x_at(k) * GRP, GRP)
        g = dot_t(X[mine, :], X[...])
        hi = g.astype(bf16)
        g_hi[mine, :] = hi
        g_lo[mine, :] = (g - hi.astype(f32)).astype(bf16)

    grads = gathers(curv.astype(bf16), 1)
    for g in [grads] + others + [grads] + others + [grads] + others + [grads]:
        next(g, None)
    token_gram(0)
    run(grads)
    p1 = agrad[1] * slope[...] + bendag[...] * pt1[...]
    pfull[group, :] = p1.astype(bf16)

    def share_p1():
        def use(k):
            block = rows(x_at(k) * GRP, GRP)
            term = dot(g_hi[group, block], pfull[block, :]) + dot(g_lo[group, block], pfull[block, :])
            if k == 0:
                ptx[...] = term
            else:
                ptx[...] = ptx[...] + term

        cps = [
            send(pfull.at[group], pfull.at[group], pf_s.at[k - 1], pf_r.at[k - 1], x_peer(k))
            for k in range(1, N_X)
        ]
        use(0)
        yield
        for k in (1, 3, 2):
            wait_all([cps[k - 1]])
            use(N_X - k)

    def own_sums():
        arv[0, 0, 0] = tile_sum(p1 * pt1[...])
        yield

    run(share_p1(), own_sums())

    hact[...] = (slope[...] * ptx[...]).astype(bf16)

    def image_one():
        own = pfull[:, pl.ds(pl.multiple_of(x * PAD, PAD), PAD)].T
        for k in range(0, D, 512):
            kw[:, k : k + 512] = dot(own, X[:, k : k + 512])[0:ROWS, :]
            if k % 1536 == 1024:
                yield

    run(scatters(2, to_branch), all_sum(0, 2), image_one())
    count = float(ROWS * 256 * D)
    q = jnp.sum(arv[0, 2, 0], keepdims=True) / count
    ss = jnp.sum(arv[0, 2, 1], keepdims=True) / count
    s1 = lax.rsqrt(ss + norm_eps)
    h11 = s1 * s1 * q
    curv = loss_curv(bsum[...], tot[2] - h11 * tot[1], *weights())

    def remainder():
        ptx[...] = ptx[...] - h11 * pt1[...]
        acc = None
        for k in range(0, D, 1536):
            w = kw[:, k : k + 1536] - h11 * start[:, k : k + 1536]
            kw[:, k : k + 1536] = w
            s = tile_sum(w * w)
            acc = s if acc is None else acc + s
            token_gram(k // 1536 + 1)
            yield
        arv[1, 0, 0] = acc

    run(gathers(curv.astype(bf16), 2), remainder())
    out_w = pltpu.make_async_copy(kw, kw_hbm, out_sem.at[0])
    out_w.start()
    for b in range(N_X):
        cols = pl.ds(b * PAD, PAD)
        pr2[1, b] = (agrad[0, :, cols] * slope[:, cols] + bendag[:, cols] * ptx[:, cols]).astype(bf16)
    pr2[0, x] = pr2[1, x]
    cps = [
        send(pr2.at[1, x_at(k)], pr2.at[0, x], p2_s.at[k - 1], p2_r.at[k - 1], x_peer(k))
        for k in range(1, N_X)
    ]
    sums = [None, None]
    for b in range(N_X):
        cols = pl.ds(b * PAD, PAD)
        for j, other in enumerate((pt1, ptx)):
            t = tile_sum(other[:, cols] * pr2[1, b].astype(f32))
            sums[j] = t if sums[j] is None else sums[j] + t
    for j in range(2):
        arv[1, 0, 1 + j] = sums[j]
    wait_all(cps)
    own = pr2[0].reshape(TOK, PAD)
    arv[1, 0, 3] = tile_sum((dot(g_hi[...], own) + dot(g_lo[...], own)) * own.astype(f32))
    outs = [out_w]

    def image_two():
        turned = own.T
        for k in range(0, D, 512):
            k2[:, k : k + 512] = dot(turned, X[:, k : k + 512])[0:ROWS, :]
            if k == 2048:
                yield
        outs.append(pltpu.make_async_copy(k2, k2_hbm, out_sem.at[1]))
        outs[1].start()

    run(all_sum(1, 4), image_two())
    ww, sk, wk, kk = [jnp.sum(arv[1, 2, j], keepdims=True) / count for j in range(4)]
    sq1 = s1 * s1 * ww
    scale2 = lax.rsqrt(sq1 + norm_eps)
    s2 = scale2 * s1
    h12 = s1 * s2 * sk
    h22 = s2 * s2 * wk
    cross = s1 * s2 * (q - h11 * ss)
    sq2 = (
        s2 * s2 * kk
        - 2.0 * (h12 * h12 + h22 * h22)
        + h12 * h12 * (s1 * s1 * ss)
        + h22 * h22 * (s2 * s2 * ww)
        + 2.0 * h12 * h22 * cross
    )
    sq2 = jnp.maximum(sq2, 0.0)
    s3 = lax.rsqrt(sq2 + norm_eps)
    results = (h11, h12, h22, jnp.sqrt(sq1), jnp.sqrt(sq2), s2, s3 * s2, -s3 * h12 * s1, -s3 * h22 * s2)
    for j, value in enumerate(results):
        mix[j] = value[0, 0]
    for cp in outs:
        cp.wait()
    settle(0)


def combine(mix, kw_hbm, k2_hbm, start_hbm, basis_hbm, quot, coef, kw, k2, start, out, in_sem, out_sem):
    parts = [pl.ds(r, PIECE) for r in range(0, ROWS, PIECE)]
    ins = [
        [
            pltpu.make_async_copy(src.at[at], dst.at[at], in_sem.at[j, p])
            for j, (src, dst) in enumerate(((kw_hbm, kw), (k2_hbm, k2), (start_hbm, start)))
        ]
        for p, at in enumerate(parts)
    ]
    for cps in ins:
        for cp in cps:
            cp.start()
    quot[0] = mix[0]
    coef[0, 0] = mix[1]
    coef[0, 1] = mix[2]
    coef[1, 0] = mix[3]
    coef[1, 1] = mix[4]
    outs = []
    for p, at in enumerate(parts):
        for cp in ins[p]:
            cp.wait()
        w = kw[at, :]
        out[0, at, :] = mix[5] * w
        out[1, at, :] = mix[6] * k2[at, :] + mix[7] * start[at, :] + mix[8] * w
        for j in range(2):
            cp = pltpu.make_async_copy(out.at[j, at], basis_hbm.at[j, at], out_sem.at[j, p])
            cp.start()
            outs.append(cp)
    for cp in outs:
        cp.wait()


def per_device(hidden_in, targets, norm_gain, up_weight, down_weight, start):
    vm, dma = pltpu.VMEM, pltpu.SemaphoreType.DMA
    any_spec = pl.BlockSpec(memory_space=pl.ANY)
    smem_spec = pl.BlockSpec(memory_space=pltpu.SMEM)
    scratch = [
        vm((OWN, D), bf16),
        vm((OWN, D), bf16),
        vm((D,), f32),
        vm((HID, D), bf16),
        vm((HID, D), bf16),
        vm((ROWS, D), f32),
        vm((HID, D), bf16),
        vm((TOK, D), bf16),
        vm((CHUNKS, N_Z, OWN, W), bf16),
        vm((2, GRP, D), f32),
        vm((3, CHUNKS, 3, BLK, W), bf16),
        vm((3, CHUNKS, 3, BLK, W), bf16),
        vm((3, CHUNKS, 2, BLK, W), bf16),
        vm((3, CHUNKS, 2, BLK, W), bf16),
        vm((3, CHUNKS, 2, BLK, W), bf16),
        vm((3, CHUNKS, 2, BLK, W), bf16),
        vm((3, CHUNKS, N_Z, OWN, W), bf16),
        vm((3, CHUNKS, N_Z - 1, OWN, W), bf16),
        vm((3, CHUNKS, N_Z, OWN, W), bf16),
        vm((3, GRP, D), bf16),
        vm((GRP, HID), f32),
        vm((GRP, HID), f32),
        vm((GRP, HID), bf16),
        vm((2, GRP, HID), f32),
        vm((GRP, HID), f32),
        vm((GRP, HID), f32),
        vm((TOK, PAD), f32),
        vm((N_X, GRP, PAD), f32),
        vm((TOK, HID), bf16),
        vm((2, N_X, GRP, PAD), bf16),
        vm((TOK, TOK), bf16),
        vm((TOK, TOK), bf16),
        vm((ROWS, D), f32),
        vm((ROWS, D), f32),
        vm((2, 3, 4, 8, 128), f32),
        vm((2, 2, 15, 4, 8, 128), f32),
        vm((3, OWN, D), f32),
        vm((OWN, D), f32),
        dma((2 * N_X + 4,)),
    ]
    pairs = [
        (CHUNKS,), (CHUNKS, 6), (CHUNKS, 4),
        (2, 4), (2, 4), (2, 4), (4,), (12,), (4,), (N_X - 1,),
        (3, CHUNKS), (3, CHUNKS, 4), (3, CHUNKS, 2), (3, CHUNKS),
        (3, CHUNKS), (3, CHUNKS, 6), (3, CHUNKS, 4),
        (N_X - 1,), (N_X - 1,), (2, 2),
    ]
    for shape in pairs:
        scratch += [dma(shape), dma(shape)]
    scratch.append(dma((2,)))
    kw, k2, mix = pl.pallas_call(
        kernel,
        out_shape=(
            jax.ShapeDtypeStruct((ROWS, D), f32),
            jax.ShapeDtypeStruct((ROWS, D), f32),
            jax.ShapeDtypeStruct((9,), f32),
        ),
        in_specs=[any_spec] * 6,
        out_specs=(any_spec, any_spec, smem_spec),
        scratch_shapes=scratch,
        compiler_params=pltpu.CompilerParams(
            collective_id=0, has_side_effects=True, vmem_limit_bytes=60 * 1024 * 1024
        ),
        cost_estimate=pl.CostEstimate(flops=5 * 10**9, bytes_accessed=14 * 10**6, transcendentals=10**5),
    )(hidden_in, targets, norm_gain, up_weight, down_weight, start)
    pieces = ROWS // PIECE
    return pl.pallas_call(
        combine,
        out_shape=(
            jax.ShapeDtypeStruct((2, ROWS, D), f32),
            jax.ShapeDtypeStruct((1,), f32),
            jax.ShapeDtypeStruct((2, 2), f32),
        ),
        in_specs=[smem_spec, any_spec, any_spec, any_spec],
        out_specs=(any_spec, smem_spec, smem_spec),
        scratch_shapes=[
            vm((ROWS, D), f32),
            vm((ROWS, D), f32),
            vm((ROWS, D), f32),
            vm((2, ROWS, D), f32),
            dma((3, pieces)),
            dma((2, pieces)),
        ],
        compiler_params=pltpu.CompilerParams(vmem_limit_bytes=60 * 1024 * 1024),
        cost_estimate=pl.CostEstimate(flops=10**7, bytes_accessed=9 * 10**6, transcendentals=0),
    )(mix, kw, k2, start)


def solution(mesh):
    placed = (
        P(("dp", "zero"), None),
        P(("dp", "zero"), None),
        P(),
        P("zero", None),
        P("zero", None),
        P(("zero", "dp"), None),
    )
    return jax.shard_map(
        per_device,
        mesh=mesh,
        in_specs=placed,
        out_specs=(P(None, ("zero", "dp"), None), P(), P()),
        check_vma=False,
    )
```

```python
import jax
import jax.numpy as jnp
from jax import lax
from jax.experimental import pallas as pl
from jax.experimental.pallas import tpu as pltpu
from jax.sharding import PartitionSpec as P

MESH = pl.DeviceIdType.MESH
f32, bf16 = jnp.float32, jnp.bfloat16
norm_eps = 1e-06
gelu_coef = 0.7978845608028654

N_X, N_Y, N_Z, N_C = 4, 4, 8, 2
D = 4608
ROWS = 96
PAD = 128
HID = N_X * PAD
GRP = 128
TOK = N_X * GRP
HALF = GRP // N_C
BLK = HALF // N_Y
OWN = BLK // N_Z
CHUNKS = 2
W = D // CHUNKS
KEEP = 40
PIECE = 32


def gelu_value(inputs):
    return (
        0.5 * inputs * (1.0 + jnp.tanh(gelu_coef * (inputs + 0.044715 * inputs * inputs * inputs)))
    )


def gelu_parts(inputs):
    unit_dir = jnp.ones_like(inputs)

    def first_slope(points):
        return jax.jvp(gelu_value, (points,), (unit_dir,))[1]

    return (
        gelu_value(inputs),
        first_slope(inputs),
        jax.jvp(first_slope, (inputs,), (unit_dir,))[1],
    )


def loss_parts(summed, target, gain):
    r = lax.rsqrt(jnp.sum(summed * summed, axis=-1, keepdims=True) / D + norm_eps)
    normed = summed * r
    pull = (normed * gain - target) * gain
    mean = jnp.sum(pull * normed, axis=-1, keepdims=True) / D
    grad = r * (pull - normed * mean) / float(TOK)
    mix = gain * gain * normed + pull
    bias = jnp.sum(mix * normed, axis=-1, keepdims=True) / D
    scale = r * r * (gain * gain - mean) / float(TOK)
    along = -(scale * normed + r * grad)
    across = -r * normed / float(TOK)
    return grad, normed, mix, scale, along, across, r, bias


def dot_t(a, b):
    return lax.dot_general(a, b, (((1,), (1,)), ((), ())), preferred_element_type=f32)


def dot(a, b):
    return jnp.dot(a, b, preferred_element_type=f32)


def tile_sum(v):
    rows, cols = v.shape
    acc = v[0:8, :]
    for i in range(8, rows, 8):
        acc = acc + v[i : i + 8, :]
    out = acc[:, 0:128]
    for k in range(128, cols, 128):
        out = out + acc[:, k : k + 128]
    return out


def par(*gens):
    gens = list(gens)
    while gens:
        for g in list(gens):
            try:
                next(g)
            except StopIteration:
                gens.remove(g)
        if gens:
            yield


def run(*gens):
    for _ in par(*gens):
        pass


def play(gens, order):
    for j in order:
        next(gens[j], None)
    run(*gens)


def kernel(
    hin_hbm, tgt_hbm, gain_hbm, up_hbm, down_hbm, start_hbm,
    kw_hbm, k2_hbm, mix,
    hin, tgt, gain, up, down, start, dirs, X, xz, part,
    sb, rc, y1b, y1r, y2b, y2r, sz, rz, az, A,
    slope, bendag, hact, agrad, pt1, ptx,
    pfull, pr2, g_hi, g_lo, kw, k2, arv, arr, tot, bsum, lin,
    ld_sem, xz_s, xz_r, xy_s, xy_r, xc_s, xc_r,
    xa_s, xa_r, xac_s, xac_r, sx_s, sx_r,
    rc_s, rc_r, y1_s, y1_r, y2_s, y2_r, rz_s, rz_r,
    az_s, az_r, ay_s, ay_r, ac_s, ac_r,
    pf_s, pf_r, p2_s, p2_r, ar_s, ar_r, out_sem,
):
    x = lax.axis_index("dp")
    shard = lax.axis_index("zero")
    y, z, c = shard // 16, (shard // 2) % 8, shard % 2

    def dev(nx, ny, nz, nc):
        return (nx, ny * 16 + nz * 2 + nc)

    pending = []

    xs = [x] + [(x + k) % N_X for k in range(1, N_X)]
    ys = [y] + [(y + k) % N_Y for k in range(1, N_Y)]
    zs = [z] + [(z + k) % N_Z for k in range(1, N_Z)]

    def x_at(k):
        return xs[k % N_X]

    def y_at(k):
        return ys[k % N_Y]

    def x_peer(k):
        return dev(x_at(k), y, z, c)

    def y_peer(k):
        return dev(x, y_at(k), z, c)

    def z_peer(k):
        return dev(x, y, zs[k], c)

    c_peer = dev(x, y, z, 1 - c)

    def cross_peer(k):
        return dev(x, y_at(k), z, 1 - c)

    def xy_peer(k):
        return dev(x_at(k // N_Y), y_at(k % N_Y), z, c)

    def zc_peer(k):
        return dev(x, y, zs[k // N_C], c if k % N_C == 0 else 1 - c)

    def send(src, dst, ssem, rsem, to):
        cp = pltpu.make_async_remote_copy(
            src_ref=src, dst_ref=dst, send_sem=ssem, recv_sem=rsem, device_id=to, device_id_type=MESH
        )
        cp.start()
        pending.append(cp)
        return cp

    def send_all(copies, bytes_of, ssem, rsem):
        for src, dst, to in copies:
            pltpu.make_async_remote_copy(
                src_ref=src, dst_ref=dst, send_sem=ssem, recv_sem=rsem, device_id=to, device_id_type=MESH
            ).start()
        cp = pltpu.make_async_remote_copy(
            src_ref=bytes_of,
            dst_ref=bytes_of,
            send_sem=ssem,
            recv_sem=rsem,
            device_id=c_peer,
            device_id_type=MESH,
        )
        pending.append(cp)
        return [cp]

    def settle(keep=KEEP):
        while len(pending) > keep:
            pending.pop(0).wait_send()

    def rows(start_row, count):
        return pl.ds(pl.multiple_of(start_row, 16), count)

    def wait_all(cps):
        settle()
        for cp in cps:
            cp.wait_recv()

    small = [
        pltpu.make_async_copy(src, dst, ld_sem.at[2 * N_X + 1 + j])
        for j, (src, dst) in enumerate(((hin_hbm, hin), (tgt_hbm, tgt), (gain_hbm, gain)))
    ]
    for cp in small:
        cp.start()
    loads = []
    for b in range(N_X):
        for j, (src, dst) in enumerate(((up_hbm, up), (down_hbm, down))):
            loads.append(
                pltpu.make_async_copy(
                    src.at[pl.ds(b * ROWS, ROWS)], dst.at[pl.ds(b * PAD, ROWS)], ld_sem.at[2 * b + j]
                )
            )
    loads.append(pltpu.make_async_copy(start_hbm, start, ld_sem.at[2 * N_X]))
    for cp in loads:
        cp.start()

    barrier = pltpu.get_barrier_semaphore()
    peers = [xy_peer(k) for k in range(1, N_X * N_Y)] + [zc_peer(k) for k in range(1, N_Z * N_C)]
    peers += [cross_peer(1), cross_peer(-1)]
    for p in peers:
        pl.semaphore_signal(barrier, inc=1, device_id=p, device_id_type=MESH)
    pl.semaphore_wait(barrier, len(peers))
    for cp in small:
        cp.wait()

    def ring_gather(ref, blocks, c0, w, peer, ssem, rsem, then=None, cross=None):
        half = w // 2
        nb = len(blocks)
        first = []
        for b, (row_of, count) in enumerate(blocks):
            at = (rows(row_of(0), count), pl.ds(c0, w))
            first.append(
                [
                    send(ref.at[at], ref.at[at], ssem.at[2 * b + j], rsem.at[2 * b + j], peer(to))
                    for j, to in enumerate((1, -1))
                ]
            )
        if then:
            then(0)
        yield
        second = []
        for b, (row_of, count) in enumerate(blocks):
            for j, to in enumerate((1, -1)):
                wait_all([first[b][j]])
                at = (rows(row_of(-to), count), pl.ds(c0 + j * half, half))
                i = 2 * (nb + b) + j
                second.append(send(ref.at[at], ref.at[at], ssem.at[i], rsem.at[i], peer(to)))
                if cross:
                    second.append(send(ref.at[at], ref.at[at], ssem.at[i + 2], rsem.at[i + 2], cross(to)))
        if then:
            then(-1)
            then(1)
        yield
        wait_all(second)
        if then:
            then(2)

    def gather_z(own, buf, ssem, rsem):
        buf[z] = own
        copies = [(buf.at[z], buf.at[z], z_peer(k)) for k in range(1, N_Z)]
        return send_all(copies, buf.at[pl.ds(0, N_Z - 1)], ssem, rsem)

    def join16(buf):
        return buf[...].reshape(BLK, W)

    def gather(own, i, h):
        c0, out = h * W, A.at[i]
        cols = pl.ds(c0, W)
        cps = gather_z(own(slice(c0, c0 + W)), az.at[i, h], az_s.at[i, h], az_r.at[i, h])
        yield
        wait_all(cps)
        out[rows(c * HALF + y * BLK, BLK), cols] = join16(az.at[i, h])
        passed = []

        def pass_on(k):
            if k != 2 or i == 0:
                at = (rows(c * HALF + y_at(k) * BLK, BLK), cols)
                passed.append(send(out.at[at], out.at[at], ac_s.at[i, h, k % 4], ac_r.at[i, h, k % 4], c_peer))

        yield from ring_gather(
            out,
            [(lambda k: c * HALF + y_at(k) * BLK, BLK)],
            c0,
            W,
            y_peer,
            ay_s.at[i, h],
            ay_r.at[i, h],
            pass_on,
            cross_peer if i else None,
        )
        if i == 0:
            yield
        wait_all(passed)
        part_grad = dot_t(out[:, cols], down[:, cols])
        if h == 0:
            agrad[i % 2] = part_grad
        else:
            agrad[i % 2] = agrad[i % 2] + part_grad

    def scatter(i, h, make):
        c0 = h * W
        cols = slice(c0, c0 + W)
        make(i, h)
        buf = part.at[i % 2]

        def mine(k):
            return buf[rows(c * HALF + y_at(k) * BLK, BLK), cols]

        def other(k):
            return buf[rows((1 - c) * HALF + y_at(k) * BLK, BLK), cols]

        half = W // 2
        y1b[i, h, 0] = mine(2).astype(bf16)
        y1b[i, h, 1] = other(2).astype(bf16)
        cps = [
            send(
                y1b.at[i, h, p, :, pl.ds(j * half, half)],
                y1r.at[i, h, p, :, pl.ds(j * half, half)],
                y1_s.at[i, h, 2 * p + j],
                y1_r.at[i, h, 2 * p + j],
                peer(to),
            )
            for p, peer in enumerate((y_peer, cross_peer))
            for j, to in enumerate((1, -1))
        ]
        for n, k in enumerate((0, 1, -1)):
            sb[i, h, n] = other(k).astype(bf16)
        cps.append(send(sb.at[i, h], rc.at[i, h], rc_s.at[i, h], rc_r.at[i, h], c_peer))
        yield
        wait_all(cps)
        got = y1r[i, h, 0].astype(f32) + y1r[i, h, 1].astype(f32)
        for j, to in enumerate((1, -1)):
            both_cores = mine(to) + rc[i, h, 1 + j].astype(f32)
            for p in range(2):
                at = slice(p * half, (p + 1) * half)
                piece = both_cores[:, at] + got[:, at] if p == j else both_cores[:, at]
                y2b[i, h, j, :, at] = piece.astype(bf16)
        cps = [
            send(y2b.at[i, h, j], y2r.at[i, h, j], y2_s.at[i, h, j], y2_r.at[i, h, j], y_peer(to))
            for j, to in enumerate((1, -1))
        ]
        yield
        wait_all(cps)
        total = mine(0) + rc[i, h, 0].astype(f32) + y2r[i, h, 0].astype(f32) + y2r[i, h, 1].astype(f32)
        sz[i, h] = total.astype(bf16).reshape(N_Z, OWN, W)
        copies = [(sz.at[i, h, zs[k]], rz.at[i, h, k - 1], z_peer(k)) for k in range(1, N_Z)]
        cps = send_all(copies, rz.at[i, h], rz_s.at[i, h], rz_r.at[i, h])
        yield
        wait_all(cps)
        s3 = sz[i, h, z].astype(f32)
        for k in range(N_Z - 1):
            s3 = s3 + rz[i, h, k].astype(f32)
        tot[i, :, cols] = s3
        if i > 0:
            inner = [jnp.sum(lin[j, :, cols] * s3, axis=-1, keepdims=True) for j in range(2)]
            inners[i] = inner if h == 0 else [p + q for p, q in zip(inners[i], inner)]

    inners = [None, None, None]

    def scatters(i, make):
        return par(*[scatter(i, h, make) for h in range(CHUNKS)])

    def gathers(own, i):
        return par(*[gather(own, i, h) for h in range(CHUNKS)])

    def all_sum(i, n):
        for s, peer in enumerate((xy_peer, zc_peer)):
            copies = [
                (arv.at[i, s, pl.ds(0, n)], arr.at[i, s, k - 1, pl.ds(0, n)], peer(k)) for k in range(1, 16)
            ]
            cps = send_all(copies, arr.at[i, s, :, pl.ds(0, n)], ar_s.at[i, s], ar_r.at[i, s])
            yield
            wait_all(cps)
            acc = arv[i, s, 0:n]
            for k in range(1, 16):
                acc = acc + arr[i, s, k - 1, 0:n]
            arv[i, s + 1, 0:n] = acc

    group = rows(x * GRP, GRP)

    def group_tokens(h):
        c0 = h * W
        cols = pl.ds(c0, W)
        cps = gather_z(hin[:, c0 : c0 + W], xz.at[h], xz_s.at[h], xz_r.at[h])
        yield
        wait_all(cps)
        X[rows(x * GRP + c * HALF + y * BLK, BLK), cols] = join16(xz.at[h])
        passed = []

        def pass_on(k):
            if k != 2:
                at = (rows(x * GRP + c * HALF + y_at(k) * BLK, BLK), cols)
                passed.append(send(X.at[at], X.at[at], xc_s.at[h, k % 4], xc_r.at[h, k % 4], c_peer))

        yield from ring_gather(
            X,
            [(lambda k: x * GRP + c * HALF + y_at(k) * BLK, BLK)],
            c0,
            W,
            y_peer,
            xy_s.at[h],
            xy_r.at[h],
            pass_on,
            cross_peer,
        )
        wait_all(passed)
        pre = dot_t(X[group, cols], up[:, cols])
        if h == 0:
            agrad[0] = pre
        else:
            agrad[0] = agrad[0] + pre

    def accumulate_pt1(h, k):
        cols = pl.ds(h * W, W)
        block = rows(x_at(k) * PAD, PAD)
        lanes = pl.ds(pl.multiple_of(x_at(k) * PAD, PAD), PAD)
        term = dot_t(X[group, cols], dirs[block, cols])
        if h == 0:
            pt1[:, lanes] = term
        else:
            pt1[:, lanes] = pt1[:, lanes] + term

    def start_rows(h):
        ring = ring_gather(
            dirs, [(lambda k: x_at(k) * PAD, ROWS)], h * W, W, x_peer, sx_s.at[h], sx_r.at[h]
        )
        next(ring)
        yield
        next(ring)
        yield
        for k in (0, -1, 1):
            accumulate_pt1(h, k)
        yield
        run(ring)
        accumulate_pt1(h, 2)

    def other_tokens(h):
        cols = pl.ds(h * W, W)
        passed = []

        def pass_on(k):
            if k != 0:
                at = (rows(x_at(k) * GRP + c * HALF, HALF), cols)
                passed.append(send(X.at[at], X.at[at], xac_s.at[h, k % 4], xac_r.at[h, k % 4], c_peer))

        yield from ring_gather(
            X, [(lambda k: x_at(k) * GRP + c * HALF, HALF)], h * W, W, x_peer, xa_s.at[h], xa_r.at[h], pass_on
        )
        yield
        wait_all(passed)

    def local_work():
        loads[-1].wait()
        dirs[rows(x * PAD, ROWS), :] = start[...].astype(bf16)
        for g in s_gens:
            next(g)
        for b in range(N_X):
            pad = pl.ds(b * PAD + ROWS, PAD - ROWS)
            up[pad, :] = jnp.zeros((PAD - ROWS, D), bf16)
            down[pad, :] = jnp.zeros((PAD - ROWS, D), bf16)
            dirs[pad, :] = jnp.zeros((PAD - ROWS, D), bf16)
        yield
        for cp in loads[:-1]:
            cp.wait()
        arv[0, 0, 1] = tile_sum(start[...] * start[...])

    s_gens = [start_rows(h) for h in range(CHUNKS)]
    both = list(range(CHUNKS))
    n = CHUNKS
    play([group_tokens(h) for h in range(CHUNKS)] + [local_work()], both + [n] + both + [n] + both + both)

    def to_branch(i, h):
        for k in range(h * W, (h + 1) * W, W // 3):
            part[i % 2, :, k : k + W // 3] = dot(hact[...], down[:, k : k + W // 3])

    def weights():
        return tgt[...].astype(f32), gain[...]

    state = []

    def loss_curv(tangent, inner):
        r, bias = state
        a = inner[0] / D
        d = r * (inner[1] / D - a * bias)
        return lambda at: (lin[2, :, at] * tangent(at) + a * lin[3, :, at] + d * lin[4, :, at]).astype(bf16)

    def forward():
        for b in range(N_X):
            cols = pl.ds(b * PAD, PAD)
            value, first, second = gelu_parts(agrad[0, :, cols])
            hact[:, cols] = value.astype(bf16)
            slope[:, cols] = first
            bendag[:, cols] = second
        yield from scatters(0, to_branch)
        bsum[...] = hin[...].astype(f32) + tot[0]
        parts = loss_parts(bsum[...], *weights())
        for j in range(5):
            lin[j] = parts[1 + j]
        state.extend(parts[6:])
        grad = parts[0].astype(bf16)
        yield from gathers(lambda at: grad[:, at], 0)
        bendag[...] = bendag[...] * agrad[0]

    def first_tangent():
        hact[...] = (slope[...] * pt1[...]).astype(bf16)
        yield from scatters(1, to_branch)

    fwd = forward()
    others = [other_tokens(h) for h in range(CHUNKS)]
    for g in [s_gens[0], fwd] + s_gens[1:] + s_gens + [fwd, fwd] + s_gens:
        next(g, None)
    tangent = first_tangent()
    for g in [tangent, fwd] + others:
        next(g, None)
    run(tangent, fwd)
    curv = loss_curv(lambda at: tot[1, :, at], inners[1])

    def token_gram(k):
        mine = rows(x_at(k) * GRP, GRP)
        g = dot_t(X[mine, :], X[...])
        hi = g.astype(bf16)
        g_hi[mine, :] = hi
        g_lo[mine, :] = (g - hi.astype(f32)).astype(bf16)

    grads = gathers(curv, 1)
    for g in [grads] + others + [grads] + others + [grads] + others + [grads]:
        next(g, None)
    token_gram(0)
    run(grads)
    p1 = agrad[1] * slope[...] + bendag[...] * pt1[...]
    pfull[group, :] = p1.astype(bf16)

    def share_p1():
        def use(k):
            block = rows(x_at(k) * GRP, GRP)
            term = dot(g_hi[group, block], pfull[block, :]) + dot(g_lo[group, block], pfull[block, :])
            if k == 0:
                ptx[...] = term
            else:
                ptx[...] = ptx[...] + term

        cps = [
            send(pfull.at[group], pfull.at[group], pf_s.at[k - 1], pf_r.at[k - 1], x_peer(k))
            for k in range(1, N_X)
        ]
        use(0)
        yield
        for k in (1, 3, 2):
            wait_all([cps[k - 1]])
            use(N_X - k)

    def own_sums():
        arv[0, 0, 0] = tile_sum(p1 * pt1[...])
        yield

    run(share_p1(), own_sums())

    hact[...] = (slope[...] * ptx[...]).astype(bf16)

    def image_one():
        own = pfull[:, pl.ds(pl.multiple_of(x * PAD, PAD), PAD)].T
        for k in range(0, D, 512):
            kw[:, k : k + 512] = dot(own, X[:, k : k + 512])[0:ROWS, :]
            if k % 1536 == 1024:
                yield

    run(scatters(2, to_branch), all_sum(0, 2), image_one())
    count = float(ROWS * 256 * D)
    q = jnp.sum(arv[0, 2, 0], keepdims=True) / count
    ss = jnp.sum(arv[0, 2, 1], keepdims=True) / count
    s1 = lax.rsqrt(ss + norm_eps)
    h11 = s1 * s1 * q
    curv = loss_curv(
        lambda at: tot[2, :, at] - h11 * tot[1, :, at], [p - h11 * q for p, q in zip(inners[2], inners[1])]
    )

    def remainder():
        ptx[...] = ptx[...] - h11 * pt1[...]
        acc = None
        for k in range(0, D, 1536):
            w = kw[:, k : k + 1536] - h11 * start[:, k : k + 1536]
            kw[:, k : k + 1536] = w
            s = tile_sum(w * w)
            acc = s if acc is None else acc + s
            token_gram(k // 1536 + 1)
            yield
        arv[1, 0, 0] = acc

    run(gathers(curv, 2), remainder())
    out_w = pltpu.make_async_copy(kw, kw_hbm, out_sem.at[0])
    out_w.start()
    for b in range(N_X):
        cols = pl.ds(b * PAD, PAD)
        pr2[1, b] = (agrad[0, :, cols] * slope[:, cols] + bendag[:, cols] * ptx[:, cols]).astype(bf16)
    pr2[0, x] = pr2[1, x]
    cps = [
        send(pr2.at[1, x_at(k)], pr2.at[0, x], p2_s.at[k - 1], p2_r.at[k - 1], x_peer(k))
        for k in range(1, N_X)
    ]
    sums = [None, None]
    for b in range(N_X):
        cols = pl.ds(b * PAD, PAD)
        for j, other in enumerate((pt1, ptx)):
            t = tile_sum(other[:, cols] * pr2[1, b].astype(f32))
            sums[j] = t if sums[j] is None else sums[j] + t
    for j in range(2):
        arv[1, 0, 1 + j] = sums[j]
    wait_all(cps)
    own = pr2[0].reshape(TOK, PAD)
    arv[1, 0, 3] = tile_sum((dot(g_hi[...], own) + dot(g_lo[...], own)) * own.astype(f32))
    outs = [out_w]

    def image_two():
        turned = own.T
        for k in range(0, D, 512):
            k2[:, k : k + 512] = dot(turned, X[:, k : k + 512])[0:ROWS, :]
            if k == 2048:
                yield
        outs.append(pltpu.make_async_copy(k2, k2_hbm, out_sem.at[1]))
        outs[1].start()

    run(all_sum(1, 4), image_two())
    ww, sk, wk, kk = [jnp.sum(arv[1, 2, j], keepdims=True) / count for j in range(4)]
    sq1 = s1 * s1 * ww
    scale2 = lax.rsqrt(sq1 + norm_eps)
    s2 = scale2 * s1
    h12 = s1 * s2 * sk
    h22 = s2 * s2 * wk
    cross = s1 * s2 * (q - h11 * ss)
    sq2 = (
        s2 * s2 * kk
        - 2.0 * (h12 * h12 + h22 * h22)
        + h12 * h12 * (s1 * s1 * ss)
        + h22 * h22 * (s2 * s2 * ww)
        + 2.0 * h12 * h22 * cross
    )
    sq2 = jnp.maximum(sq2, 0.0)
    s3 = lax.rsqrt(sq2 + norm_eps)
    results = (h11, h12, h22, jnp.sqrt(sq1), jnp.sqrt(sq2), s2, s3 * s2, -s3 * h12 * s1, -s3 * h22 * s2)
    for j, value in enumerate(results):
        mix[j] = value[0, 0]
    for cp in outs:
        cp.wait()
    settle(0)


def combine(mix, kw_hbm, k2_hbm, start_hbm, basis_hbm, quot, coef, kw, k2, start, out, in_sem, out_sem):
    parts = [pl.ds(r, PIECE) for r in range(0, ROWS, PIECE)]
    ins = [
        [
            pltpu.make_async_copy(src.at[at], dst.at[at], in_sem.at[j, p])
            for j, (src, dst) in enumerate(((kw_hbm, kw), (k2_hbm, k2), (start_hbm, start)))
        ]
        for p, at in enumerate(parts)
    ]
    for cps in ins:
        for cp in cps:
            cp.start()
    quot[0] = mix[0]
    coef[0, 0] = mix[1]
    coef[0, 1] = mix[2]
    coef[1, 0] = mix[3]
    coef[1, 1] = mix[4]
    outs = []
    for p, at in enumerate(parts):
        for cp in ins[p]:
            cp.wait()
        w = kw[at, :]
        out[0, at, :] = mix[5] * w
        out[1, at, :] = mix[6] * k2[at, :] + mix[7] * start[at, :] + mix[8] * w
        for j in range(2):
            cp = pltpu.make_async_copy(out.at[j, at], basis_hbm.at[j, at], out_sem.at[j, p])
            cp.start()
            outs.append(cp)
    for cp in outs:
        cp.wait()


def per_device(hidden_in, targets, norm_gain, up_weight, down_weight, start):
    vm, dma = pltpu.VMEM, pltpu.SemaphoreType.DMA
    any_spec = pl.BlockSpec(memory_space=pl.ANY)
    smem_spec = pl.BlockSpec(memory_space=pltpu.SMEM)
    scratch = [
        vm((OWN, D), bf16),
        vm((OWN, D), bf16),
        vm((D,), f32),
        vm((HID, D), bf16),
        vm((HID, D), bf16),
        vm((ROWS, D), f32),
        vm((HID, D), bf16),
        vm((TOK, D), bf16),
        vm((CHUNKS, N_Z, OWN, W), bf16),
        vm((2, GRP, D), f32),
        vm((3, CHUNKS, 3, BLK, W), bf16),
        vm((3, CHUNKS, 3, BLK, W), bf16),
        vm((3, CHUNKS, 2, BLK, W), bf16),
        vm((3, CHUNKS, 2, BLK, W), bf16),
        vm((3, CHUNKS, 2, BLK, W), bf16),
        vm((3, CHUNKS, 2, BLK, W), bf16),
        vm((3, CHUNKS, N_Z, OWN, W), bf16),
        vm((3, CHUNKS, N_Z - 1, OWN, W), bf16),
        vm((3, CHUNKS, N_Z, OWN, W), bf16),
        vm((3, GRP, D), bf16),
        vm((GRP, HID), f32),
        vm((GRP, HID), f32),
        vm((GRP, HID), bf16),
        vm((2, GRP, HID), f32),
        vm((GRP, HID), f32),
        vm((GRP, HID), f32),
        vm((TOK, HID), bf16),
        vm((2, N_X, GRP, PAD), bf16),
        vm((TOK, TOK), bf16),
        vm((TOK, TOK), bf16),
        vm((ROWS, D), f32),
        vm((ROWS, D), f32),
        vm((2, 3, 4, 8, 128), f32),
        vm((2, 2, 15, 4, 8, 128), f32),
        vm((3, OWN, D), f32),
        vm((OWN, D), f32),
        vm((5, OWN, D), f32),
        dma((2 * N_X + 4,)),
    ]
    pairs = [
        (CHUNKS,), (CHUNKS, 6), (CHUNKS, 4),
        (CHUNKS, 4), (CHUNKS, 4), (CHUNKS, 4),
        (3, CHUNKS), (3, CHUNKS, 4), (3, CHUNKS, 2), (3, CHUNKS),
        (3, CHUNKS), (3, CHUNKS, 6), (3, CHUNKS, 4),
        (N_X - 1,), (N_X - 1,), (2, 2),
    ]
    for shape in pairs:
        scratch += [dma(shape), dma(shape)]
    scratch.append(dma((2,)))
    kw, k2, mix = pl.pallas_call(
        kernel,
        out_shape=(
            jax.ShapeDtypeStruct((ROWS, D), f32),
            jax.ShapeDtypeStruct((ROWS, D), f32),
            jax.ShapeDtypeStruct((9,), f32),
        ),
        in_specs=[any_spec] * 6,
        out_specs=(any_spec, any_spec, smem_spec),
        scratch_shapes=scratch,
        compiler_params=pltpu.CompilerParams(
            collective_id=0, has_side_effects=True, vmem_limit_bytes=60 * 1024 * 1024
        ),
        cost_estimate=pl.CostEstimate(flops=5 * 10**9, bytes_accessed=14 * 10**6, transcendentals=10**5),
    )(hidden_in, targets, norm_gain, up_weight, down_weight, start)
    pieces = ROWS // PIECE
    return pl.pallas_call(
        combine,
        out_shape=(
            jax.ShapeDtypeStruct((2, ROWS, D), f32),
            jax.ShapeDtypeStruct((1,), f32),
            jax.ShapeDtypeStruct((2, 2), f32),
        ),
        in_specs=[smem_spec, any_spec, any_spec, any_spec],
        out_specs=(any_spec, smem_spec, smem_spec),
        scratch_shapes=[
            vm((ROWS, D), f32),
            vm((ROWS, D), f32),
            vm((ROWS, D), f32),
            vm((2, ROWS, D), f32),
            dma((3, pieces)),
            dma((2, pieces)),
        ],
        compiler_params=pltpu.CompilerParams(vmem_limit_bytes=60 * 1024 * 1024),
        cost_estimate=pl.CostEstimate(flops=10**7, bytes_accessed=9 * 10**6, transcendentals=0),
    )(mix, kw, k2, start)


def solution(mesh):
    placed = (
        P(("dp", "zero"), None),
        P(("dp", "zero"), None),
        P(),
        P("zero", None),
        P("zero", None),
        P(("zero", "dp"), None),
    )
    return jax.shard_map(
        per_device,
        mesh=mesh,
        in_specs=placed,
        out_specs=(P(None, ("zero", "dp"), None), P(), P()),
        check_vma=False,
    )
```

```python
import jax
import jax.numpy as jnp
from jax import lax
from jax.experimental import pallas as pl
from jax.experimental.pallas import tpu as pltpu
from jax.sharding import PartitionSpec as P

MESH = pl.DeviceIdType.MESH
f32, bf16 = jnp.float32, jnp.bfloat16
norm_eps = 1e-06
gelu_coef = 0.7978845608028654

N_X, N_Y, N_Z, N_C = 4, 4, 8, 2
D = 4608
ROWS = 96
PAD = 128
HID = N_X * PAD
GRP = 128
TOK = N_X * GRP
HALF = GRP // N_C
BLK = HALF // N_Y
OWN = BLK // N_Z
CHUNKS = 2
W = D // CHUNKS
KEEP = 40
PIECE = 32


def gelu_value(inputs):
    return (
        0.5 * inputs * (1.0 + jnp.tanh(gelu_coef * (inputs + 0.044715 * inputs * inputs * inputs)))
    )


def gelu_parts(inputs):
    unit_dir = jnp.ones_like(inputs)

    def first_slope(points):
        return jax.jvp(gelu_value, (points,), (unit_dir,))[1]

    return (
        gelu_value(inputs),
        first_slope(inputs),
        jax.jvp(first_slope, (inputs,), (unit_dir,))[1],
    )


def loss_parts(summed, target, gain):
    r = lax.rsqrt(jnp.sum(summed * summed, axis=-1, keepdims=True) / D + norm_eps)
    normed = summed * r
    pull = (normed * gain - target) * gain
    mean = jnp.sum(pull * normed, axis=-1, keepdims=True) / D
    grad = r * (pull - normed * mean) / float(TOK)
    mix = gain * gain * normed + pull
    bias = jnp.sum(mix * normed, axis=-1, keepdims=True) / D
    scale = r * r * (gain * gain - mean) / float(TOK)
    along = -(scale * normed + r * grad)
    across = -r * normed / float(TOK)
    return grad, normed, mix, scale, along, across, r, bias


def dot_t(a, b):
    return lax.dot_general(a, b, (((1,), (1,)), ((), ())), preferred_element_type=f32)


def dot(a, b):
    return jnp.dot(a, b, preferred_element_type=f32)


def tile_sum(v):
    rows, cols = v.shape
    acc = v[0:8, :]
    for i in range(8, rows, 8):
        acc = acc + v[i : i + 8, :]
    out = acc[:, 0:128]
    for k in range(128, cols, 128):
        out = out + acc[:, k : k + 128]
    return out


def par(*gens):
    gens = list(gens)
    while gens:
        for g in list(gens):
            try:
                next(g)
            except StopIteration:
                gens.remove(g)
        if gens:
            yield


def loop(count, body):
    def step(k, carry):
        body(k)
        return carry

    lax.fori_loop(0, count, step, 0)


def span(k, size):
    return pl.ds(pl.multiple_of(k * size, size), size)


def run(*gens):
    for _ in par(*gens):
        pass


def play(gens, order):
    for j in order:
        next(gens[j], None)
    run(*gens)


def kernel(
    hin_hbm, tgt_hbm, gain_hbm, up_hbm, down_hbm, start_hbm,
    kw_hbm, k2_hbm, mix,
    hin, tgt, gain, up, down, start, dirs, X, xz, part,
    sb, rc, y1b, y1r, y2b, y2r, sz, rz, az, A,
    slope, bendag, hact, agrad, pt1, ptx,
    pfull, pr2, g_hi, g_lo, kw, k2, arv, arr, tot, bsum, lin,
    ld_sem, xz_s, xz_r, xy_s, xy_r, xc_s, xc_r,
    xa_s, xa_r, xac_s, xac_r, sx_s, sx_r,
    rc_s, rc_r, y1_s, y1_r, y2_s, y2_r, rz_s, rz_r,
    az_s, az_r, ay_s, ay_r, ac_s, ac_r,
    pf_s, pf_r, p2_s, p2_r, ar_s, ar_r, out_sem,
):
    x = lax.axis_index("dp")
    shard = lax.axis_index("zero")
    y, z, c = shard // 16, (shard // 2) % 8, shard % 2

    def dev(nx, ny, nz, nc):
        return (nx, ny * 16 + nz * 2 + nc)

    pending = []

    xs = [x] + [(x + k) % N_X for k in range(1, N_X)]
    ys = [y] + [(y + k) % N_Y for k in range(1, N_Y)]
    zs = [z] + [(z + k) % N_Z for k in range(1, N_Z)]

    def x_at(k):
        return xs[k % N_X]

    def y_at(k):
        return ys[k % N_Y]

    def x_peer(k):
        return dev(x_at(k), y, z, c)

    def y_peer(k):
        return dev(x, y_at(k), z, c)

    def z_peer(k):
        return dev(x, y, zs[k], c)

    c_peer = dev(x, y, z, 1 - c)

    def cross_peer(k):
        return dev(x, y_at(k), z, 1 - c)

    def xy_peer(k):
        return dev(x_at(k // N_Y), y_at(k % N_Y), z, c)

    def zc_peer(k):
        return dev(x, y, zs[k // N_C], c if k % N_C == 0 else 1 - c)

    def send(src, dst, ssem, rsem, to):
        cp = pltpu.make_async_remote_copy(
            src_ref=src, dst_ref=dst, send_sem=ssem, recv_sem=rsem, device_id=to, device_id_type=MESH
        )
        cp.start()
        pending.append(cp)
        return cp

    def send_all(copies, bytes_of, ssem, rsem):
        for src, dst, to in copies:
            pltpu.make_async_remote_copy(
                src_ref=src, dst_ref=dst, send_sem=ssem, recv_sem=rsem, device_id=to, device_id_type=MESH
            ).start()
        cp = pltpu.make_async_remote_copy(
            src_ref=bytes_of,
            dst_ref=bytes_of,
            send_sem=ssem,
            recv_sem=rsem,
            device_id=c_peer,
            device_id_type=MESH,
        )
        pending.append(cp)
        return [cp]

    def settle(keep=KEEP):
        while len(pending) > keep:
            pending.pop(0).wait_send()

    def rows(start_row, count):
        return pl.ds(pl.multiple_of(start_row, 16), count)

    def wait_all(cps):
        settle()
        for cp in cps:
            cp.wait_recv()

    small = [
        pltpu.make_async_copy(src, dst, ld_sem.at[2 * N_X + 1 + j])
        for j, (src, dst) in enumerate(((hin_hbm, hin), (tgt_hbm, tgt), (gain_hbm, gain)))
    ]
    for cp in small:
        cp.start()
    loads = []
    for b in range(N_X):
        for j, (src, dst) in enumerate(((up_hbm, up), (down_hbm, down))):
            loads.append(
                pltpu.make_async_copy(
                    src.at[pl.ds(b * ROWS, ROWS)], dst.at[pl.ds(b * PAD, ROWS)], ld_sem.at[2 * b + j]
                )
            )
    loads.append(pltpu.make_async_copy(start_hbm, start, ld_sem.at[2 * N_X]))
    for cp in loads:
        cp.start()

    barrier = pltpu.get_barrier_semaphore()
    peers = [xy_peer(k) for k in range(1, N_X * N_Y)] + [zc_peer(k) for k in range(1, N_Z * N_C)]
    peers += [cross_peer(1), cross_peer(-1)]
    for p in peers:
        pl.semaphore_signal(barrier, inc=1, device_id=p, device_id_type=MESH)
    pl.semaphore_wait(barrier, len(peers))
    for cp in small:
        cp.wait()

    def ring_gather(ref, blocks, c0, w, peer, ssem, rsem, then=None, cross=None):
        half = w // 2
        nb = len(blocks)
        first = []
        for b, (row_of, count) in enumerate(blocks):
            at = (rows(row_of(0), count), pl.ds(c0, w))
            first.append(
                [
                    send(ref.at[at], ref.at[at], ssem.at[2 * b + j], rsem.at[2 * b + j], peer(to))
                    for j, to in enumerate((1, -1))
                ]
            )
        if then:
            then(0)
        yield
        second = []
        for b, (row_of, count) in enumerate(blocks):
            for j, to in enumerate((1, -1)):
                wait_all([first[b][j]])
                at = (rows(row_of(-to), count), pl.ds(c0 + j * half, half))
                i = 2 * (nb + b) + j
                second.append(send(ref.at[at], ref.at[at], ssem.at[i], rsem.at[i], peer(to)))
                if cross:
                    second.append(send(ref.at[at], ref.at[at], ssem.at[i + 2], rsem.at[i + 2], cross(to)))
        if then:
            then(-1)
            then(1)
        yield
        wait_all(second)
        if then:
            then(2)

    def gather_z(own, buf, ssem, rsem):
        buf[z] = own
        copies = [(buf.at[z], buf.at[z], z_peer(k)) for k in range(1, N_Z)]
        return send_all(copies, buf.at[pl.ds(0, N_Z - 1)], ssem, rsem)

    def join16(buf):
        return buf[...].reshape(BLK, W)

    def by_hidden(tokens, weight, cols, out, fresh):
        def body(k):
            hid = span(k, 2 * PAD)
            term = dot_t(tokens, weight[hid, cols])
            out[:, hid] = term if fresh else out[:, hid] + term

        loop(HID // (2 * PAD), body)

    def gather(own, i, h):
        c0, out = h * W, A.at[i]
        cols = pl.ds(c0, W)
        cps = gather_z(own(slice(c0, c0 + W)), az.at[i, h], az_s.at[i, h], az_r.at[i, h])
        yield
        wait_all(cps)
        out[rows(c * HALF + y * BLK, BLK), cols] = join16(az.at[i, h])
        passed = []

        def pass_on(k):
            if k != 2 or i == 0:
                at = (rows(c * HALF + y_at(k) * BLK, BLK), cols)
                passed.append(send(out.at[at], out.at[at], ac_s.at[i, h, k % 4], ac_r.at[i, h, k % 4], c_peer))

        yield from ring_gather(
            out,
            [(lambda k: c * HALF + y_at(k) * BLK, BLK)],
            c0,
            W,
            y_peer,
            ay_s.at[i, h],
            ay_r.at[i, h],
            pass_on,
            cross_peer if i else None,
        )
        if i == 0:
            yield
        wait_all(passed)
        by_hidden(out[:, cols], down, cols, agrad.at[i % 2], h == 0)

    def scatter(i, h, make):
        c0 = h * W
        cols = slice(c0, c0 + W)
        make(i, h)
        buf = part.at[i % 2]

        def mine(k):
            return buf[rows(c * HALF + y_at(k) * BLK, BLK), cols]

        def other(k):
            return buf[rows((1 - c) * HALF + y_at(k) * BLK, BLK), cols]

        half = W // 2
        y1b[i, h, 0] = mine(2).astype(bf16)
        y1b[i, h, 1] = other(2).astype(bf16)
        cps = [
            send(
                y1b.at[i, h, p, :, pl.ds(j * half, half)],
                y1r.at[i, h, p, :, pl.ds(j * half, half)],
                y1_s.at[i, h, 2 * p + j],
                y1_r.at[i, h, 2 * p + j],
                peer(to),
            )
            for p, peer in enumerate((y_peer, cross_peer))
            for j, to in enumerate((1, -1))
        ]
        for n, k in enumerate((0, 1, -1)):
            sb[i, h, n] = other(k).astype(bf16)
        cps.append(send(sb.at[i, h], rc.at[i, h], rc_s.at[i, h], rc_r.at[i, h], c_peer))
        yield
        wait_all(cps)
        got = y1r[i, h, 0].astype(f32) + y1r[i, h, 1].astype(f32)
        for j, to in enumerate((1, -1)):
            both_cores = mine(to) + rc[i, h, 1 + j].astype(f32)
            for p in range(2):
                at = slice(p * half, (p + 1) * half)
                piece = both_cores[:, at] + got[:, at] if p == j else both_cores[:, at]
                y2b[i, h, j, :, at] = piece.astype(bf16)
        cps = [
            send(y2b.at[i, h, j], y2r.at[i, h, j], y2_s.at[i, h, j], y2_r.at[i, h, j], y_peer(to))
            for j, to in enumerate((1, -1))
        ]
        yield
        wait_all(cps)
        total = mine(0) + rc[i, h, 0].astype(f32) + y2r[i, h, 0].astype(f32) + y2r[i, h, 1].astype(f32)
        sz[i, h] = total.astype(bf16).reshape(N_Z, OWN, W)
        copies = [(sz.at[i, h, zs[k]], rz.at[i, h, k - 1], z_peer(k)) for k in range(1, N_Z)]
        cps = send_all(copies, rz.at[i, h], rz_s.at[i, h], rz_r.at[i, h])
        yield
        wait_all(cps)
        s3 = sz[i, h, z].astype(f32)
        for k in range(N_Z - 1):
            s3 = s3 + rz[i, h, k].astype(f32)
        tot[i, :, cols] = s3
        if i > 0:
            inner = [jnp.sum(lin[j, :, cols] * s3, axis=-1, keepdims=True) for j in range(2)]
            inners[i] = inner if h == 0 else [p + q for p, q in zip(inners[i], inner)]

    inners = [None, None, None]

    def scatters(i, make):
        return par(*[scatter(i, h, make) for h in range(CHUNKS)])

    def gathers(own, i):
        return par(*[gather(own, i, h) for h in range(CHUNKS)])

    def all_sum(i, n):
        for s, peer in enumerate((xy_peer, zc_peer)):
            copies = [
                (arv.at[i, s, pl.ds(0, n)], arr.at[i, s, k - 1, pl.ds(0, n)], peer(k)) for k in range(1, 16)
            ]
            cps = send_all(copies, arr.at[i, s, :, pl.ds(0, n)], ar_s.at[i, s], ar_r.at[i, s])
            yield
            wait_all(cps)
            acc = arv[i, s, 0:n]
            for k in range(1, 16):
                acc = acc + arr[i, s, k - 1, 0:n]
            arv[i, s + 1, 0:n] = acc

    group = rows(x * GRP, GRP)

    def group_tokens(h):
        c0 = h * W
        cols = pl.ds(c0, W)
        cps = gather_z(hin[:, c0 : c0 + W], xz.at[h], xz_s.at[h], xz_r.at[h])
        yield
        wait_all(cps)
        X[rows(x * GRP + c * HALF + y * BLK, BLK), cols] = join16(xz.at[h])
        passed = []

        def pass_on(k):
            if k != 2:
                at = (rows(x * GRP + c * HALF + y_at(k) * BLK, BLK), cols)
                passed.append(send(X.at[at], X.at[at], xc_s.at[h, k % 4], xc_r.at[h, k % 4], c_peer))

        yield from ring_gather(
            X,
            [(lambda k: x * GRP + c * HALF + y_at(k) * BLK, BLK)],
            c0,
            W,
            y_peer,
            xy_s.at[h],
            xy_r.at[h],
            pass_on,
            cross_peer,
        )
        wait_all(passed)
        by_hidden(X[group, cols], up, cols, agrad.at[0], h == 0)

    def accumulate_pt1(h, k):
        cols = pl.ds(h * W, W)
        block = span((x + k) % N_X, PAD)
        term = dot_t(X[group, cols], dirs[block, cols])
        pt1[:, block] = term if h == 0 else pt1[:, block] + term

    def start_rows(h):
        ring = ring_gather(
            dirs, [(lambda k: x_at(k) * PAD, ROWS)], h * W, W, x_peer, sx_s.at[h], sx_r.at[h]
        )
        next(ring)
        yield
        next(ring)
        yield
        loop(3, lambda k: accumulate_pt1(h, k + 3))
        yield
        run(ring)
        accumulate_pt1(h, 2)

    def other_tokens(h):
        cols = pl.ds(h * W, W)
        passed = []

        def pass_on(k):
            if k != 0:
                at = (rows(x_at(k) * GRP + c * HALF, HALF), cols)
                passed.append(send(X.at[at], X.at[at], xac_s.at[h, k % 4], xac_r.at[h, k % 4], c_peer))

        yield from ring_gather(
            X, [(lambda k: x_at(k) * GRP + c * HALF, HALF)], h * W, W, x_peer, xa_s.at[h], xa_r.at[h], pass_on
        )
        yield
        wait_all(passed)

    def local_work():
        loads[-1].wait()

        def cast(k):
            dirs[rows(x * PAD + k * 16, 16), :] = start[span(k, 16), :].astype(bf16)

        loop(ROWS // 16, cast)
        for g in s_gens:
            next(g)

        def clear(b):
            pad = rows(b * PAD + ROWS, PAD - ROWS)
            for ref in (up, down, dirs):
                ref[pad, :] = jnp.zeros((PAD - ROWS, D), bf16)

        loop(N_X, clear)
        yield
        for cp in loads[:-1]:
            cp.wait()
        arv[0, 0, 1] = jnp.zeros((8, 128), f32)

        def square(k):
            v = start[span(k, 16), :]
            arv[0, 0, 1] = arv[0, 0, 1] + tile_sum(v * v)

        loop(ROWS // 16, square)

    s_gens = [start_rows(h) for h in range(CHUNKS)]
    both = list(range(CHUNKS))
    n = CHUNKS
    play([group_tokens(h) for h in range(CHUNKS)] + [local_work()], both + [n] + both + [n] + both + both)

    def to_branch(i, h):
        def body(k):
            at = pl.ds(pl.multiple_of(h * W + k * (W // 3), 256), W // 3)
            part[i % 2, :, at] = dot(hact[...], down[:, at])

        loop(3, body)

    def weights():
        return tgt[...].astype(f32), gain[...]

    state = []

    def loss_curv(tangent, inner):
        r, bias = state
        a = inner[0] / D
        d = r * (inner[1] / D - a * bias)
        return lambda at: (lin[2, :, at] * tangent(at) + a * lin[3, :, at] + d * lin[4, :, at]).astype(bf16)

    def forward():
        def body(b):
            cols = span(b, PAD)
            value, first, second = gelu_parts(agrad[0, :, cols])
            hact[:, cols] = value.astype(bf16)
            slope[:, cols] = first
            bendag[:, cols] = second

        loop(N_X, body)
        yield from scatters(0, to_branch)
        bsum[...] = hin[...].astype(f32) + tot[0]
        parts = loss_parts(bsum[...], *weights())
        for j in range(5):
            lin[j] = parts[1 + j]
        state.extend(parts[6:])
        grad = parts[0].astype(bf16)
        yield from gathers(lambda at: grad[:, at], 0)
        bendag[...] = bendag[...] * agrad[0]

    def first_tangent():
        hact[...] = (slope[...] * pt1[...]).astype(bf16)
        yield from scatters(1, to_branch)

    fwd = forward()
    others = [other_tokens(h) for h in range(CHUNKS)]
    for g in [s_gens[0], fwd] + s_gens[1:] + s_gens + [fwd, fwd] + s_gens:
        next(g, None)
    tangent = first_tangent()
    for g in [tangent, fwd] + others:
        next(g, None)
    run(tangent, fwd)
    curv = loss_curv(lambda at: tot[1, :, at], inners[1])

    def token_gram(k):
        mine = span((x + k) % N_X, GRP)

        def body(j):
            at = span(j, 256)
            g = dot_t(X[mine, :], X[at, :])
            hi = g.astype(bf16)
            g_hi[mine, at] = hi
            g_lo[mine, at] = (g - hi.astype(f32)).astype(bf16)

        loop(TOK // 256, body)

    grads = gathers(curv, 1)
    for g in [grads] + others + [grads] + others + [grads] + others + [grads]:
        next(g, None)
    token_gram(0)
    run(grads)
    p1 = agrad[1] * slope[...] + bendag[...] * pt1[...]
    pfull[group, :] = p1.astype(bf16)

    def share_p1():
        def use(k):
            block = rows(x_at(k) * GRP, GRP)
            term = dot(g_hi[group, block], pfull[block, :]) + dot(g_lo[group, block], pfull[block, :])
            if k == 0:
                ptx[...] = term
            else:
                ptx[...] = ptx[...] + term

        cps = [
            send(pfull.at[group], pfull.at[group], pf_s.at[k - 1], pf_r.at[k - 1], x_peer(k))
            for k in range(1, N_X)
        ]
        use(0)
        yield
        for k in (1, 3, 2):
            wait_all([cps[k - 1]])
            use(N_X - k)

    def own_sums():
        arv[0, 0, 0] = tile_sum(p1 * pt1[...])
        yield

    run(share_p1(), own_sums())

    hact[...] = (slope[...] * ptx[...]).astype(bf16)

    def image(factor, out):
        def body(k):
            at = span(k, 512)
            out[:, at] = dot(factor, X[:, at])[0:ROWS, :]

        loop(D // 512, body)

    def image_one():
        own = pfull[:, pl.ds(pl.multiple_of(x * PAD, PAD), PAD)].T
        image(own, kw)
        yield

    run(scatters(2, to_branch), all_sum(0, 2), image_one())
    count = float(ROWS * 256 * D)
    q = jnp.sum(arv[0, 2, 0], keepdims=True) / count
    ss = jnp.sum(arv[0, 2, 1], keepdims=True) / count
    s1 = lax.rsqrt(ss + norm_eps)
    h11 = s1 * s1 * q
    curv = loss_curv(
        lambda at: tot[2, :, at] - h11 * tot[1, :, at], [p - h11 * q for p, q in zip(inners[2], inners[1])]
    )

    def remainder():
        ptx[...] = ptx[...] - h11 * pt1[...]
        arv[1, 0, 0] = jnp.zeros((8, 128), f32)

        def body(k):
            at = span(k, 512)
            w = kw[:, at] - h11 * start[:, at]
            kw[:, at] = w
            arv[1, 0, 0] = arv[1, 0, 0] + tile_sum(w * w)

        loop(D // 512, body)
        yield
        loop(N_X - 1, lambda k: token_gram(k + 1))
        yield

    run(gathers(curv, 2), remainder())
    out_w = pltpu.make_async_copy(kw, kw_hbm, out_sem.at[0])
    out_w.start()
    for b in range(N_X):
        cols = pl.ds(b * PAD, PAD)
        pr2[1, b] = (agrad[0, :, cols] * slope[:, cols] + bendag[:, cols] * ptx[:, cols]).astype(bf16)
    pr2[0, x] = pr2[1, x]
    cps = [
        send(pr2.at[1, x_at(k)], pr2.at[0, x], p2_s.at[k - 1], p2_r.at[k - 1], x_peer(k))
        for k in range(1, N_X)
    ]
    sums = [None, None]
    for b in range(N_X):
        cols = pl.ds(b * PAD, PAD)
        for j, other in enumerate((pt1, ptx)):
            t = tile_sum(other[:, cols] * pr2[1, b].astype(f32))
            sums[j] = t if sums[j] is None else sums[j] + t
    for j in range(2):
        arv[1, 0, 1 + j] = sums[j]
    wait_all(cps)
    own = pr2[0].reshape(TOK, PAD)
    arv[1, 0, 3] = jnp.zeros((8, 128), f32)

    def own_square(k):
        at = span(k, GRP)
        near = dot(g_hi[at, :], own) + dot(g_lo[at, :], own)
        arv[1, 0, 3] = arv[1, 0, 3] + tile_sum(near * pr2[0, k].astype(f32))

    loop(N_X, own_square)
    outs = [out_w]

    def image_two():
        turned = own.T
        image(turned, k2)
        yield
        outs.append(pltpu.make_async_copy(k2, k2_hbm, out_sem.at[1]))
        outs[1].start()

    run(all_sum(1, 4), image_two())
    ww, sk, wk, kk = [jnp.sum(arv[1, 2, j], keepdims=True) / count for j in range(4)]
    sq1 = s1 * s1 * ww
    scale2 = lax.rsqrt(sq1 + norm_eps)
    s2 = scale2 * s1
    h12 = s1 * s2 * sk
    h22 = s2 * s2 * wk
    cross = s1 * s2 * (q - h11 * ss)
    sq2 = (
        s2 * s2 * kk
        - 2.0 * (h12 * h12 + h22 * h22)
        + h12 * h12 * (s1 * s1 * ss)
        + h22 * h22 * (s2 * s2 * ww)
        + 2.0 * h12 * h22 * cross
    )
    sq2 = jnp.maximum(sq2, 0.0)
    s3 = lax.rsqrt(sq2 + norm_eps)
    results = (h11, h12, h22, jnp.sqrt(sq1), jnp.sqrt(sq2), s2, s3 * s2, -s3 * h12 * s1, -s3 * h22 * s2)
    for j, value in enumerate(results):
        mix[j] = value[0, 0]
    for cp in outs:
        cp.wait()
    settle(0)


def combine(mix, kw_hbm, k2_hbm, start_hbm, basis_hbm, quot, coef, kw, k2, start, out, in_sem, out_sem):
    parts = [pl.ds(r, PIECE) for r in range(0, ROWS, PIECE)]
    ins = [
        [
            pltpu.make_async_copy(src.at[at], dst.at[at], in_sem.at[j, p])
            for j, (src, dst) in enumerate(((kw_hbm, kw), (k2_hbm, k2), (start_hbm, start)))
        ]
        for p, at in enumerate(parts)
    ]
    for cps in ins:
        for cp in cps:
            cp.start()
    quot[0] = mix[0]
    coef[0, 0] = mix[1]
    coef[0, 1] = mix[2]
    coef[1, 0] = mix[3]
    coef[1, 1] = mix[4]
    outs = []
    for p, at in enumerate(parts):
        for cp in ins[p]:
            cp.wait()

        def body(k, p=p):
            part = pl.ds(pl.multiple_of(p * PIECE + k * 8, 8), 8)
            w = kw[part, :]
            out[0, part, :] = mix[5] * w
            out[1, part, :] = mix[6] * k2[part, :] + mix[7] * start[part, :] + mix[8] * w

        loop(PIECE // 8, body)
        for j in range(2):
            cp = pltpu.make_async_copy(out.at[j, at], basis_hbm.at[j, at], out_sem.at[j, p])
            cp.start()
            outs.append(cp)
    for cp in outs:
        cp.wait()


def per_device(hidden_in, targets, norm_gain, up_weight, down_weight, start):
    vm, dma = pltpu.VMEM, pltpu.SemaphoreType.DMA
    any_spec = pl.BlockSpec(memory_space=pl.ANY)
    smem_spec = pl.BlockSpec(memory_space=pltpu.SMEM)
    scratch = [
        vm((OWN, D), bf16),
        vm((OWN, D), bf16),
        vm((D,), f32),
        vm((HID, D), bf16),
        vm((HID, D), bf16),
        vm((ROWS, D), f32),
        vm((HID, D), bf16),
        vm((TOK, D), bf16),
        vm((CHUNKS, N_Z, OWN, W), bf16),
        vm((2, GRP, D), f32),
        vm((3, CHUNKS, 3, BLK, W), bf16),
        vm((3, CHUNKS, 3, BLK, W), bf16),
        vm((3, CHUNKS, 2, BLK, W), bf16),
        vm((3, CHUNKS, 2, BLK, W), bf16),
        vm((3, CHUNKS, 2, BLK, W), bf16),
        vm((3, CHUNKS, 2, BLK, W), bf16),
        vm((3, CHUNKS, N_Z, OWN, W), bf16),
        vm((3, CHUNKS, N_Z - 1, OWN, W), bf16),
        vm((3, CHUNKS, N_Z, OWN, W), bf16),
        vm((3, GRP, D), bf16),
        vm((GRP, HID), f32),
        vm((GRP, HID), f32),
        vm((GRP, HID), bf16),
        vm((2, GRP, HID), f32),
        vm((GRP, HID), f32),
        vm((GRP, HID), f32),
        vm((TOK, HID), bf16),
        vm((2, N_X, GRP, PAD), bf16),
        vm((TOK, TOK), bf16),
        vm((TOK, TOK), bf16),
        vm((ROWS, D), f32),
        vm((ROWS, D), f32),
        vm((2, 3, 4, 8, 128), f32),
        vm((2, 2, 15, 4, 8, 128), f32),
        vm((3, OWN, D), f32),
        vm((OWN, D), f32),
        vm((5, OWN, D), f32),
        dma((2 * N_X + 4,)),
    ]
    pairs = [
        (CHUNKS,), (CHUNKS, 6), (CHUNKS, 4),
        (CHUNKS, 4), (CHUNKS, 4), (CHUNKS, 4),
        (3, CHUNKS), (3, CHUNKS, 4), (3, CHUNKS, 2), (3, CHUNKS),
        (3, CHUNKS), (3, CHUNKS, 6), (3, CHUNKS, 4),
        (N_X - 1,), (N_X - 1,), (2, 2),
    ]
    for shape in pairs:
        scratch += [dma(shape), dma(shape)]
    scratch.append(dma((2,)))
    kw, k2, mix = pl.pallas_call(
        kernel,
        out_shape=(
            jax.ShapeDtypeStruct((ROWS, D), f32),
            jax.ShapeDtypeStruct((ROWS, D), f32),
            jax.ShapeDtypeStruct((9,), f32),
        ),
        in_specs=[any_spec] * 6,
        out_specs=(any_spec, any_spec, smem_spec),
        scratch_shapes=scratch,
        compiler_params=pltpu.CompilerParams(
            collective_id=0, has_side_effects=True, vmem_limit_bytes=60 * 1024 * 1024
        ),
        cost_estimate=pl.CostEstimate(flops=5 * 10**9, bytes_accessed=14 * 10**6, transcendentals=10**5),
    )(hidden_in, targets, norm_gain, up_weight, down_weight, start)
    pieces = ROWS // PIECE
    return pl.pallas_call(
        combine,
        out_shape=(
            jax.ShapeDtypeStruct((2, ROWS, D), f32),
            jax.ShapeDtypeStruct((1,), f32),
            jax.ShapeDtypeStruct((2, 2), f32),
        ),
        in_specs=[smem_spec, any_spec, any_spec, any_spec],
        out_specs=(any_spec, smem_spec, smem_spec),
        scratch_shapes=[
            vm((ROWS, D), f32),
            vm((ROWS, D), f32),
            vm((ROWS, D), f32),
            vm((2, ROWS, D), f32),
            dma((3, pieces)),
            dma((2, pieces)),
        ],
        compiler_params=pltpu.CompilerParams(vmem_limit_bytes=60 * 1024 * 1024),
        cost_estimate=pl.CostEstimate(flops=10**7, bytes_accessed=9 * 10**6, transcendentals=0),
    )(mix, kw, k2, start)


def solution(mesh):
    placed = (
        P(("dp", "zero"), None),
        P(("dp", "zero"), None),
        P(),
        P("zero", None),
        P("zero", None),
        P(("zero", "dp"), None),
    )
    return jax.shard_map(
        per_device,
        mesh=mesh,
        in_specs=placed,
        out_specs=(P(None, ("zero", "dp"), None), P(), P()),
        check_vma=False,
    )
```

```python
import jax
import jax.numpy as jnp
from jax import lax
from jax.experimental import pallas as pl
from jax.experimental.pallas import tpu as pltpu
from jax.sharding import PartitionSpec as P

MESH = pl.DeviceIdType.MESH
f32, bf16 = jnp.float32, jnp.bfloat16
norm_eps = 1e-06
gelu_coef = 0.7978845608028654

N_X, N_Y, N_Z, N_C = 4, 4, 8, 2
D = 4608
ROWS = 96
PAD = 128
HID = N_X * PAD
GRP = 128
TOK = N_X * GRP
HALF = GRP // N_C
BLK = HALF // N_Y
OWN = BLK // N_Z
CHUNKS = 3
W = D // CHUNKS
KEEP = 40
PIECE = 32


def gelu_value(inputs):
    return (
        0.5 * inputs * (1.0 + jnp.tanh(gelu_coef * (inputs + 0.044715 * inputs * inputs * inputs)))
    )


def gelu_parts(inputs):
    unit_dir = jnp.ones_like(inputs)

    def first_slope(points):
        return jax.jvp(gelu_value, (points,), (unit_dir,))[1]

    return (
        gelu_value(inputs),
        first_slope(inputs),
        jax.jvp(first_slope, (inputs,), (unit_dir,))[1],
    )


def loss_parts(summed, target, gain):
    r = lax.rsqrt(jnp.sum(summed * summed, axis=-1, keepdims=True) / D + norm_eps)
    normed = summed * r
    pull = (normed * gain - target) * gain
    mean = jnp.sum(pull * normed, axis=-1, keepdims=True) / D
    grad = r * (pull - normed * mean) / float(TOK)
    mix = gain * gain * normed + pull
    bias = jnp.sum(mix * normed, axis=-1, keepdims=True) / D
    scale = r * r * (gain * gain - mean) / float(TOK)
    along = -(scale * normed + r * grad)
    across = -r * normed / float(TOK)
    return grad, normed, mix, scale, along, across, r, bias


def dot_t(a, b):
    return lax.dot_general(a, b, (((1,), (1,)), ((), ())), preferred_element_type=f32)


def dot(a, b):
    return jnp.dot(a, b, preferred_element_type=f32)


def tile_sum(v):
    rows, cols = v.shape
    acc = v[0:8, :]
    for i in range(8, rows, 8):
        acc = acc + v[i : i + 8, :]
    out = acc[:, 0:128]
    for k in range(128, cols, 128):
        out = out + acc[:, k : k + 128]
    return out


def par(*gens):
    gens = list(gens)
    while gens:
        for g in list(gens):
            try:
                next(g)
            except StopIteration:
                gens.remove(g)
        if gens:
            yield


def run(*gens):
    for _ in par(*gens):
        pass


def play(gens, order):
    for j in order:
        next(gens[j], None)
    run(*gens)


def kernel(
    hin_hbm, tgt_hbm, gain_hbm, up_hbm, down_hbm, start_hbm,
    kw_hbm, k2_hbm, mix,
    hin, tgt, gain, up, down, start, dirs, X, xz, part,
    sb, rc, y1b, y1r, y2b, y2r, sz, rz, az, A,
    slope, bendag, hact, agrad, pt1, ptx,
    pfull, pr2, g_hi, g_lo, kw, k2, arv, arr, tot, bsum, lin,
    ld_sem, xz_s, xz_r, xy_s, xy_r, xc_s, xc_r,
    xa_s, xa_r, xac_s, xac_r, sx_s, sx_r,
    rc_s, rc_r, y1_s, y1_r, y2_s, y2_r, rz_s, rz_r,
    az_s, az_r, ay_s, ay_r, ac_s, ac_r,
    pf_s, pf_r, p2_s, p2_r, ar_s, ar_r, out_sem,
):
    x = lax.axis_index("dp")
    shard = lax.axis_index("zero")
    y, z, c = shard // 16, (shard // 2) % 8, shard % 2

    def dev(nx, ny, nz, nc):
        return (nx, ny * 16 + nz * 2 + nc)

    pending = []

    xs = [x] + [(x + k) % N_X for k in range(1, N_X)]
    ys = [y] + [(y + k) % N_Y for k in range(1, N_Y)]
    zs = [z] + [(z + k) % N_Z for k in range(1, N_Z)]

    def x_at(k):
        return xs[k % N_X]

    def y_at(k):
        return ys[k % N_Y]

    def x_peer(k):
        return dev(x_at(k), y, z, c)

    def y_peer(k):
        return dev(x, y_at(k), z, c)

    def z_peer(k):
        return dev(x, y, zs[k], c)

    c_peer = dev(x, y, z, 1 - c)

    def cross_peer(k):
        return dev(x, y_at(k), z, 1 - c)

    def xy_peer(k):
        return dev(x_at(k // N_Y), y_at(k % N_Y), z, c)

    def zc_peer(k):
        return dev(x, y, zs[k // N_C], c if k % N_C == 0 else 1 - c)

    def send(src, dst, ssem, rsem, to):
        cp = pltpu.make_async_remote_copy(
            src_ref=src, dst_ref=dst, send_sem=ssem, recv_sem=rsem, device_id=to, device_id_type=MESH
        )
        cp.start()
        pending.append(cp)
        return cp

    def send_all(copies, bytes_of, ssem, rsem):
        for src, dst, to in copies:
            pltpu.make_async_remote_copy(
                src_ref=src, dst_ref=dst, send_sem=ssem, recv_sem=rsem, device_id=to, device_id_type=MESH
            ).start()
        cp = pltpu.make_async_remote_copy(
            src_ref=bytes_of,
            dst_ref=bytes_of,
            send_sem=ssem,
            recv_sem=rsem,
            device_id=c_peer,
            device_id_type=MESH,
        )
        pending.append(cp)
        return [cp]

    def settle(keep=KEEP):
        while len(pending) > keep:
            pending.pop(0).wait_send()

    def rows(start_row, count):
        return pl.ds(pl.multiple_of(start_row, 16), count)

    def wait_all(cps):
        settle()
        for cp in cps:
            cp.wait_recv()

    small = [
        pltpu.make_async_copy(src, dst, ld_sem.at[2 * N_X + 1 + j])
        for j, (src, dst) in enumerate(((hin_hbm, hin), (tgt_hbm, tgt), (gain_hbm, gain)))
    ]
    for cp in small:
        cp.start()
    loads = []
    for b in range(N_X):
        for j, (src, dst) in enumerate(((up_hbm, up), (down_hbm, down))):
            loads.append(
                pltpu.make_async_copy(
                    src.at[pl.ds(b * ROWS, ROWS)], dst.at[pl.ds(b * PAD, ROWS)], ld_sem.at[2 * b + j]
                )
            )
    loads.append(pltpu.make_async_copy(start_hbm, start, ld_sem.at[2 * N_X]))
    for cp in loads:
        cp.start()

    barrier = pltpu.get_barrier_semaphore()
    peers = [xy_peer(k) for k in range(1, N_X * N_Y)] + [zc_peer(k) for k in range(1, N_Z * N_C)]
    peers += [cross_peer(1), cross_peer(-1)]
    for p in peers:
        pl.semaphore_signal(barrier, inc=1, device_id=p, device_id_type=MESH)
    pl.semaphore_wait(barrier, len(peers))
    for cp in small:
        cp.wait()

    def ring_gather(ref, blocks, c0, w, peer, ssem, rsem, then=None, cross=None):
        half = w // 2
        nb = len(blocks)
        first = []
        for b, (row_of, count) in enumerate(blocks):
            at = (rows(row_of(0), count), pl.ds(c0, w))
            first.append(
                [
                    send(ref.at[at], ref.at[at], ssem.at[2 * b + j], rsem.at[2 * b + j], peer(to))
                    for j, to in enumerate((1, -1))
                ]
            )
        if then:
            then(0)
        yield
        second = []
        for b, (row_of, count) in enumerate(blocks):
            for j, to in enumerate((1, -1)):
                wait_all([first[b][j]])
                at = (rows(row_of(-to), count), pl.ds(c0 + j * half, half))
                i = 2 * (nb + b) + j
                second.append(send(ref.at[at], ref.at[at], ssem.at[i], rsem.at[i], peer(to)))
                if cross:
                    second.append(send(ref.at[at], ref.at[at], ssem.at[i + 2], rsem.at[i + 2], cross(to)))
        if then:
            then(-1)
            then(1)
        yield
        wait_all(second)
        if then:
            then(2)

    def gather_z(own, buf, ssem, rsem):
        buf[z] = own
        copies = [(buf.at[z], buf.at[z], z_peer(k)) for k in range(1, N_Z)]
        return send_all(copies, buf.at[pl.ds(0, N_Z - 1)], ssem, rsem)

    def join16(buf):
        return buf[...].reshape(BLK, W)

    def gather(own, i, h):
        c0, out = h * W, A.at[i]
        cols = pl.ds(c0, W)
        cps = gather_z(own(slice(c0, c0 + W)), az.at[i, h], az_s.at[i, h], az_r.at[i, h])
        yield
        wait_all(cps)
        out[rows(c * HALF + y * BLK, BLK), cols] = join16(az.at[i, h])
        passed = []

        def pass_on(k):
            if k != 2 or i == 0:
                at = (rows(c * HALF + y_at(k) * BLK, BLK), cols)
                passed.append(send(out.at[at], out.at[at], ac_s.at[i, h, k % 4], ac_r.at[i, h, k % 4], c_peer))

        yield from ring_gather(
            out,
            [(lambda k: c * HALF + y_at(k) * BLK, BLK)],
            c0,
            W,
            y_peer,
            ay_s.at[i, h],
            ay_r.at[i, h],
            pass_on,
            cross_peer if i else None,
        )
        if i == 0:
            yield
        wait_all(passed)
        part_grad = dot_t(out[:, cols], down[:, cols])
        if h == 0:
            agrad[i % 2] = part_grad
        else:
            agrad[i % 2] = agrad[i % 2] + part_grad

    def scatter(i, h, make):
        c0 = h * W
        cols = slice(c0, c0 + W)
        make(i, h)
        buf = part.at[i % 2]

        def mine(k):
            return buf[rows(c * HALF + y_at(k) * BLK, BLK), cols]

        def other(k):
            return buf[rows((1 - c) * HALF + y_at(k) * BLK, BLK), cols]

        half = W // 2
        y1b[i, h, 0] = mine(2).astype(bf16)
        y1b[i, h, 1] = other(2).astype(bf16)
        cps = [
            send(
                y1b.at[i, h, p, :, pl.ds(j * half, half)],
                y1r.at[i, h, p, :, pl.ds(j * half, half)],
                y1_s.at[i, h, 2 * p + j],
                y1_r.at[i, h, 2 * p + j],
                peer(to),
            )
            for p, peer in enumerate((y_peer, cross_peer))
            for j, to in enumerate((1, -1))
        ]
        for n, k in enumerate((0, 1, -1)):
            sb[i, h, n] = other(k).astype(bf16)
        cps.append(send(sb.at[i, h], rc.at[i, h], rc_s.at[i, h], rc_r.at[i, h], c_peer))
        yield
        wait_all(cps)
        got = y1r[i, h, 0].astype(f32) + y1r[i, h, 1].astype(f32)
        for j, to in enumerate((1, -1)):
            both_cores = mine(to) + rc[i, h, 1 + j].astype(f32)
            for p in range(2):
                at = slice(p * half, (p + 1) * half)
                piece = both_cores[:, at] + got[:, at] if p == j else both_cores[:, at]
                y2b[i, h, j, :, at] = piece.astype(bf16)
        cps = [
            send(y2b.at[i, h, j], y2r.at[i, h, j], y2_s.at[i, h, j], y2_r.at[i, h, j], y_peer(to))
            for j, to in enumerate((1, -1))
        ]
        yield
        wait_all(cps)
        total = mine(0) + rc[i, h, 0].astype(f32) + y2r[i, h, 0].astype(f32) + y2r[i, h, 1].astype(f32)
        sz[i, h] = total.astype(bf16).reshape(N_Z, OWN, W)
        copies = [(sz.at[i, h, zs[k]], rz.at[i, h, k - 1], z_peer(k)) for k in range(1, N_Z)]
        cps = send_all(copies, rz.at[i, h], rz_s.at[i, h], rz_r.at[i, h])
        yield
        wait_all(cps)
        s3 = sz[i, h, z].astype(f32)
        for k in range(N_Z - 1):
            s3 = s3 + rz[i, h, k].astype(f32)
        tot[i, :, cols] = s3
        if i > 0:
            inner = [jnp.sum(lin[j, :, cols] * s3, axis=-1, keepdims=True) for j in range(2)]
            inners[i] = inner if h == 0 else [p + q for p, q in zip(inners[i], inner)]

    inners = [None, None, None]

    def scatters(i, make):
        return par(*[scatter(i, h, make) for h in range(CHUNKS)])

    def gathers(own, i):
        return par(*[gather(own, i, h) for h in range(CHUNKS)])

    def all_sum(i, n):
        for s, peer in enumerate((xy_peer, zc_peer)):
            copies = [
                (arv.at[i, s, pl.ds(0, n)], arr.at[i, s, k - 1, pl.ds(0, n)], peer(k)) for k in range(1, 16)
            ]
            cps = send_all(copies, arr.at[i, s, :, pl.ds(0, n)], ar_s.at[i, s], ar_r.at[i, s])
            yield
            wait_all(cps)
            acc = arv[i, s, 0:n]
            for k in range(1, 16):
                acc = acc + arr[i, s, k - 1, 0:n]
            arv[i, s + 1, 0:n] = acc

    group = rows(x * GRP, GRP)

    def group_tokens(h):
        c0 = h * W
        cols = pl.ds(c0, W)
        cps = gather_z(hin[:, c0 : c0 + W], xz.at[h], xz_s.at[h], xz_r.at[h])
        yield
        wait_all(cps)
        X[rows(x * GRP + c * HALF + y * BLK, BLK), cols] = join16(xz.at[h])
        passed = []

        def pass_on(k):
            if k != 2:
                at = (rows(x * GRP + c * HALF + y_at(k) * BLK, BLK), cols)
                passed.append(send(X.at[at], X.at[at], xc_s.at[h, k % 4], xc_r.at[h, k % 4], c_peer))

        yield from ring_gather(
            X,
            [(lambda k: x * GRP + c * HALF + y_at(k) * BLK, BLK)],
            c0,
            W,
            y_peer,
            xy_s.at[h],
            xy_r.at[h],
            pass_on,
            cross_peer,
        )
        wait_all(passed)
        pre = dot_t(X[group, cols], up[:, cols])
        if h == 0:
            agrad[0] = pre
        else:
            agrad[0] = agrad[0] + pre

    def accumulate_pt1(h, k):
        cols = pl.ds(h * W, W)
        block = rows(x_at(k) * PAD, PAD)
        lanes = pl.ds(pl.multiple_of(x_at(k) * PAD, PAD), PAD)
        term = dot_t(X[group, cols], dirs[block, cols])
        if h == 0:
            pt1[:, lanes] = term
        else:
            pt1[:, lanes] = pt1[:, lanes] + term

    def start_rows(h):
        ring = ring_gather(
            dirs, [(lambda k: x_at(k) * PAD, ROWS)], h * W, W, x_peer, sx_s.at[h], sx_r.at[h]
        )
        next(ring)
        yield
        next(ring)
        yield
        for k in (0, -1, 1):
            accumulate_pt1(h, k)
        yield
        run(ring)
        accumulate_pt1(h, 2)

    def other_tokens(h):
        cols = pl.ds(h * W, W)
        passed = []

        def pass_on(k):
            if k != 0:
                at = (rows(x_at(k) * GRP + c * HALF, HALF), cols)
                passed.append(send(X.at[at], X.at[at], xac_s.at[h, k % 4], xac_r.at[h, k % 4], c_peer))

        yield from ring_gather(
            X, [(lambda k: x_at(k) * GRP + c * HALF, HALF)], h * W, W, x_peer, xa_s.at[h], xa_r.at[h], pass_on
        )
        yield
        wait_all(passed)

    def local_work():
        loads[-1].wait()
        dirs[rows(x * PAD, ROWS), :] = start[...].astype(bf16)
        for g in s_gens:
            next(g)
        for b in range(N_X):
            pad = pl.ds(b * PAD + ROWS, PAD - ROWS)
            up[pad, :] = jnp.zeros((PAD - ROWS, D), bf16)
            down[pad, :] = jnp.zeros((PAD - ROWS, D), bf16)
            dirs[pad, :] = jnp.zeros((PAD - ROWS, D), bf16)
        yield
        for cp in loads[:-1]:
            cp.wait()
        arv[0, 0, 1] = tile_sum(start[...] * start[...])

    s_gens = [start_rows(h) for h in range(CHUNKS)]
    both = list(range(CHUNKS))
    n = CHUNKS
    play([group_tokens(h) for h in range(CHUNKS)] + [local_work()], both + [n] + both + [n] + both + both)

    def to_branch(i, h):
        for k in range(h * W, (h + 1) * W, W // 3):
            part[i % 2, :, k : k + W // 3] = dot(hact[...], down[:, k : k + W // 3])

    def weights():
        return tgt[...].astype(f32), gain[...]

    state = []

    def loss_curv(tangent, inner):
        r, bias = state
        a = inner[0] / D
        d = r * (inner[1] / D - a * bias)
        return lambda at: (lin[2, :, at] * tangent(at) + a * lin[3, :, at] + d * lin[4, :, at]).astype(bf16)

    def forward():
        for b in range(N_X):
            cols = pl.ds(b * PAD, PAD)
            value, first, second = gelu_parts(agrad[0, :, cols])
            hact[:, cols] = value.astype(bf16)
            slope[:, cols] = first
            bendag[:, cols] = second
        yield from scatters(0, to_branch)
        bsum[...] = hin[...].astype(f32) + tot[0]
        parts = loss_parts(bsum[...], *weights())
        for j in range(5):
            lin[j] = parts[1 + j]
        state.extend(parts[6:])
        grad = parts[0].astype(bf16)
        yield from gathers(lambda at: grad[:, at], 0)
        bendag[...] = bendag[...] * agrad[0]

    def first_tangent():
        hact[...] = (slope[...] * pt1[...]).astype(bf16)
        yield from scatters(1, to_branch)

    fwd = forward()
    others = [other_tokens(h) for h in range(CHUNKS)]
    for g in [s_gens[0], fwd] + s_gens[1:] + s_gens + [fwd, fwd] + s_gens:
        next(g, None)
    tangent = first_tangent()
    for g in [tangent, fwd] + others:
        next(g, None)
    run(tangent, fwd)
    curv = loss_curv(lambda at: tot[1, :, at], inners[1])

    def token_gram(k):
        mine = rows(x_at(k) * GRP, GRP)
        g = dot_t(X[mine, :], X[...])
        hi = g.astype(bf16)
        g_hi[mine, :] = hi
        g_lo[mine, :] = (g - hi.astype(f32)).astype(bf16)

    grads = gathers(curv, 1)
    for g in [grads] + others + [grads] + others + [grads] + others + [grads]:
        next(g, None)
    token_gram(0)
    run(grads)
    p1 = agrad[1] * slope[...] + bendag[...] * pt1[...]
    pfull[group, :] = p1.astype(bf16)

    def share_p1():
        def use(k):
            block = rows(x_at(k) * GRP, GRP)
            term = dot(g_hi[group, block], pfull[block, :]) + dot(g_lo[group, block], pfull[block, :])
            if k == 0:
                ptx[...] = term
            else:
                ptx[...] = ptx[...] + term

        cps = [
            send(pfull.at[group], pfull.at[group], pf_s.at[k - 1], pf_r.at[k - 1], x_peer(k))
            for k in range(1, N_X)
        ]
        use(0)
        yield
        for k in (1, 3, 2):
            wait_all([cps[k - 1]])
            use(N_X - k)

    def own_sums():
        arv[0, 0, 0] = tile_sum(p1 * pt1[...])
        yield

    run(share_p1(), own_sums())

    hact[...] = (slope[...] * ptx[...]).astype(bf16)

    def image_one():
        own = pfull[:, pl.ds(pl.multiple_of(x * PAD, PAD), PAD)].T
        for k in range(0, D, 512):
            kw[:, k : k + 512] = dot(own, X[:, k : k + 512])[0:ROWS, :]
            if k % 1536 == 1024:
                yield

    run(scatters(2, to_branch), all_sum(0, 2), image_one())
    count = float(ROWS * 256 * D)
    q = jnp.sum(arv[0, 2, 0], keepdims=True) / count
    ss = jnp.sum(arv[0, 2, 1], keepdims=True) / count
    s1 = lax.rsqrt(ss + norm_eps)
    h11 = s1 * s1 * q
    curv = loss_curv(
        lambda at: tot[2, :, at] - h11 * tot[1, :, at], [p - h11 * q for p, q in zip(inners[2], inners[1])]
    )

    def remainder():
        ptx[...] = ptx[...] - h11 * pt1[...]
        acc = None
        for k in range(0, D, 1536):
            w = kw[:, k : k + 1536] - h11 * start[:, k : k + 1536]
            kw[:, k : k + 1536] = w
            s = tile_sum(w * w)
            acc = s if acc is None else acc + s
            token_gram(k // 1536 + 1)
            yield
        arv[1, 0, 0] = acc

    run(gathers(curv, 2), remainder())
    out_w = pltpu.make_async_copy(kw, kw_hbm, out_sem.at[0])
    out_w.start()
    for b in range(N_X):
        cols = pl.ds(b * PAD, PAD)
        pr2[1, b] = (agrad[0, :, cols] * slope[:, cols] + bendag[:, cols] * ptx[:, cols]).astype(bf16)
    pr2[0, x] = pr2[1, x]
    cps = [
        send(pr2.at[1, x_at(k)], pr2.at[0, x], p2_s.at[k - 1], p2_r.at[k - 1], x_peer(k))
        for k in range(1, N_X)
    ]
    sums = [None, None]
    for b in range(N_X):
        cols = pl.ds(b * PAD, PAD)
        for j, other in enumerate((pt1, ptx)):
            t = tile_sum(other[:, cols] * pr2[1, b].astype(f32))
            sums[j] = t if sums[j] is None else sums[j] + t
    for j in range(2):
        arv[1, 0, 1 + j] = sums[j]
    wait_all(cps)
    own = pr2[0].reshape(TOK, PAD)
    arv[1, 0, 3] = tile_sum((dot(g_hi[...], own) + dot(g_lo[...], own)) * own.astype(f32))
    outs = [out_w]

    def image_two():
        turned = own.T
        for k in range(0, D, 512):
            k2[:, k : k + 512] = dot(turned, X[:, k : k + 512])[0:ROWS, :]
            if k == 2048:
                yield
        outs.append(pltpu.make_async_copy(k2, k2_hbm, out_sem.at[1]))
        outs[1].start()

    run(all_sum(1, 4), image_two())
    ww, sk, wk, kk = [jnp.sum(arv[1, 2, j], keepdims=True) / count for j in range(4)]
    sq1 = s1 * s1 * ww
    scale2 = lax.rsqrt(sq1 + norm_eps)
    s2 = scale2 * s1
    h12 = s1 * s2 * sk
    h22 = s2 * s2 * wk
    cross = s1 * s2 * (q - h11 * ss)
    sq2 = (
        s2 * s2 * kk
        - 2.0 * (h12 * h12 + h22 * h22)
        + h12 * h12 * (s1 * s1 * ss)
        + h22 * h22 * (s2 * s2 * ww)
        + 2.0 * h12 * h22 * cross
    )
    sq2 = jnp.maximum(sq2, 0.0)
    s3 = lax.rsqrt(sq2 + norm_eps)
    results = (h11, h12, h22, jnp.sqrt(sq1), jnp.sqrt(sq2), s2, s3 * s2, -s3 * h12 * s1, -s3 * h22 * s2)
    for j, value in enumerate(results):
        mix[j] = value[0, 0]
    for cp in outs:
        cp.wait()
    settle(0)


def combine(mix, kw_hbm, k2_hbm, start_hbm, basis_hbm, quot, coef, kw, k2, start, out, in_sem, out_sem):
    parts = [pl.ds(r, PIECE) for r in range(0, ROWS, PIECE)]
    ins = [
        [
            pltpu.make_async_copy(src.at[at], dst.at[at], in_sem.at[j, p])
            for j, (src, dst) in enumerate(((kw_hbm, kw), (k2_hbm, k2), (start_hbm, start)))
        ]
        for p, at in enumerate(parts)
    ]
    for cps in ins:
        for cp in cps:
            cp.start()
    quot[0] = mix[0]
    coef[0, 0] = mix[1]
    coef[0, 1] = mix[2]
    coef[1, 0] = mix[3]
    coef[1, 1] = mix[4]
    outs = []
    for p, at in enumerate(parts):
        for cp in ins[p]:
            cp.wait()
        w = kw[at, :]
        out[0, at, :] = mix[5] * w
        out[1, at, :] = mix[6] * k2[at, :] + mix[7] * start[at, :] + mix[8] * w
        for j in range(2):
            cp = pltpu.make_async_copy(out.at[j, at], basis_hbm.at[j, at], out_sem.at[j, p])
            cp.start()
            outs.append(cp)
    for cp in outs:
        cp.wait()


def per_device(hidden_in, targets, norm_gain, up_weight, down_weight, start):
    vm, dma = pltpu.VMEM, pltpu.SemaphoreType.DMA
    any_spec = pl.BlockSpec(memory_space=pl.ANY)
    smem_spec = pl.BlockSpec(memory_space=pltpu.SMEM)
    scratch = [
        vm((OWN, D), bf16),
        vm((OWN, D), bf16),
        vm((D,), f32),
        vm((HID, D), bf16),
        vm((HID, D), bf16),
        vm((ROWS, D), f32),
        vm((HID, D), bf16),
        vm((TOK, D), bf16),
        vm((CHUNKS, N_Z, OWN, W), bf16),
        vm((2, GRP, D), f32),
        vm((3, CHUNKS, 3, BLK, W), bf16),
        vm((3, CHUNKS, 3, BLK, W), bf16),
        vm((3, CHUNKS, 2, BLK, W), bf16),
        vm((3, CHUNKS, 2, BLK, W), bf16),
        vm((3, CHUNKS, 2, BLK, W), bf16),
        vm((3, CHUNKS, 2, BLK, W), bf16),
        vm((3, CHUNKS, N_Z, OWN, W), bf16),
        vm((3, CHUNKS, N_Z - 1, OWN, W), bf16),
        vm((3, CHUNKS, N_Z, OWN, W), bf16),
        vm((3, GRP, D), bf16),
        vm((GRP, HID), f32),
        vm((GRP, HID), f32),
        vm((GRP, HID), bf16),
        vm((2, GRP, HID), f32),
        vm((GRP, HID), f32),
        vm((GRP, HID), f32),
        vm((TOK, HID), bf16),
        vm((2, N_X, GRP, PAD), bf16),
        vm((TOK, TOK), bf16),
        vm((TOK, TOK), bf16),
        vm((ROWS, D), f32),
        vm((ROWS, D), f32),
        vm((2, 3, 4, 8, 128), f32),
        vm((2, 2, 15, 4, 8, 128), f32),
        vm((3, OWN, D), f32),
        vm((OWN, D), f32),
        vm((5, OWN, D), f32),
        dma((2 * N_X + 4,)),
    ]
    pairs = [
        (CHUNKS,), (CHUNKS, 6), (CHUNKS, 4),
        (CHUNKS, 4), (CHUNKS, 4), (CHUNKS, 4),
        (3, CHUNKS), (3, CHUNKS, 4), (3, CHUNKS, 2), (3, CHUNKS),
        (3, CHUNKS), (3, CHUNKS, 6), (3, CHUNKS, 4),
        (N_X - 1,), (N_X - 1,), (2, 2),
    ]
    for shape in pairs:
        scratch += [dma(shape), dma(shape)]
    scratch.append(dma((2,)))
    kw, k2, mix = pl.pallas_call(
        kernel,
        out_shape=(
            jax.ShapeDtypeStruct((ROWS, D), f32),
            jax.ShapeDtypeStruct((ROWS, D), f32),
            jax.ShapeDtypeStruct((9,), f32),
        ),
        in_specs=[any_spec] * 6,
        out_specs=(any_spec, any_spec, smem_spec),
        scratch_shapes=scratch,
        compiler_params=pltpu.CompilerParams(
            collective_id=0, has_side_effects=True, vmem_limit_bytes=60 * 1024 * 1024
        ),
        cost_estimate=pl.CostEstimate(flops=5 * 10**9, bytes_accessed=14 * 10**6, transcendentals=10**5),
    )(hidden_in, targets, norm_gain, up_weight, down_weight, start)
    pieces = ROWS // PIECE
    return pl.pallas_call(
        combine,
        out_shape=(
            jax.ShapeDtypeStruct((2, ROWS, D), f32),
            jax.ShapeDtypeStruct((1,), f32),
            jax.ShapeDtypeStruct((2, 2), f32),
        ),
        in_specs=[smem_spec, any_spec, any_spec, any_spec],
        out_specs=(any_spec, smem_spec, smem_spec),
        scratch_shapes=[
            vm((ROWS, D), f32),
            vm((ROWS, D), f32),
            vm((ROWS, D), f32),
            vm((2, ROWS, D), f32),
            dma((3, pieces)),
            dma((2, pieces)),
        ],
        compiler_params=pltpu.CompilerParams(vmem_limit_bytes=60 * 1024 * 1024),
        cost_estimate=pl.CostEstimate(flops=10**7, bytes_accessed=9 * 10**6, transcendentals=0),
    )(mix, kw, k2, start)


def solution(mesh):
    placed = (
        P(("dp", "zero"), None),
        P(("dp", "zero"), None),
        P(),
        P("zero", None),
        P("zero", None),
        P(("zero", "dp"), None),
    )
    return jax.shard_map(
        per_device,
        mesh=mesh,
        in_specs=placed,
        out_specs=(P(None, ("zero", "dp"), None), P(), P()),
        check_vma=False,
    )
```

```python
import jax
import jax.numpy as jnp
from jax import lax
from jax.experimental import pallas as pl
from jax.experimental.pallas import tpu as pltpu
from jax.sharding import PartitionSpec as P

MESH = pl.DeviceIdType.MESH
f32, bf16 = jnp.float32, jnp.bfloat16
norm_eps = 1e-06
gelu_coef = 0.7978845608028654

N_X, N_Y, N_Z, N_C = 4, 4, 8, 2
D = 4608
ROWS = 96
PAD = 128
HID = N_X * PAD
GRP = 128
TOK = N_X * GRP
HALF = GRP // N_C
BLK = HALF // N_Y
OWN = BLK // N_Z
CHUNKS = 3
W = D // CHUNKS
KEEP = 40
PIECE = 32


def gelu_value(inputs):
    return (
        0.5 * inputs * (1.0 + jnp.tanh(gelu_coef * (inputs + 0.044715 * inputs * inputs * inputs)))
    )


def gelu_parts(inputs):
    unit_dir = jnp.ones_like(inputs)

    def first_slope(points):
        return jax.jvp(gelu_value, (points,), (unit_dir,))[1]

    return (
        gelu_value(inputs),
        first_slope(inputs),
        jax.jvp(first_slope, (inputs,), (unit_dir,))[1],
    )


def loss_parts(summed, target, gain):
    r = lax.rsqrt(jnp.sum(summed * summed, axis=-1, keepdims=True) / D + norm_eps)
    normed = summed * r
    pull = (normed * gain - target) * gain
    mean = jnp.sum(pull * normed, axis=-1, keepdims=True) / D
    grad = r * (pull - normed * mean) / float(TOK)
    mix = gain * gain * normed + pull
    bias = jnp.sum(mix * normed, axis=-1, keepdims=True) / D
    scale = r * r * (gain * gain - mean) / float(TOK)
    along = -(scale * normed + r * grad)
    across = -r * normed / float(TOK)
    return grad, normed, mix, scale, along, across, r, bias


def dot_t(a, b):
    return lax.dot_general(a, b, (((1,), (1,)), ((), ())), preferred_element_type=f32)


def dot(a, b):
    return jnp.dot(a, b, preferred_element_type=f32)


def tile_sum(v):
    rows, cols = v.shape
    acc = v[0:8, :]
    for i in range(8, rows, 8):
        acc = acc + v[i : i + 8, :]
    out = acc[:, 0:128]
    for k in range(128, cols, 128):
        out = out + acc[:, k : k + 128]
    return out


def par(*gens):
    gens = list(gens)
    while gens:
        for g in list(gens):
            try:
                next(g)
            except StopIteration:
                gens.remove(g)
        if gens:
            yield


def run(*gens):
    for _ in par(*gens):
        pass


def play(gens, order):
    for j in order:
        next(gens[j], None)
    run(*gens)


def kernel(
    hin_hbm, tgt_hbm, gain_hbm, up_hbm, down_hbm, start_hbm,
    kw_hbm, k2_hbm, mix,
    hin, tgt, gain, up, down, start, dirs, X, xz, part,
    sb, rc, y1b, y1r, y2b, y2r, sz, rz, az, A,
    slope, bendag, hact, agrad, pt1, ptx,
    pfull, pr2, g_hi, g_lo, kw, k2, arv, arr, tot, bsum, lin,
    ld_sem, xz_s, xz_r, xy_s, xy_r, xc_s, xc_r,
    xa_s, xa_r, xac_s, xac_r, sx_s, sx_r,
    rc_s, rc_r, y1_s, y1_r, y2_s, y2_r, rz_s, rz_r,
    az_s, az_r, ay_s, ay_r, ac_s, ac_r,
    pf_s, pf_r, p2_s, p2_r, ar_s, ar_r, out_sem,
):
    x = lax.axis_index("dp")
    shard = lax.axis_index("zero")
    y, z, c = shard // 16, (shard // 2) % 8, shard % 2

    def dev(nx, ny, nz, nc):
        return (nx, ny * 16 + nz * 2 + nc)

    pending = []

    xs = [x] + [(x + k) % N_X for k in range(1, N_X)]
    ys = [y] + [(y + k) % N_Y for k in range(1, N_Y)]
    zs = [z] + [(z + k) % N_Z for k in range(1, N_Z)]

    def x_at(k):
        return xs[k % N_X]

    def y_at(k):
        return ys[k % N_Y]

    def x_peer(k):
        return dev(x_at(k), y, z, c)

    def y_peer(k):
        return dev(x, y_at(k), z, c)

    def z_peer(k):
        return dev(x, y, zs[k], c)

    c_peer = dev(x, y, z, 1 - c)

    def cross_peer(k):
        return dev(x, y_at(k), z, 1 - c)

    def xy_peer(k):
        return dev(x_at(k // N_Y), y_at(k % N_Y), z, c)

    def zc_peer(k):
        return dev(x, y, zs[k // N_C], c if k % N_C == 0 else 1 - c)

    def send(src, dst, ssem, rsem, to):
        cp = pltpu.make_async_remote_copy(
            src_ref=src, dst_ref=dst, send_sem=ssem, recv_sem=rsem, device_id=to, device_id_type=MESH
        )
        cp.start()
        pending.append(cp)
        return cp

    def send_all(copies, bytes_of, ssem, rsem):
        for src, dst, to in copies:
            pltpu.make_async_remote_copy(
                src_ref=src, dst_ref=dst, send_sem=ssem, recv_sem=rsem, device_id=to, device_id_type=MESH
            ).start()
        cp = pltpu.make_async_remote_copy(
            src_ref=bytes_of,
            dst_ref=bytes_of,
            send_sem=ssem,
            recv_sem=rsem,
            device_id=c_peer,
            device_id_type=MESH,
        )
        pending.append(cp)
        return [cp]

    def settle(keep=KEEP):
        while len(pending) > keep:
            pending.pop(0).wait_send()

    def rows(start_row, count):
        return pl.ds(pl.multiple_of(start_row, 16), count)

    def wait_all(cps):
        settle()
        for cp in cps:
            cp.wait_recv()

    small = [
        pltpu.make_async_copy(src, dst, ld_sem.at[2 * N_X + 1 + j])
        for j, (src, dst) in enumerate(((hin_hbm, hin), (tgt_hbm, tgt), (gain_hbm, gain)))
    ]
    for cp in small:
        cp.start()
    loads = []
    for b in range(N_X):
        for j, (src, dst) in enumerate(((up_hbm, up), (down_hbm, down))):
            loads.append(
                pltpu.make_async_copy(
                    src.at[pl.ds(b * ROWS, ROWS)], dst.at[pl.ds(b * PAD, ROWS)], ld_sem.at[2 * b + j]
                )
            )
    loads.append(pltpu.make_async_copy(start_hbm, start, ld_sem.at[2 * N_X]))
    for cp in loads:
        cp.start()

    barrier = pltpu.get_barrier_semaphore()
    peers = [xy_peer(k) for k in range(1, N_X * N_Y)] + [zc_peer(k) for k in range(1, N_Z * N_C)]
    peers += [cross_peer(1), cross_peer(-1)]
    for p in peers:
        pl.semaphore_signal(barrier, inc=1, device_id=p, device_id_type=MESH)
    pl.semaphore_wait(barrier, len(peers))
    for cp in small:
        cp.wait()

    def ring_gather(ref, blocks, c0, w, peer, ssem, rsem, then=None, cross=None):
        half = w // 2
        nb = len(blocks)
        first = []
        for b, (row_of, count) in enumerate(blocks):
            at = (rows(row_of(0), count), pl.ds(c0, w))
            first.append(
                [
                    send(ref.at[at], ref.at[at], ssem.at[2 * b + j], rsem.at[2 * b + j], peer(to))
                    for j, to in enumerate((1, -1))
                ]
            )
        if then:
            then(0)
        yield
        second = []
        for b, (row_of, count) in enumerate(blocks):
            for j, to in enumerate((1, -1)):
                wait_all([first[b][j]])
                at = (rows(row_of(-to), count), pl.ds(c0 + j * half, half))
                i = 2 * (nb + b) + j
                second.append(send(ref.at[at], ref.at[at], ssem.at[i], rsem.at[i], peer(to)))
                if cross:
                    second.append(send(ref.at[at], ref.at[at], ssem.at[i + 2], rsem.at[i + 2], cross(to)))
        if then:
            then(-1)
            then(1)
        yield
        wait_all(second)
        if then:
            then(2)

    def gather_z(own, buf, ssem, rsem):
        buf[z] = own
        copies = [(buf.at[z], buf.at[z], z_peer(k)) for k in range(1, N_Z)]
        return send_all(copies, buf.at[pl.ds(0, N_Z - 1)], ssem, rsem)

    def join16(buf):
        return buf[...].reshape(BLK, W)

    def gather(own, i, h):
        c0, out = h * W, A.at[i]
        cols = pl.ds(c0, W)
        cps = gather_z(own(slice(c0, c0 + W)), az.at[i, h], az_s.at[i, h], az_r.at[i, h])
        yield
        wait_all(cps)
        out[rows(c * HALF + y * BLK, BLK), cols] = join16(az.at[i, h])
        passed = []

        def pass_on(k):
            if k != 2 or i == 0:
                at = (rows(c * HALF + y_at(k) * BLK, BLK), cols)
                passed.append(send(out.at[at], out.at[at], ac_s.at[i, h, k % 4], ac_r.at[i, h, k % 4], c_peer))

        yield from ring_gather(
            out,
            [(lambda k: c * HALF + y_at(k) * BLK, BLK)],
            c0,
            W,
            y_peer,
            ay_s.at[i, h],
            ay_r.at[i, h],
            pass_on,
            cross_peer if i else None,
        )
        if i == 0:
            yield
        wait_all(passed)
        part_grad = dot_t(out[:, cols], down[:, cols])
        if h == 0:
            agrad[i % 2] = part_grad
        else:
            agrad[i % 2] = agrad[i % 2] + part_grad

    def scatter(i, h, make):
        c0 = h * W
        cols = slice(c0, c0 + W)
        make(i, h)
        buf = part.at[i % 2]

        def mine(k):
            return buf[rows(c * HALF + y_at(k) * BLK, BLK), cols]

        def other(k):
            return buf[rows((1 - c) * HALF + y_at(k) * BLK, BLK), cols]

        half = W // 2
        y1b[i, h, 0] = mine(2).astype(bf16)
        y1b[i, h, 1] = other(2).astype(bf16)
        cps = [
            send(
                y1b.at[i, h, p, :, pl.ds(j * half, half)],
                y1r.at[i, h, p, :, pl.ds(j * half, half)],
                y1_s.at[i, h, 2 * p + j],
                y1_r.at[i, h, 2 * p + j],
                peer(to),
            )
            for p, peer in enumerate((y_peer, cross_peer))
            for j, to in enumerate((1, -1))
        ]
        for n, k in enumerate((0, 1, -1)):
            sb[i, h, n] = other(k).astype(bf16)
        cps.append(send(sb.at[i, h], rc.at[i, h], rc_s.at[i, h], rc_r.at[i, h], c_peer))
        yield
        wait_all(cps)
        got = y1r[i, h, 0].astype(f32) + y1r[i, h, 1].astype(f32)
        for j, to in enumerate((1, -1)):
            both_cores = mine(to) + rc[i, h, 1 + j].astype(f32)
            for p in range(2):
                at = slice(p * half, (p + 1) * half)
                piece = both_cores[:, at] + got[:, at] if p == j else both_cores[:, at]
                y2b[i, h, j, :, at] = piece.astype(bf16)
        cps = [
            send(y2b.at[i, h, j], y2r.at[i, h, j], y2_s.at[i, h, j], y2_r.at[i, h, j], y_peer(to))
            for j, to in enumerate((1, -1))
        ]
        yield
        wait_all(cps)
        total = mine(0) + rc[i, h, 0].astype(f32) + y2r[i, h, 0].astype(f32) + y2r[i, h, 1].astype(f32)
        sz[i, h] = total.astype(bf16).reshape(N_Z, OWN, W)
        copies = [(sz.at[i, h, zs[k]], rz.at[i, h, k - 1], z_peer(k)) for k in range(1, N_Z)]
        cps = send_all(copies, rz.at[i, h], rz_s.at[i, h], rz_r.at[i, h])
        yield
        wait_all(cps)
        s3 = sz[i, h, z].astype(f32)
        for k in range(N_Z - 1):
            s3 = s3 + rz[i, h, k].astype(f32)
        tot[i, :, cols] = s3
        if i > 0:
            inner = [jnp.sum(lin[j, :, cols] * s3, axis=-1, keepdims=True) for j in range(2)]
            inners[i] = inner if h == 0 else [p + q for p, q in zip(inners[i], inner)]

    inners = [None, None, None]

    def scatters(i, make):
        return par(*[scatter(i, h, make) for h in range(CHUNKS)])

    def gathers(own, i):
        return par(*[gather(own, i, h) for h in range(CHUNKS)])

    def all_sum(i, n):
        for s, peer in enumerate((xy_peer, zc_peer)):
            copies = [
                (arv.at[i, s, pl.ds(0, n)], arr.at[i, s, k - 1, pl.ds(0, n)], peer(k)) for k in range(1, 16)
            ]
            cps = send_all(copies, arr.at[i, s, :, pl.ds(0, n)], ar_s.at[i, s], ar_r.at[i, s])
            yield
            wait_all(cps)
            acc = arv[i, s, 0:n]
            for k in range(1, 16):
                acc = acc + arr[i, s, k - 1, 0:n]
            arv[i, s + 1, 0:n] = acc

    group = rows(x * GRP, GRP)

    def group_tokens(h):
        c0 = h * W
        cols = pl.ds(c0, W)
        cps = gather_z(hin[:, c0 : c0 + W], xz.at[h], xz_s.at[h], xz_r.at[h])
        yield
        wait_all(cps)
        X[rows(x * GRP + c * HALF + y * BLK, BLK), cols] = join16(xz.at[h])
        passed = []

        def pass_on(k):
            if k != 2:
                at = (rows(x * GRP + c * HALF + y_at(k) * BLK, BLK), cols)
                passed.append(send(X.at[at], X.at[at], xc_s.at[h, k % 4], xc_r.at[h, k % 4], c_peer))

        yield from ring_gather(
            X,
            [(lambda k: x * GRP + c * HALF + y_at(k) * BLK, BLK)],
            c0,
            W,
            y_peer,
            xy_s.at[h],
            xy_r.at[h],
            pass_on,
            cross_peer,
        )
        wait_all(passed)
        pre = dot_t(X[group, cols], up[:, cols])
        if h == 0:
            agrad[0] = pre
        else:
            agrad[0] = agrad[0] + pre

    def accumulate_pt1(h, k):
        cols = pl.ds(h * W, W)
        block = rows(x_at(k) * PAD, PAD)
        lanes = pl.ds(pl.multiple_of(x_at(k) * PAD, PAD), PAD)
        term = dot_t(X[group, cols], dirs[block, cols])
        if h == 0:
            pt1[:, lanes] = term
        else:
            pt1[:, lanes] = pt1[:, lanes] + term

    def start_rows(h):
        ring = ring_gather(
            dirs, [(lambda k: x_at(k) * PAD, ROWS)], h * W, W, x_peer, sx_s.at[h], sx_r.at[h]
        )
        next(ring)
        yield
        next(ring)
        yield
        for k in (0, -1, 1):
            accumulate_pt1(h, k)
        yield
        run(ring)
        accumulate_pt1(h, 2)

    def other_tokens(h):
        cols = pl.ds(h * W, W)
        passed = []

        def pass_on(k):
            if k != 0:
                at = (rows(x_at(k) * GRP + c * HALF, HALF), cols)
                passed.append(send(X.at[at], X.at[at], xac_s.at[h, k % 4], xac_r.at[h, k % 4], c_peer))

        yield from ring_gather(
            X, [(lambda k: x_at(k) * GRP + c * HALF, HALF)], h * W, W, x_peer, xa_s.at[h], xa_r.at[h], pass_on
        )
        yield
        wait_all(passed)

    def local_work():
        loads[-1].wait()
        dirs[rows(x * PAD, ROWS), :] = start[...].astype(bf16)
        for g in s_gens:
            next(g)
        for b in range(N_X):
            pad = pl.ds(b * PAD + ROWS, PAD - ROWS)
            up[pad, :] = jnp.zeros((PAD - ROWS, D), bf16)
            down[pad, :] = jnp.zeros((PAD - ROWS, D), bf16)
            dirs[pad, :] = jnp.zeros((PAD - ROWS, D), bf16)
        yield
        for cp in loads[:-1]:
            cp.wait()
        arv[0, 0, 1] = tile_sum(start[...] * start[...])

    s_gens = [start_rows(h) for h in range(CHUNKS)]
    both = list(range(CHUNKS))
    n = CHUNKS
    play([group_tokens(h) for h in range(CHUNKS)] + [local_work()], both + [n] + both + [n] + both + both)

    def to_branch(i, h):
        for k in range(h * W, (h + 1) * W, W // 3):
            part[i % 2, :, k : k + W // 3] = dot(hact[...], down[:, k : k + W // 3])

    def weights():
        return tgt[...].astype(f32), gain[...]

    state = []

    def loss_curv(tangent, inner):
        r, bias = state
        a = inner[0] / D
        d = r * (inner[1] / D - a * bias)
        return lambda at: (lin[2, :, at] * tangent(at) + a * lin[3, :, at] + d * lin[4, :, at]).astype(bf16)

    def forward():
        for b in range(N_X):
            cols = pl.ds(b * PAD, PAD)
            value, first, second = gelu_parts(agrad[0, :, cols])
            hact[:, cols] = value.astype(bf16)
            slope[:, cols] = first
            bendag[:, cols] = second
        yield from scatters(0, to_branch)
        bsum[...] = hin[...].astype(f32) + tot[0]
        parts = loss_parts(bsum[...], *weights())
        for j in range(5):
            lin[j] = parts[1 + j]
        state.extend(parts[6:])
        grad = parts[0].astype(bf16)
        yield from gathers(lambda at: grad[:, at], 0)
        bendag[...] = bendag[...] * agrad[0]

    def first_tangent():
        hact[...] = (slope[...] * pt1[...]).astype(bf16)
        yield from scatters(1, to_branch)

    fwd = forward()
    others = [other_tokens(h) for h in range(CHUNKS)]
    for g in [s_gens[0], fwd] + s_gens[1:] + s_gens + [fwd, fwd] + s_gens:
        next(g, None)
    tangent = first_tangent()
    for g in [tangent, fwd] + others:
        next(g, None)
    for g in [tangent, fwd, tangent, fwd, others[0]]:
        next(g, None)
    run(tangent)
    curv = loss_curv(lambda at: tot[1, :, at], inners[1])

    def token_gram(k):
        mine = rows(x_at(k) * GRP, GRP)
        g = dot_t(X[mine, :], X[...])
        hi = g.astype(bf16)
        g_hi[mine, :] = hi
        g_lo[mine, :] = (g - hi.astype(f32)).astype(bf16)

    grads = gathers(curv, 1)
    for g in [grads, fwd, *others[1:], fwd, grads, others[0], grads, *others[1:], *others]:
        next(g, None)
    run(fwd, *others)
    token_gram(0)
    run(grads)
    p1 = agrad[1] * slope[...] + bendag[...] * pt1[...]
    pfull[group, :] = p1.astype(bf16)

    def share_p1():
        def use(k):
            block = rows(x_at(k) * GRP, GRP)
            term = dot(g_hi[group, block], pfull[block, :]) + dot(g_lo[group, block], pfull[block, :])
            if k == 0:
                ptx[...] = term
            else:
                ptx[...] = ptx[...] + term

        cps = [
            send(pfull.at[group], pfull.at[group], pf_s.at[k - 1], pf_r.at[k - 1], x_peer(k))
            for k in range(1, N_X)
        ]
        use(0)
        yield
        for k in (1, 3, 2):
            wait_all([cps[k - 1]])
            use(N_X - k)

    def own_sums():
        arv[0, 0, 0] = tile_sum(p1 * pt1[...])
        yield

    run(share_p1(), own_sums())

    hact[...] = (slope[...] * ptx[...]).astype(bf16)

    def image_one():
        own = pfull[:, pl.ds(pl.multiple_of(x * PAD, PAD), PAD)].T
        for k in range(0, D, 512):
            kw[:, k : k + 512] = dot(own, X[:, k : k + 512])[0:ROWS, :]
            if k % 1536 == 1024:
                yield

    count = float(ROWS * 256 * D)
    firsts = []

    def first_sums():
        yield from all_sum(0, 2)
        q = jnp.sum(arv[0, 2, 0], keepdims=True) / count
        ss = jnp.sum(arv[0, 2, 1], keepdims=True) / count
        s1 = lax.rsqrt(ss + norm_eps)
        firsts.extend([q, ss, s1, s1 * s1 * q])

    run(scatters(2, to_branch), first_sums(), image_one())
    q, ss, s1, h11 = firsts
    curv = loss_curv(
        lambda at: tot[2, :, at] - h11 * tot[1, :, at], [p - h11 * q for p, q in zip(inners[2], inners[1])]
    )

    def remainder():
        ptx[...] = ptx[...] - h11 * pt1[...]
        acc = None
        for k in range(0, D, 1536):
            w = kw[:, k : k + 1536] - h11 * start[:, k : k + 1536]
            kw[:, k : k + 1536] = w
            s = tile_sum(w * w)
            acc = s if acc is None else acc + s
            token_gram(k // 1536 + 1)
            yield
        arv[1, 0, 0] = acc

    run(gathers(curv, 2), remainder())
    out_w = pltpu.make_async_copy(kw, kw_hbm, out_sem.at[0])
    out_w.start()
    for b in range(N_X):
        cols = pl.ds(b * PAD, PAD)
        pr2[1, b] = (agrad[0, :, cols] * slope[:, cols] + bendag[:, cols] * ptx[:, cols]).astype(bf16)
    pr2[0, x] = pr2[1, x]
    cps = [
        send(pr2.at[1, x_at(k)], pr2.at[0, x], p2_s.at[k - 1], p2_r.at[k - 1], x_peer(k))
        for k in range(1, N_X)
    ]
    sums = [None, None]
    for b in range(N_X):
        cols = pl.ds(b * PAD, PAD)
        for j, other in enumerate((pt1, ptx)):
            t = tile_sum(other[:, cols] * pr2[1, b].astype(f32))
            sums[j] = t if sums[j] is None else sums[j] + t
    for j in range(2):
        arv[1, 0, 1 + j] = sums[j]
    wait_all(cps)
    own = pr2[0].reshape(TOK, PAD)
    arv[1, 0, 3] = tile_sum((dot(g_hi[...], own) + dot(g_lo[...], own)) * own.astype(f32))
    outs = [out_w]

    def image_two():
        turned = own.T
        for k in range(0, D, 512):
            k2[:, k : k + 512] = dot(turned, X[:, k : k + 512])[0:ROWS, :]
            if k == 2048:
                yield
        outs.append(pltpu.make_async_copy(k2, k2_hbm, out_sem.at[1]))
        outs[1].start()

    run(all_sum(1, 4), image_two())
    ww, sk, wk, kk = [jnp.sum(arv[1, 2, j], keepdims=True) / count for j in range(4)]
    sq1 = s1 * s1 * ww
    scale2 = lax.rsqrt(sq1 + norm_eps)
    s2 = scale2 * s1
    h12 = s1 * s2 * sk
    h22 = s2 * s2 * wk
    cross = s1 * s2 * (q - h11 * ss)
    sq2 = (
        s2 * s2 * kk
        - 2.0 * (h12 * h12 + h22 * h22)
        + h12 * h12 * (s1 * s1 * ss)
        + h22 * h22 * (s2 * s2 * ww)
        + 2.0 * h12 * h22 * cross
    )
    sq2 = jnp.maximum(sq2, 0.0)
    s3 = lax.rsqrt(sq2 + norm_eps)
    results = (h11, h12, h22, jnp.sqrt(sq1), jnp.sqrt(sq2), s2, s3 * s2, -s3 * h12 * s1, -s3 * h22 * s2)
    for j, value in enumerate(results):
        mix[j] = value[0, 0]
    for cp in outs:
        cp.wait()
    settle(0)


def combine(mix, kw_hbm, k2_hbm, start_hbm, basis_hbm, quot, coef, kw, k2, start, out, in_sem, out_sem):
    parts = [pl.ds(r, PIECE) for r in range(0, ROWS, PIECE)]
    ins = [
        [
            pltpu.make_async_copy(src.at[at], dst.at[at], in_sem.at[j, p])
            for j, (src, dst) in enumerate(((kw_hbm, kw), (k2_hbm, k2), (start_hbm, start)))
        ]
        for p, at in enumerate(parts)
    ]
    for cps in ins:
        for cp in cps:
            cp.start()
    quot[0] = mix[0]
    coef[0, 0] = mix[1]
    coef[0, 1] = mix[2]
    coef[1, 0] = mix[3]
    coef[1, 1] = mix[4]
    outs = []
    for p, at in enumerate(parts):
        for cp in ins[p]:
            cp.wait()
        w = kw[at, :]
        out[0, at, :] = mix[5] * w
        out[1, at, :] = mix[6] * k2[at, :] + mix[7] * start[at, :] + mix[8] * w
        for j in range(2):
            cp = pltpu.make_async_copy(out.at[j, at], basis_hbm.at[j, at], out_sem.at[j, p])
            cp.start()
            outs.append(cp)
    for cp in outs:
        cp.wait()


def per_device(hidden_in, targets, norm_gain, up_weight, down_weight, start):
    vm, dma = pltpu.VMEM, pltpu.SemaphoreType.DMA
    any_spec = pl.BlockSpec(memory_space=pl.ANY)
    smem_spec = pl.BlockSpec(memory_space=pltpu.SMEM)
    scratch = [
        vm((OWN, D), bf16),
        vm((OWN, D), bf16),
        vm((D,), f32),
        vm((HID, D), bf16),
        vm((HID, D), bf16),
        vm((ROWS, D), f32),
        vm((HID, D), bf16),
        vm((TOK, D), bf16),
        vm((CHUNKS, N_Z, OWN, W), bf16),
        vm((2, GRP, D), f32),
        vm((3, CHUNKS, 3, BLK, W), bf16),
        vm((3, CHUNKS, 3, BLK, W), bf16),
        vm((3, CHUNKS, 2, BLK, W), bf16),
        vm((3, CHUNKS, 2, BLK, W), bf16),
        vm((3, CHUNKS, 2, BLK, W), bf16),
        vm((3, CHUNKS, 2, BLK, W), bf16),
        vm((3, CHUNKS, N_Z, OWN, W), bf16),
        vm((3, CHUNKS, N_Z - 1, OWN, W), bf16),
        vm((3, CHUNKS, N_Z, OWN, W), bf16),
        vm((3, GRP, D), bf16),
        vm((GRP, HID), f32),
        vm((GRP, HID), f32),
        vm((GRP, HID), bf16),
        vm((2, GRP, HID), f32),
        vm((GRP, HID), f32),
        vm((GRP, HID), f32),
        vm((TOK, HID), bf16),
        vm((2, N_X, GRP, PAD), bf16),
        vm((TOK, TOK), bf16),
        vm((TOK, TOK), bf16),
        vm((ROWS, D), f32),
        vm((ROWS, D), f32),
        vm((2, 3, 4, 8, 128), f32),
        vm((2, 2, 15, 4, 8, 128), f32),
        vm((3, OWN, D), f32),
        vm((OWN, D), f32),
        vm((5, OWN, D), f32),
        dma((2 * N_X + 4,)),
    ]
    pairs = [
        (CHUNKS,), (CHUNKS, 6), (CHUNKS, 4),
        (CHUNKS, 4), (CHUNKS, 4), (CHUNKS, 4),
        (3, CHUNKS), (3, CHUNKS, 4), (3, CHUNKS, 2), (3, CHUNKS),
        (3, CHUNKS), (3, CHUNKS, 6), (3, CHUNKS, 4),
        (N_X - 1,), (N_X - 1,), (2, 2),
    ]
    for shape in pairs:
        scratch += [dma(shape), dma(shape)]
    scratch.append(dma((2,)))
    kw, k2, mix = pl.pallas_call(
        kernel,
        out_shape=(
            jax.ShapeDtypeStruct((ROWS, D), f32),
            jax.ShapeDtypeStruct((ROWS, D), f32),
            jax.ShapeDtypeStruct((9,), f32),
        ),
        in_specs=[any_spec] * 6,
        out_specs=(any_spec, any_spec, smem_spec),
        scratch_shapes=scratch,
        compiler_params=pltpu.CompilerParams(
            collective_id=0, has_side_effects=True, vmem_limit_bytes=60 * 1024 * 1024
        ),
        cost_estimate=pl.CostEstimate(flops=5 * 10**9, bytes_accessed=14 * 10**6, transcendentals=10**5),
    )(hidden_in, targets, norm_gain, up_weight, down_weight, start)
    pieces = ROWS // PIECE
    return pl.pallas_call(
        combine,
        out_shape=(
            jax.ShapeDtypeStruct((2, ROWS, D), f32),
            jax.ShapeDtypeStruct((1,), f32),
            jax.ShapeDtypeStruct((2, 2), f32),
        ),
        in_specs=[smem_spec, any_spec, any_spec, any_spec],
        out_specs=(any_spec, smem_spec, smem_spec),
        scratch_shapes=[
            vm((ROWS, D), f32),
            vm((ROWS, D), f32),
            vm((ROWS, D), f32),
            vm((2, ROWS, D), f32),
            dma((3, pieces)),
            dma((2, pieces)),
        ],
        compiler_params=pltpu.CompilerParams(vmem_limit_bytes=60 * 1024 * 1024),
        cost_estimate=pl.CostEstimate(flops=10**7, bytes_accessed=9 * 10**6, transcendentals=0),
    )(mix, kw, k2, start)


def solution(mesh):
    placed = (
        P(("dp", "zero"), None),
        P(("dp", "zero"), None),
        P(),
        P("zero", None),
        P("zero", None),
        P(("zero", "dp"), None),
    )
    return jax.shard_map(
        per_device,
        mesh=mesh,
        in_specs=placed,
        out_specs=(P(None, ("zero", "dp"), None), P(), P()),
        check_vma=False,
    )
```

```python
import jax
import jax.numpy as jnp
from jax import lax
from jax.experimental import pallas as pl
from jax.experimental.pallas import tpu as pltpu
from jax.sharding import PartitionSpec as P

MESH = pl.DeviceIdType.MESH
f32, bf16 = jnp.float32, jnp.bfloat16
norm_eps = 1e-06
gelu_coef = 0.7978845608028654

N_X, N_Y, N_Z, N_C = 4, 4, 8, 2
D = 4608
ROWS = 96
PAD = 128
HID = N_X * PAD
GRP = 128
TOK = N_X * GRP
HALF = GRP // N_C
BLK = HALF // N_Y
OWN = BLK // N_Z
CHUNKS = 3
W = D // CHUNKS
KEEP = 40
PIECE = 32


def gelu_value(inputs):
    return (
        0.5 * inputs * (1.0 + jnp.tanh(gelu_coef * (inputs + 0.044715 * inputs * inputs * inputs)))
    )


def gelu_parts(inputs):
    unit_dir = jnp.ones_like(inputs)

    def first_slope(points):
        return jax.jvp(gelu_value, (points,), (unit_dir,))[1]

    return (
        gelu_value(inputs),
        first_slope(inputs),
        jax.jvp(first_slope, (inputs,), (unit_dir,))[1],
    )


def loss_parts(summed, target, gain):
    r = lax.rsqrt(jnp.sum(summed * summed, axis=-1, keepdims=True) / D + norm_eps)
    normed = summed * r
    pull = (normed * gain - target) * gain
    mean = jnp.sum(pull * normed, axis=-1, keepdims=True) / D
    grad = r * (pull - normed * mean) / float(TOK)
    mix = gain * gain * normed + pull
    bias = jnp.sum(mix * normed, axis=-1, keepdims=True) / D
    scale = r * r * (gain * gain - mean) / float(TOK)
    along = -(scale * normed + r * grad)
    across = -r * normed / float(TOK)
    return grad, normed, mix, scale, along, across, r, bias


def dot_t(a, b):
    return lax.dot_general(a, b, (((1,), (1,)), ((), ())), preferred_element_type=f32)


def dot(a, b):
    return jnp.dot(a, b, preferred_element_type=f32)


def tile_sum(v):
    rows, cols = v.shape
    acc = v[0:8, :]
    for i in range(8, rows, 8):
        acc = acc + v[i : i + 8, :]
    out = acc[:, 0:128]
    for k in range(128, cols, 128):
        out = out + acc[:, k : k + 128]
    return out


def par(*gens):
    gens = list(gens)
    while gens:
        for g in list(gens):
            try:
                next(g)
            except StopIteration:
                gens.remove(g)
        if gens:
            yield


def run(*gens):
    for _ in par(*gens):
        pass


def play(gens, order):
    for j in order:
        next(gens[j], None)
    run(*gens)


def kernel(
    hin_hbm, tgt_hbm, gain_hbm, up_hbm, down_hbm, start_hbm,
    kw_hbm, k2_hbm, mix,
    hin, tgt, gain, up, down, start, dirs, X, xz, part,
    sb, rc, y1b, y1r, y2b, y2r, sz, rz, az, A,
    slope, bendag, hact, agrad, pt1, ptx,
    pfull, pr2, g_hi, g_lo, kw, k2, arv, arr, tot, bsum, lin,
    ld_sem, xz_s, xz_r, xy_s, xy_r, xc_s, xc_r,
    xa_s, xa_r, xac_s, xac_r, sx_s, sx_r,
    rc_s, rc_r, y1_s, y1_r, y2_s, y2_r, rz_s, rz_r,
    az_s, az_r, ay_s, ay_r, ac_s, ac_r,
    pf_s, pf_r, p2_s, p2_r, ar_s, ar_r, out_sem,
):
    x = lax.axis_index("dp")
    shard = lax.axis_index("zero")
    y, z, c = shard // 16, (shard // 2) % 8, shard % 2

    def dev(nx, ny, nz, nc):
        return (nx, ny * 16 + nz * 2 + nc)

    pending = []

    xs = [x] + [(x + k) % N_X for k in range(1, N_X)]
    ys = [y] + [(y + k) % N_Y for k in range(1, N_Y)]
    zs = [z] + [(z + k) % N_Z for k in range(1, N_Z)]

    def x_at(k):
        return xs[k % N_X]

    def y_at(k):
        return ys[k % N_Y]

    def x_peer(k):
        return dev(x_at(k), y, z, c)

    def y_peer(k):
        return dev(x, y_at(k), z, c)

    def z_peer(k):
        return dev(x, y, zs[k], c)

    c_peer = dev(x, y, z, 1 - c)

    def cross_peer(k):
        return dev(x, y_at(k), z, 1 - c)

    def xy_peer(k):
        return dev(x_at(k // N_Y), y_at(k % N_Y), z, c)

    def zc_peer(k):
        return dev(x, y, zs[k // N_C], c if k % N_C == 0 else 1 - c)

    def send(src, dst, ssem, rsem, to):
        cp = pltpu.make_async_remote_copy(
            src_ref=src, dst_ref=dst, send_sem=ssem, recv_sem=rsem, device_id=to, device_id_type=MESH
        )
        cp.start()
        pending.append(cp)
        return cp

    def send_all(copies, bytes_of, ssem, rsem):
        for src, dst, to in copies:
            pltpu.make_async_remote_copy(
                src_ref=src, dst_ref=dst, send_sem=ssem, recv_sem=rsem, device_id=to, device_id_type=MESH
            ).start()
        cp = pltpu.make_async_remote_copy(
            src_ref=bytes_of,
            dst_ref=bytes_of,
            send_sem=ssem,
            recv_sem=rsem,
            device_id=c_peer,
            device_id_type=MESH,
        )
        pending.append(cp)
        return [cp]

    def settle(keep=KEEP):
        while len(pending) > keep:
            pending.pop(0).wait_send()

    def rows(start_row, count):
        return pl.ds(pl.multiple_of(start_row, 16), count)

    def wait_all(cps):
        settle()
        for cp in cps:
            cp.wait_recv()

    small = [
        pltpu.make_async_copy(src, dst, ld_sem.at[2 * N_X + 1 + j])
        for j, (src, dst) in enumerate(((hin_hbm, hin), (tgt_hbm, tgt), (gain_hbm, gain)))
    ]
    for cp in small:
        cp.start()
    loads = []
    for b in range(N_X):
        for j, (src, dst) in enumerate(((up_hbm, up), (down_hbm, down))):
            loads.append(
                pltpu.make_async_copy(
                    src.at[pl.ds(b * ROWS, ROWS)], dst.at[pl.ds(b * PAD, ROWS)], ld_sem.at[2 * b + j]
                )
            )
    loads.append(pltpu.make_async_copy(start_hbm, start, ld_sem.at[2 * N_X]))
    for cp in loads:
        cp.start()

    barrier = pltpu.get_barrier_semaphore()
    peers = [xy_peer(k) for k in range(1, N_X * N_Y)] + [zc_peer(k) for k in range(1, N_Z * N_C)]
    peers += [cross_peer(1), cross_peer(-1)]
    for p in peers:
        pl.semaphore_signal(barrier, inc=1, device_id=p, device_id_type=MESH)
    pl.semaphore_wait(barrier, len(peers))
    for cp in small:
        cp.wait()

    def ring_gather(ref, blocks, c0, w, peer, ssem, rsem, then=None, cross=None):
        half = w // 2
        nb = len(blocks)
        first = []
        for b, (row_of, count) in enumerate(blocks):
            at = (rows(row_of(0), count), pl.ds(c0, w))
            first.append(
                [
                    send(ref.at[at], ref.at[at], ssem.at[2 * b + j], rsem.at[2 * b + j], peer(to))
                    for j, to in enumerate((1, -1))
                ]
            )
        if then:
            then(0)
        yield
        second = []
        for b, (row_of, count) in enumerate(blocks):
            for j, to in enumerate((1, -1)):
                wait_all([first[b][j]])
                at = (rows(row_of(-to), count), pl.ds(c0 + j * half, half))
                i = 2 * (nb + b) + j
                second.append(send(ref.at[at], ref.at[at], ssem.at[i], rsem.at[i], peer(to)))
                if cross:
                    second.append(send(ref.at[at], ref.at[at], ssem.at[i + 2], rsem.at[i + 2], cross(to)))
        if then:
            then(-1)
            then(1)
        yield
        wait_all(second)
        if then:
            then(2)

    def gather_z(own, buf, ssem, rsem):
        buf[z] = own
        copies = [(buf.at[z], buf.at[z], z_peer(k)) for k in range(1, N_Z)]
        return send_all(copies, buf.at[pl.ds(0, N_Z - 1)], ssem, rsem)

    def join16(buf):
        return buf[...].reshape(BLK, W)

    def gather(own, i, h):
        c0, out = h * W, A.at[i]
        cols = pl.ds(c0, W)
        cps = gather_z(own(slice(c0, c0 + W)), az.at[i, h], az_s.at[i, h], az_r.at[i, h])
        yield
        wait_all(cps)
        out[rows(c * HALF + y * BLK, BLK), cols] = join16(az.at[i, h])
        passed = []

        def pass_on(k):
            if k != 2 or i == 0:
                at = (rows(c * HALF + y_at(k) * BLK, BLK), cols)
                passed.append(send(out.at[at], out.at[at], ac_s.at[i, h, k % 4], ac_r.at[i, h, k % 4], c_peer))

        yield from ring_gather(
            out,
            [(lambda k: c * HALF + y_at(k) * BLK, BLK)],
            c0,
            W,
            y_peer,
            ay_s.at[i, h],
            ay_r.at[i, h],
            pass_on,
            cross_peer if i else None,
        )
        if i == 0:
            yield
        wait_all(passed)
        part_grad = dot_t(out[:, cols], down[:, cols])
        if h == 0:
            agrad[i % 2] = part_grad
        else:
            agrad[i % 2] = agrad[i % 2] + part_grad

    def scatter(i, h, make):
        c0 = h * W
        cols = slice(c0, c0 + W)
        make(i, h)
        buf = part.at[i % 2]

        def mine(k):
            return buf[rows(c * HALF + y_at(k) * BLK, BLK), cols]

        def other(k):
            return buf[rows((1 - c) * HALF + y_at(k) * BLK, BLK), cols]

        half = W // 2
        y1b[i, h, 0] = mine(2).astype(bf16)
        y1b[i, h, 1] = other(2).astype(bf16)
        cps = [
            send(
                y1b.at[i, h, p, :, pl.ds(j * half, half)],
                y1r.at[i, h, p, :, pl.ds(j * half, half)],
                y1_s.at[i, h, 2 * p + j],
                y1_r.at[i, h, 2 * p + j],
                peer(to),
            )
            for p, peer in enumerate((y_peer, cross_peer))
            for j, to in enumerate((1, -1))
        ]
        for n, k in enumerate((0, 1, -1)):
            sb[i, h, n] = other(k).astype(bf16)
        cps.append(send(sb.at[i, h], rc.at[i, h], rc_s.at[i, h], rc_r.at[i, h], c_peer))
        yield
        wait_all(cps)
        got = y1r[i, h, 0].astype(f32) + y1r[i, h, 1].astype(f32)
        for j, to in enumerate((1, -1)):
            both_cores = mine(to) + rc[i, h, 1 + j].astype(f32)
            for p in range(2):
                at = slice(p * half, (p + 1) * half)
                piece = both_cores[:, at] + got[:, at] if p == j else both_cores[:, at]
                y2b[i, h, j, :, at] = piece.astype(bf16)
        cps = [
            send(y2b.at[i, h, j], y2r.at[i, h, j], y2_s.at[i, h, j], y2_r.at[i, h, j], y_peer(to))
            for j, to in enumerate((1, -1))
        ]
        yield
        wait_all(cps)
        total = mine(0) + rc[i, h, 0].astype(f32) + y2r[i, h, 0].astype(f32) + y2r[i, h, 1].astype(f32)
        sz[i, h] = total.astype(bf16).reshape(N_Z, OWN, W)
        copies = [(sz.at[i, h, zs[k]], rz.at[i, h, k - 1], z_peer(k)) for k in range(1, N_Z)]
        cps = send_all(copies, rz.at[i, h], rz_s.at[i, h], rz_r.at[i, h])
        yield
        wait_all(cps)
        s3 = sz[i, h, z].astype(f32)
        for k in range(N_Z - 1):
            s3 = s3 + rz[i, h, k].astype(f32)
        tot[i, :, cols] = s3
        if i > 0:
            inner = [jnp.sum(lin[j, :, cols] * s3, axis=-1, keepdims=True) for j in range(2)]
            inners[i] = inner if h == 0 else [p + q for p, q in zip(inners[i], inner)]

    inners = [None, None, None]

    def scatters(i, make):
        return par(*[scatter(i, h, make) for h in range(CHUNKS)])

    def gathers(own, i):
        return par(*[gather(own, i, h) for h in range(CHUNKS)])

    def all_sum(i, n):
        for s, peer in enumerate((xy_peer, zc_peer)):
            copies = [
                (arv.at[i, s, pl.ds(0, n)], arr.at[i, s, k - 1, pl.ds(0, n)], peer(k)) for k in range(1, 16)
            ]
            cps = send_all(copies, arr.at[i, s, :, pl.ds(0, n)], ar_s.at[i, s], ar_r.at[i, s])
            yield
            wait_all(cps)
            acc = arv[i, s, 0:n]
            for k in range(1, 16):
                acc = acc + arr[i, s, k - 1, 0:n]
            arv[i, s + 1, 0:n] = acc

    group = rows(x * GRP, GRP)

    def group_tokens(h):
        c0 = h * W
        cols = pl.ds(c0, W)
        cps = gather_z(hin[:, c0 : c0 + W], xz.at[h], xz_s.at[h], xz_r.at[h])
        yield
        wait_all(cps)
        X[rows(x * GRP + c * HALF + y * BLK, BLK), cols] = join16(xz.at[h])
        passed = []

        def pass_on(k):
            if k != 2:
                at = (rows(x * GRP + c * HALF + y_at(k) * BLK, BLK), cols)
                passed.append(send(X.at[at], X.at[at], xc_s.at[h, k % 4], xc_r.at[h, k % 4], c_peer))

        yield from ring_gather(
            X,
            [(lambda k: x * GRP + c * HALF + y_at(k) * BLK, BLK)],
            c0,
            W,
            y_peer,
            xy_s.at[h],
            xy_r.at[h],
            pass_on,
            cross_peer,
        )
        wait_all(passed)
        pre = dot_t(X[group, cols], up[:, cols])
        if h == 0:
            agrad[0] = pre
        else:
            agrad[0] = agrad[0] + pre

    def accumulate_pt1(h, k):
        cols = pl.ds(h * W, W)
        block = rows(x_at(k) * PAD, PAD)
        lanes = pl.ds(pl.multiple_of(x_at(k) * PAD, PAD), PAD)
        term = dot_t(X[group, cols], dirs[block, cols])
        if h == 0:
            pt1[:, lanes] = term
        else:
            pt1[:, lanes] = pt1[:, lanes] + term

    def start_rows(h):
        ring = ring_gather(
            dirs, [(lambda k: x_at(k) * PAD, ROWS)], h * W, W, x_peer, sx_s.at[h], sx_r.at[h]
        )
        next(ring)
        yield
        next(ring)
        yield
        for k in (0, -1, 1):
            accumulate_pt1(h, k)
        yield
        run(ring)
        accumulate_pt1(h, 2)

    def other_tokens(h):
        cols = pl.ds(h * W, W)
        passed = []

        def pass_on(k):
            if k != 0:
                at = (rows(x_at(k) * GRP + c * HALF, HALF), cols)
                passed.append(send(X.at[at], X.at[at], xac_s.at[h, k % 4], xac_r.at[h, k % 4], c_peer))

        yield from ring_gather(
            X, [(lambda k: x_at(k) * GRP + c * HALF, HALF)], h * W, W, x_peer, xa_s.at[h], xa_r.at[h], pass_on
        )
        yield
        wait_all(passed)

    def local_work():
        loads[-1].wait()
        dirs[rows(x * PAD, ROWS), :] = start[...].astype(bf16)
        for g in s_gens:
            next(g)
        for b in range(N_X):
            pad = pl.ds(b * PAD + ROWS, PAD - ROWS)
            up[pad, :] = jnp.zeros((PAD - ROWS, D), bf16)
            down[pad, :] = jnp.zeros((PAD - ROWS, D), bf16)
            dirs[pad, :] = jnp.zeros((PAD - ROWS, D), bf16)
        yield
        for cp in loads[:-1]:
            cp.wait()
        arv[0, 0, 1] = tile_sum(start[...] * start[...])

    s_gens = [start_rows(h) for h in range(CHUNKS)]
    both = list(range(CHUNKS))
    n = CHUNKS
    play([group_tokens(h) for h in range(CHUNKS)] + [local_work()], both + [n] + both + [n] + both + both)

    def to_branch(i, h):
        for k in range(h * W, (h + 1) * W, W // 3):
            part[i % 2, :, k : k + W // 3] = dot(hact[...], down[:, k : k + W // 3])

    def weights():
        return tgt[...].astype(f32), gain[...]

    state = []

    def loss_curv(tangent, inner):
        r, bias = state
        a = inner[0] / D
        d = r * (inner[1] / D - a * bias)
        return lambda at: (lin[2, :, at] * tangent(at) + a * lin[3, :, at] + d * lin[4, :, at]).astype(bf16)

    def forward():
        for b in range(N_X):
            cols = pl.ds(b * PAD, PAD)
            value, first, second = gelu_parts(agrad[0, :, cols])
            hact[:, cols] = value.astype(bf16)
            slope[:, cols] = first
            bendag[:, cols] = second
        yield from scatters(0, to_branch)
        bsum[...] = hin[...].astype(f32) + tot[0]
        parts = loss_parts(bsum[...], *weights())
        for j in range(5):
            lin[j] = parts[1 + j]
        state.extend(parts[6:])
        grad = parts[0].astype(bf16)
        yield from gathers(lambda at: grad[:, at], 0)
        bendag[...] = bendag[...] * agrad[0]

    def first_tangent():
        hact[...] = (slope[...] * pt1[...]).astype(bf16)
        yield from scatters(1, to_branch)

    fwd = forward()
    others = [other_tokens(h) for h in range(CHUNKS)]
    for g in [s_gens[0], fwd] + s_gens[1:] + s_gens + [fwd, fwd] + s_gens:
        next(g, None)
    tangent = first_tangent()
    for g in [tangent, *others, tangent, fwd, tangent, fwd, others[0]]:
        next(g, None)
    run(tangent)
    curv = loss_curv(lambda at: tot[1, :, at], inners[1])

    def token_gram(k):
        mine = rows(x_at(k) * GRP, GRP)
        g = dot_t(X[mine, :], X[...])
        hi = g.astype(bf16)
        g_hi[mine, :] = hi
        g_lo[mine, :] = (g - hi.astype(f32)).astype(bf16)

    grads = gathers(curv, 1)
    for g in [grads, fwd, *others[1:], fwd, grads, others[0], fwd, grads, *others[1:], *others]:
        next(g, None)
    run(fwd, *others)
    token_gram(0)
    run(grads)
    p1 = agrad[1] * slope[...] + bendag[...] * pt1[...]
    pfull[group, :] = p1.astype(bf16)

    def share_p1():
        def use(k):
            block = rows(x_at(k) * GRP, GRP)
            term = dot(g_hi[group, block], pfull[block, :]) + dot(g_lo[group, block], pfull[block, :])
            if k == 0:
                ptx[...] = term
            else:
                ptx[...] = ptx[...] + term

        cps = [
            send(pfull.at[group], pfull.at[group], pf_s.at[k - 1], pf_r.at[k - 1], x_peer(k))
            for k in range(1, N_X)
        ]
        use(0)
        yield
        for k in (1, 3, 2):
            wait_all([cps[k - 1]])
            use(N_X - k)

    def own_sums():
        arv[0, 0, 0] = tile_sum(p1 * pt1[...])
        yield

    run(share_p1(), own_sums())

    hact[...] = (slope[...] * ptx[...]).astype(bf16)

    def image_one():
        own = pfull[:, pl.ds(pl.multiple_of(x * PAD, PAD), PAD)].T
        for k in range(0, D, 512):
            kw[:, k : k + 512] = dot(own, X[:, k : k + 512])[0:ROWS, :]
            if k % 1536 == 1024:
                yield

    count = float(ROWS * 256 * D)
    firsts = []

    def first_sums():
        yield from all_sum(0, 2)
        q = jnp.sum(arv[0, 2, 0], keepdims=True) / count
        ss = jnp.sum(arv[0, 2, 1], keepdims=True) / count
        s1 = lax.rsqrt(ss + norm_eps)
        firsts.extend([q, ss, s1, s1 * s1 * q])

    run(scatters(2, to_branch), first_sums(), image_one())
    q, ss, s1, h11 = firsts
    curv = loss_curv(
        lambda at: tot[2, :, at] - h11 * tot[1, :, at], [p - h11 * q for p, q in zip(inners[2], inners[1])]
    )

    def remainder():
        ptx[...] = ptx[...] - h11 * pt1[...]
        acc = None
        for k in range(0, D, 1536):
            w = kw[:, k : k + 1536] - h11 * start[:, k : k + 1536]
            kw[:, k : k + 1536] = w
            s = tile_sum(w * w)
            acc = s if acc is None else acc + s
            token_gram(k // 1536 + 1)
            yield
        arv[1, 0, 0] = acc

    run(gathers(curv, 2), remainder())
    out_w = pltpu.make_async_copy(kw, kw_hbm, out_sem.at[0])
    out_w.start()
    for b in range(N_X):
        cols = pl.ds(b * PAD, PAD)
        pr2[1, b] = (agrad[0, :, cols] * slope[:, cols] + bendag[:, cols] * ptx[:, cols]).astype(bf16)
    pr2[0, x] = pr2[1, x]
    cps = [
        send(pr2.at[1, x_at(k)], pr2.at[0, x], p2_s.at[k - 1], p2_r.at[k - 1], x_peer(k))
        for k in range(1, N_X)
    ]
    sums = [None, None]
    for b in range(N_X):
        cols = pl.ds(b * PAD, PAD)
        for j, other in enumerate((pt1, ptx)):
            t = tile_sum(other[:, cols] * pr2[1, b].astype(f32))
            sums[j] = t if sums[j] is None else sums[j] + t
    for j in range(2):
        arv[1, 0, 1 + j] = sums[j]
    wait_all(cps)
    own = pr2[0].reshape(TOK, PAD)
    arv[1, 0, 3] = tile_sum((dot(g_hi[...], own) + dot(g_lo[...], own)) * own.astype(f32))
    outs = [out_w]

    def image_two():
        turned = own.T
        for k in range(0, D, 512):
            k2[:, k : k + 512] = dot(turned, X[:, k : k + 512])[0:ROWS, :]
            if k == 2048:
                yield
        outs.append(pltpu.make_async_copy(k2, k2_hbm, out_sem.at[1]))
        outs[1].start()

    run(all_sum(1, 4), image_two())
    ww, sk, wk, kk = [jnp.sum(arv[1, 2, j], keepdims=True) / count for j in range(4)]
    sq1 = s1 * s1 * ww
    scale2 = lax.rsqrt(sq1 + norm_eps)
    s2 = scale2 * s1
    h12 = s1 * s2 * sk
    h22 = s2 * s2 * wk
    cross = s1 * s2 * (q - h11 * ss)
    sq2 = (
        s2 * s2 * kk
        - 2.0 * (h12 * h12 + h22 * h22)
        + h12 * h12 * (s1 * s1 * ss)
        + h22 * h22 * (s2 * s2 * ww)
        + 2.0 * h12 * h22 * cross
    )
    sq2 = jnp.maximum(sq2, 0.0)
    s3 = lax.rsqrt(sq2 + norm_eps)
    results = (h11, h12, h22, jnp.sqrt(sq1), jnp.sqrt(sq2), s2, s3 * s2, -s3 * h12 * s1, -s3 * h22 * s2)
    for j, value in enumerate(results):
        mix[j] = value[0, 0]
    for cp in outs:
        cp.wait()
    settle(0)


def combine(mix, kw_hbm, k2_hbm, start_hbm, basis_hbm, quot, coef, kw, k2, start, out, in_sem, out_sem):
    parts = [pl.ds(r, PIECE) for r in range(0, ROWS, PIECE)]
    ins = [
        [
            pltpu.make_async_copy(src.at[at], dst.at[at], in_sem.at[j, p])
            for j, (src, dst) in enumerate(((kw_hbm, kw), (k2_hbm, k2), (start_hbm, start)))
        ]
        for p, at in enumerate(parts)
    ]
    for cps in ins:
        for cp in cps:
            cp.start()
    quot[0] = mix[0]
    coef[0, 0] = mix[1]
    coef[0, 1] = mix[2]
    coef[1, 0] = mix[3]
    coef[1, 1] = mix[4]
    outs = []
    for p, at in enumerate(parts):
        for cp in ins[p]:
            cp.wait()
        w = kw[at, :]
        out[0, at, :] = mix[5] * w
        out[1, at, :] = mix[6] * k2[at, :] + mix[7] * start[at, :] + mix[8] * w
        for j in range(2):
            cp = pltpu.make_async_copy(out.at[j, at], basis_hbm.at[j, at], out_sem.at[j, p])
            cp.start()
            outs.append(cp)
    for cp in outs:
        cp.wait()


def per_device(hidden_in, targets, norm_gain, up_weight, down_weight, start):
    vm, dma = pltpu.VMEM, pltpu.SemaphoreType.DMA
    any_spec = pl.BlockSpec(memory_space=pl.ANY)
    smem_spec = pl.BlockSpec(memory_space=pltpu.SMEM)
    scratch = [
        vm((OWN, D), bf16),
        vm((OWN, D), bf16),
        vm((D,), f32),
        vm((HID, D), bf16),
        vm((HID, D), bf16),
        vm((ROWS, D), f32),
        vm((HID, D), bf16),
        vm((TOK, D), bf16),
        vm((CHUNKS, N_Z, OWN, W), bf16),
        vm((2, GRP, D), f32),
        vm((3, CHUNKS, 3, BLK, W), bf16),
        vm((3, CHUNKS, 3, BLK, W), bf16),
        vm((3, CHUNKS, 2, BLK, W), bf16),
        vm((3, CHUNKS, 2, BLK, W), bf16),
        vm((3, CHUNKS, 2, BLK, W), bf16),
        vm((3, CHUNKS, 2, BLK, W), bf16),
        vm((3, CHUNKS, N_Z, OWN, W), bf16),
        vm((3, CHUNKS, N_Z - 1, OWN, W), bf16),
        vm((3, CHUNKS, N_Z, OWN, W), bf16),
        vm((3, GRP, D), bf16),
        vm((GRP, HID), f32),
        vm((GRP, HID), f32),
        vm((GRP, HID), bf16),
        vm((2, GRP, HID), f32),
        vm((GRP, HID), f32),
        vm((GRP, HID), f32),
        vm((TOK, HID), bf16),
        vm((2, N_X, GRP, PAD), bf16),
        vm((TOK, TOK), bf16),
        vm((TOK, TOK), bf16),
        vm((ROWS, D), f32),
        vm((ROWS, D), f32),
        vm((2, 3, 4, 8, 128), f32),
        vm((2, 2, 15, 4, 8, 128), f32),
        vm((3, OWN, D), f32),
        vm((OWN, D), f32),
        vm((5, OWN, D), f32),
        dma((2 * N_X + 4,)),
    ]
    pairs = [
        (CHUNKS,), (CHUNKS, 6), (CHUNKS, 4),
        (CHUNKS, 4), (CHUNKS, 4), (CHUNKS, 4),
        (3, CHUNKS), (3, CHUNKS, 4), (3, CHUNKS, 2), (3, CHUNKS),
        (3, CHUNKS), (3, CHUNKS, 6), (3, CHUNKS, 4),
        (N_X - 1,), (N_X - 1,), (2, 2),
    ]
    for shape in pairs:
        scratch += [dma(shape), dma(shape)]
    scratch.append(dma((2,)))
    kw, k2, mix = pl.pallas_call(
        kernel,
        out_shape=(
            jax.ShapeDtypeStruct((ROWS, D), f32),
            jax.ShapeDtypeStruct((ROWS, D), f32),
            jax.ShapeDtypeStruct((9,), f32),
        ),
        in_specs=[any_spec] * 6,
        out_specs=(any_spec, any_spec, smem_spec),
        scratch_shapes=scratch,
        compiler_params=pltpu.CompilerParams(
            collective_id=0, has_side_effects=True, vmem_limit_bytes=60 * 1024 * 1024
        ),
        cost_estimate=pl.CostEstimate(flops=5 * 10**9, bytes_accessed=14 * 10**6, transcendentals=10**5),
    )(hidden_in, targets, norm_gain, up_weight, down_weight, start)
    pieces = ROWS // PIECE
    return pl.pallas_call(
        combine,
        out_shape=(
            jax.ShapeDtypeStruct((2, ROWS, D), f32),
            jax.ShapeDtypeStruct((1,), f32),
            jax.ShapeDtypeStruct((2, 2), f32),
        ),
        in_specs=[smem_spec, any_spec, any_spec, any_spec],
        out_specs=(any_spec, smem_spec, smem_spec),
        scratch_shapes=[
            vm((ROWS, D), f32),
            vm((ROWS, D), f32),
            vm((ROWS, D), f32),
            vm((2, ROWS, D), f32),
            dma((3, pieces)),
            dma((2, pieces)),
        ],
        compiler_params=pltpu.CompilerParams(vmem_limit_bytes=60 * 1024 * 1024),
        cost_estimate=pl.CostEstimate(flops=10**7, bytes_accessed=9 * 10**6, transcendentals=0),
    )(mix, kw, k2, start)


def solution(mesh):
    placed = (
        P(("dp", "zero"), None),
        P(("dp", "zero"), None),
        P(),
        P("zero", None),
        P("zero", None),
        P(("zero", "dp"), None),
    )
    return jax.shard_map(
        per_device,
        mesh=mesh,
        in_specs=placed,
        out_specs=(P(None, ("zero", "dp"), None), P(), P()),
        check_vma=False,
    )
```
